32 devices in a mesh: grp: 2 (over core), row: 8 (over z, x), head: 2 (over y).
Axes of the slice: x: 2, y: 2, z: 4, core: 2. Of those that a mesh axis runs over, the one named last changes fastest.
Arguments:
- tokens: int32 [2, 256], P('grp'), may hold values from 0 to 22
- lengths: int32 [2], P('grp'), may hold values from 128 to 256, as said below
- recycle: int32 [2], P('grp'), may hold values from 1 to 4, as said below
- resolved: int32 [2, 256], P('grp'), may hold values from 0 to 1, as said below
- coords: float32 [2, 3, 256], P('grp')
- plm_embed: bfloat16 [23, 1280], replicated, may hold values from -6 to 6
- plm_uv: bfloat16 [2, 1280, 2560], P(None, None, 'head'), may hold values from -0.15625 to 0.15625
- plm_qk: bfloat16 [1280, 256], replicated, may hold values from -0.15625 to 0.15625
- plm_affine: float32 [4, 256], replicated, may hold values from -1 to 1
- plm_out: bfloat16 [2560, 1280], P('head'), may hold values from -0.125 to 0.125
- w_in: float32 [1280, 256], replicated, may hold values from -0.15625 to 0.15625
- w_pairin: float32 [2, 256, 128], replicated, may hold values from -0.375 to 0.375
- w_tri: float32 [6, 128, 128], replicated, may hold values from -0.5 to 0.5
- vecs: float32 [4, 128], replicated
- row_in: float32 [1280], replicated, may hold values from 2e-07 to 2e-06
- col_in: float32 [256], replicated, may hold values from 2e-07 to 2e-06
- row_pairin: float32 [2, 256], replicated, may hold values from 2e-07 to 2e-06
- col_pairin: float32 [2, 128], replicated, may hold values from 2e-07 to 2e-06
- row_tri: float32 [6, 128], replicated, may hold values from 2e-07 to 2e-06
- col_tri: float32 [6, 128], replicated, may hold values from 2e-07 to 2e-06
- sq_vecs: float32 [4, 128], replicated, may hold values from 1e-07 to 0.001
Outputs:
- loss_sum: float32 [], replicated
- loss_count: float32 [], replicated
- grad_in: float32 [1280, 256], replicated
- new_row_in: float32 [1280], replicated
- new_col_in: float32 [256], replicated
- new_in: float32 [1280, 256], replicated
- grad_pairin: float32 [2, 256, 128], replicated
- new_row_pairin: float32 [2, 256], replicated
- new_col_pairin: float32 [2, 128], replicated
- new_pairin: float32 [2, 256, 128], replicated
- grad_tri: float32 [6, 128, 128], replicated
- new_row_tri: float32 [6, 128], replicated
- new_col_tri: float32 [6, 128], replicated
- new_tri: float32 [6, 128, 128], replicated
- grad_vecs: float32 [4, 128], replicated
- new_sq_vecs: float32 [4, 128], replicated
- new_vecs: float32 [4, 128], replicated
The draws below stay inside these ranges and needn't reach their ends.
Inputs may be any that keep to these rules, and one draw needn't show every extreme that they name: `lengths`: one of the two items has length 256, the other at least 128 and less than 256. One of the two items has recycle count 4, the other a smaller one. Each item has resolved residues among its first 128 positions.
All inputs are finite; a program needn't handle non-finite values.
Results may differ from the reference program's by a relative error of at most 0.0076.
Values may be sent and summed in bfloat16 or wider, within the bound.
A program may use at most 704 MiB of HBM per device.

```python
import math
import jax
import jax.numpy as jnp
from jax import lax

D_PLM = 1280
EXPAND = 2560
QK = 256
VOCAB = 23
NODE = 256
PAIR = 128
RES_DEV = 32
STEP = 10
ITEMS = 2
RESIDUES = 256


def draw_lengths(key, part):
    key = jax.random.fold_in(key, 3)
    first, second = jax.random.split(key)
    other = jax.random.randint(first, (), RESIDUES // 2, RESIDUES)
    which = jax.random.randint(second, (), 0, ITEMS)
    return jnp.where(jnp.arange(ITEMS) == which, RESIDUES, other).astype(jnp.int32)


def draw_recycle(key, part):
    key = jax.random.fold_in(key, 5)
    first, second = jax.random.split(key)
    other = jax.random.randint(first, (), 1, 4)
    which = jax.random.randint(second, (), 0, ITEMS)
    return jnp.where(jnp.arange(ITEMS) == which, 4, other).astype(jnp.int32)


def draw_vecs(key, part):
    key = jax.random.fold_in(key, 7)
    keys = jax.random.split(key, 3)
    first = jax.random.normal(keys[0], (1, PAIR), jnp.float32)
    gains = jax.random.uniform(keys[1], (2, PAIR), jnp.float32, 0.5, 1.5)
    last = jax.random.normal(keys[2], (1, PAIR), jnp.float32) / math.sqrt(PAIR)
    return jnp.concatenate([first, gains, last], 0)


def draw_resolved(key, part):
    key = jax.random.fold_in(key, 11)
    keys = jax.random.split(key, 3)
    blocks = RESIDUES // RES_DEV
    block_on = jax.random.randint(keys[0], (ITEMS, blocks), 0, 2)
    forced = jax.random.randint(keys[1], (ITEMS, 1), 0, max(1, blocks // 2))
    block_on = jnp.maximum(block_on, (jnp.arange(blocks)[None, :] == forced).astype(jnp.int32))
    inner = (jax.random.randint(keys[2], (ITEMS, RESIDUES), 0, 10) < 9).astype(jnp.int32)
    return (jnp.repeat(block_on, RES_DEV, axis=1) * inner).astype(jnp.int32)


def draw_coords(key, part):
    key = jax.random.fold_in(key, 13)
    first, second = jax.random.split(key)
    blocks = RESIDUES // RES_DEV
    scales = jnp.exp(jax.random.uniform(first, (ITEMS, 1, blocks), jnp.float32, -1.5, 1.5))
    base = jax.random.normal(second, (ITEMS, 3, RESIDUES), jnp.float32)
    return jnp.clip(1.5 * base * jnp.repeat(scales, RES_DEV, axis=2), -9.0, 9.0)


def with_ends(values, own_key, low, high):
    spot = [jax.random.randint(jax.random.fold_in(own_key, axis), (), 0, length) for axis, length in enumerate(values.shape)]
    widest = values.shape.index(max(values.shape))
    beside = spot[:widest] + [(spot[widest] + 1) % values.shape[widest]] + spot[widest + 1:]
    return values.at[tuple(spot)].set(low).at[tuple(beside)].set(high)


def block_levels(rng, extent, shards, least, high):
    def one(dim, parts):
        draws = jax.random.uniform(jax.random.fold_in(jax.random.fold_in(rng, 6), dim), (parts,), jnp.float32, least / len(shards), high / len(shards))
        return jnp.repeat(jnp.exp(draws), extent[dim] // parts).reshape((-1,) + (1,) * (len(extent) - dim - 1))

    gain = one(*shards[0])
    for cut in shards[1:]:
        gain = gain * one(*cut)
    return gain


def noise(rng, extent, deviation, bound, cuts=(), held_as=jnp.bfloat16):
    drawn = jax.random.normal(rng, extent, jnp.float32) * deviation
    if len(cuts) > 0:
        drawn = block_levels(rng, extent, cuts, -0.22, 0.18) * drawn
    return jnp.clip(drawn, min=-bound, max=bound).astype(held_as)


def setup_inputs(seed: int = 0) -> dict:
    key_list = jax.random.split(jax.random.key(seed), 22)
    tokens = with_ends(jax.random.randint(key_list[0], (ITEMS, RESIDUES), 0, VOCAB), jax.random.fold_in(key_list[0], 1), 0, VOCAB - 1).astype(jnp.int32)
    lengths = draw_lengths(jax.random.fold_in(key_list[21], 71), 0)
    recycle = draw_recycle(jax.random.fold_in(key_list[21], 71), 0)
    resolved = draw_resolved(jax.random.fold_in(key_list[21], 71), 0)
    coords = draw_coords(jax.random.fold_in(key_list[21], 71), 0)
    plm_embed = noise(key_list[5], (VOCAB, D_PLM), 1.0, 6.0)
    plm_uv = noise(key_list[6], (2, D_PLM, EXPAND), D_PLM ** -0.5, 0.15625, ((2, 2),))
    plm_qk = noise(key_list[7], (D_PLM, QK), D_PLM ** -0.5, 0.15625)
    plm_affine = jnp.clip(jax.random.uniform(key_list[8], (4, QK), jnp.float32, -1.0, 1.0), -1.0, 1.0)
    plm_out = noise(key_list[9], (EXPAND, D_PLM), EXPAND ** -0.5, 0.125, ((0, 2),))
    w_in = noise(key_list[10], (D_PLM, NODE), D_PLM ** -0.5, 0.15625, (), jnp.float32)
    w_pairin = noise(key_list[11], (2, NODE, PAIR), NODE ** -0.5, 0.375, (), jnp.float32)
    w_tri = noise(key_list[12], (6, PAIR, PAIR), PAIR ** -0.5, 0.5, (), jnp.float32)
    vecs = draw_vecs(jax.random.fold_in(key_list[21], 71), 0)
    row_in = jnp.clip(jnp.exp(jax.random.uniform(key_list[14], (D_PLM,), jnp.float32, math.log(2.0000000233721948e-07), math.log(1.9999999949504854e-06))), 2.0000000233721948e-07, 1.9999999949504854e-06)
    col_in = jnp.clip(jnp.exp(jax.random.uniform(key_list[15], (NODE,), jnp.float32, math.log(2.0000000233721948e-07), math.log(1.9999999949504854e-06))), 2.0000000233721948e-07, 1.9999999949504854e-06)
    row_pairin = jnp.clip(jnp.exp(jax.random.uniform(key_list[16], (2, NODE), jnp.float32, math.log(2.0000000233721948e-07), math.log(1.9999999949504854e-06))), 2.0000000233721948e-07, 1.9999999949504854e-06)
    col_pairin = jnp.clip(jnp.exp(jax.random.uniform(key_list[17], (2, PAIR), jnp.float32, math.log(2.0000000233721948e-07), math.log(1.9999999949504854e-06))), 2.0000000233721948e-07, 1.9999999949504854e-06)
    row_tri = jnp.clip(jnp.exp(jax.random.uniform(key_list[18], (6, PAIR), jnp.float32, math.log(2.0000000233721948e-07), math.log(1.9999999949504854e-06))), 2.0000000233721948e-07, 1.9999999949504854e-06)
    col_tri = jnp.clip(jnp.exp(jax.random.uniform(key_list[19], (6, PAIR), jnp.float32, math.log(2.0000000233721948e-07), math.log(1.9999999949504854e-06))), 2.0000000233721948e-07, 1.9999999949504854e-06)
    sq_vecs = jnp.clip(jnp.exp(jax.random.uniform(key_list[20], (4, PAIR), jnp.float32, math.log(1.0000000116860974e-07), math.log(0.001))), 1.0000000116860974e-07, 0.001)
    return {"tokens": tokens, "lengths": lengths, "recycle": recycle, "resolved": resolved, "coords": coords, "plm_embed": plm_embed, "plm_uv": plm_uv, "plm_qk": plm_qk, "plm_affine": plm_affine, "plm_out": plm_out, "w_in": w_in, "w_pairin": w_pairin, "w_tri": w_tri, "vecs": vecs, "row_in": row_in, "col_in": col_in, "row_pairin": row_pairin, "col_pairin": col_pairin, "row_tri": row_tri, "col_tri": col_tri, "sq_vecs": sq_vecs}


@jax.custom_vjp
def low(v):
    return lax.optimization_barrier(v.astype(jnp.bfloat16)).astype(jnp.float32)

@jax.custom_vjp
def low_back(v):
    return v

def low_keep(v):
    return (low(v), None)

def low_pass(kept, grad):
    return (grad,)

def back_keep(v):
    return (v, None)

def back_low(kept, grad):
    return (low(grad),)
low.defvjp(low_keep, low_pass)
low_back.defvjp(back_keep, back_low)
highest = lax.Precision.HIGHEST

def layer_norm(value):
    centre = value - lax.optimization_barrier(jnp.mean(value, -1, keepdims=True))
    return centre * lax.rsqrt(lax.optimization_barrier(jnp.mean(centre * centre, -1, keepdims=True)) + 1e-05)

def plm_layer(tok, length, plm_embed, plm_uv, plm_qk, plm_affine, plm_out):
    onehot = (tok[:, None] == jnp.arange(VOCAB)[None, :]).astype(jnp.float32)
    embed = jnp.dot(onehot, plm_embed.astype(jnp.float32), precision=highest)
    normed = low(layer_norm(embed))
    ugate = jax.nn.silu(jnp.dot(normed, plm_uv[0].astype(jnp.float32), precision=highest))
    value = low(jax.nn.silu(jnp.dot(normed, plm_uv[1].astype(jnp.float32), precision=highest)))
    shared = jax.nn.silu(jnp.dot(normed, plm_qk.astype(jnp.float32), precision=highest))
    query = low(shared * plm_affine[0] + plm_affine[1])
    keyed = low(shared * plm_affine[2] + plm_affine[3])
    scores = jnp.dot(query, keyed.T, precision=highest) / math.sqrt(QK)
    valid = jnp.arange(RESIDUES) < length
    attn = low(jax.nn.softmax(jnp.where(valid[None, :], scores, -1000000000.0), axis=-1))
    mixed = low(ugate * jnp.dot(attn, value, precision=highest))
    state = embed + jnp.dot(mixed, plm_out.astype(jnp.float32), precision=highest)
    return (low(layer_norm(state)), scores)

def item_loss(params, frozen_in, scores, true_dist, pair_weight):
    w_in, w_pairin, w_tri, vecs = params
    single = low(jnp.dot(frozen_in, low(w_in), precision=highest))
    pair_low = low(w_pairin)
    side_a = jnp.dot(single, pair_low[0], precision=highest)
    side_b = jnp.dot(single, pair_low[1], precision=highest)
    pair = scores[:, :, None] * vecs[0] + side_a[:, None, :] + side_b[None, :, :]
    pnorm = low(layer_norm(pair) * vecs[1])
    tri_low = low(w_tri)
    proj = [low_back(jnp.einsum('ijc,cd->ijd', pnorm, tri_low[index], precision=highest)) for index in range(5)]
    left = low(jax.nn.sigmoid(proj[1]) * proj[0])
    right = low(jax.nn.sigmoid(proj[3]) * proj[2])
    gate = jax.nn.sigmoid(proj[4])
    update = low_back(jnp.einsum('ikc,jkc->ijc', left, right, precision=highest))
    unorm = low(layer_norm(update) * vecs[2])
    branch = low_back(jnp.einsum('ijc,cd->ijd', unorm, tri_low[5], precision=highest))
    final = pair + gate * branch
    dist = jax.nn.softplus(jnp.einsum('ijc,c->ij', final, vecs[3], precision=highest))
    diff = dist - true_dist
    return jnp.sum(pair_weight * (jnp.sqrt(diff * diff + 1.0) - 1.0))

def factored(grad, weight, row_old, col_old):
    beta = 1.0 - STEP ** (-0.8)
    sq = grad * grad + 1e-30
    row_new = beta * row_old + (1.0 - beta) * lax.optimization_barrier(jnp.mean(sq, -1))
    col_new = beta * col_old + (1.0 - beta) * lax.optimization_barrier(jnp.mean(sq, -2))
    second = row_new[..., :, None] * col_new[..., None, :] / lax.optimization_barrier(jnp.mean(row_new, -1))[..., None, None]
    step = grad * lax.rsqrt(second)
    rms = jnp.sqrt(lax.optimization_barrier(jnp.mean(step * step, axis=(-2, -1), keepdims=True)))
    step = step / jnp.maximum(1.0, rms)
    scale = jnp.maximum(0.001, jnp.sqrt(lax.optimization_barrier(jnp.mean(weight * weight, axis=(-2, -1), keepdims=True))))
    return (row_new, col_new, weight - 0.3 * scale * step)

def unfactored(grad, weight, sq_old):
    beta = 1.0 - STEP ** (-0.8)
    sq_new = beta * sq_old + (1.0 - beta) * (grad * grad + 1e-30)
    step = grad * lax.rsqrt(sq_new)
    rms = jnp.sqrt(lax.optimization_barrier(jnp.mean(step * step, -1, keepdims=True)))
    step = step / jnp.maximum(1.0, rms)
    scale = jnp.maximum(0.001, jnp.sqrt(lax.optimization_barrier(jnp.mean(weight * weight, -1, keepdims=True))))
    return (sq_new, weight - 0.3 * scale * step)

def reference(tokens, lengths, recycle, resolved, coords, plm_embed, plm_uv, plm_qk, plm_affine, plm_out, w_in, w_pairin, w_tri, vecs, row_in, col_in, row_pairin, col_pairin, row_tri, col_tri, sq_vecs):
    items = []
    loss_count = jnp.float32(0.0)
    for item in range(ITEMS):
        frozen_in, scores = plm_layer(tokens[item], lengths[item], plm_embed, plm_uv, plm_qk, plm_affine, plm_out)
        valid = ((jnp.arange(RESIDUES) < lengths[item]) & (resolved[item] > 0)).astype(jnp.float32)
        pair_weight = recycle[item].astype(jnp.float32) * valid[:, None] * valid[None, :]
        place = coords[item]
        delta = place[:, :, None] - place[:, None, :]
        true_dist = jnp.sqrt(lax.optimization_barrier(jnp.sum(delta * delta, 0)))
        loss_count = loss_count + jnp.sum(pair_weight)
        items.append((frozen_in, scores, true_dist, pair_weight))

    def total(params):
        result = jnp.float32(0.0)
        for frozen_in, scores, true_dist, pair_weight in items:
            result = result + item_loss(params, frozen_in, scores, true_dist, pair_weight)
        return result
    params = (w_in, w_pairin, w_tri, vecs)
    loss_sum, pullback = jax.vjp(total, params)
    grads = pullback(jnp.float32(1.0) / loss_count)[0]
    grad_in, grad_pairin, grad_tri, grad_vecs = grads
    new_row_in, new_col_in, new_in = factored(grad_in, w_in, row_in, col_in)
    new_row_pairin, new_col_pairin, new_pairin = factored(grad_pairin, w_pairin, row_pairin, col_pairin)
    new_row_tri, new_col_tri, new_tri = factored(grad_tri, w_tri, row_tri, col_tri)
    new_sq_vecs, new_vecs = unfactored(grad_vecs, vecs, sq_vecs)
    return (loss_sum, loss_count, grad_in, new_row_in, new_col_in, new_in, grad_pairin, new_row_pairin, new_col_pairin, new_pairin, grad_tri, new_row_tri, new_col_tri, new_tri, grad_vecs, new_sq_vecs, new_vecs)
```

```python
import math

import jax
import jax.numpy as jnp
from jax import lax
from jax.sharding import PartitionSpec as P

STEP = 10
highest = lax.Precision.HIGHEST


def normalize(value):
    centre = value - jnp.mean(value, -1, keepdims=True)
    scale = lax.rsqrt(jnp.mean(centre * centre, -1, keepdims=True) + 1e-05)
    return (centre * scale, scale)


def norm_back(normal, scale, grad):
    return scale * (
        grad
        - jnp.mean(grad, -1, keepdims=True)
        - normal * jnp.mean(grad * normal, -1, keepdims=True)
    )


def factored(grad, weight, row_old, col_old):
    beta = 1.0 - STEP ** (-0.8)
    sq = grad * grad + 1e-30
    row_new = beta * row_old + (1.0 - beta) * jnp.mean(sq, -1)
    col_new = beta * col_old + (1.0 - beta) * jnp.mean(sq, -2)
    second = row_new[..., :, None] * col_new[..., None, :] / jnp.mean(row_new, -1)[..., None, None]
    step = grad * lax.rsqrt(second)
    rms = jnp.sqrt(jnp.mean(step * step, axis=(-2, -1), keepdims=True))
    step = step / jnp.maximum(1.0, rms)
    scale = jnp.maximum(0.001, jnp.sqrt(jnp.mean(weight * weight, axis=(-2, -1), keepdims=True)))
    return (row_new, col_new, weight - 0.3 * scale * step)


def unfactored(grad, weight, sq_old):
    beta = 1.0 - STEP ** (-0.8)
    sq_new = beta * sq_old + (1.0 - beta) * (grad * grad + 1e-30)
    step = grad * lax.rsqrt(sq_new)
    rms = jnp.sqrt(jnp.mean(step * step, -1, keepdims=True))
    step = step / jnp.maximum(1.0, rms)
    scale = jnp.maximum(0.001, jnp.sqrt(jnp.mean(weight * weight, -1, keepdims=True)))
    return (sq_new, weight - 0.3 * scale * step)


def dot32(a, b):
    return jnp.dot(a, b, precision=highest)


def shards(
    tokens, lengths, recycle, resolved, coords, plm_embed, plm_uv, plm_qk, plm_affine, plm_out,
    w_in, w_pairin, w_tri, vecs, row_in, col_in, row_pairin, col_pairin, row_tri, col_tri, sq_vecs,
):
    f32, bf16 = jnp.float32, jnp.bfloat16
    total_len = tokens.shape[1]
    vocab = plm_embed.shape[0]
    length = lengths[0]
    onehot = (tokens[0][:, None] == jnp.arange(vocab)[None, :]).astype(f32)
    key_ok = (jnp.arange(total_len) < length).astype(f32)
    count = jnp.sum(onehot, 0)
    count_key = dot32(key_ok[None, :], onehot)[0]
    embed = plm_embed.astype(f32)
    normed = normalize(embed)[0].astype(bf16)
    ugate = jax.nn.silu(jnp.dot(normed, plm_uv[0], preferred_element_type=f32))
    value = jax.nn.silu(jnp.dot(normed, plm_uv[1], preferred_element_type=f32)).astype(bf16)
    shared = jax.nn.silu(jnp.dot(normed, plm_qk, preferred_element_type=f32))
    query = (shared * plm_affine[0] + plm_affine[1]).astype(bf16)
    keyed = (shared * plm_affine[2] + plm_affine[3]).astype(bf16)
    scores = jnp.dot(query, keyed.T, preferred_element_type=f32) / math.sqrt(plm_qk.shape[1])
    masked = jnp.where(count_key[None, :] > 0, scores, -1000000000.0)
    top = jnp.exp(masked - jnp.max(masked, -1, keepdims=True))
    attn = (top / jnp.sum(top * count_key, -1, keepdims=True)).astype(bf16).astype(f32)
    mixed = (ugate * dot32(attn * count_key, value.astype(f32))).astype(bf16)
    partial_out = jnp.dot(mixed, plm_out, preferred_element_type=f32)
    state = embed + lax.psum(partial_out, "head")
    frozen = normalize(state)[0].astype(bf16)

    single = jnp.dot(frozen, w_in.astype(bf16), preferred_element_type=f32).astype(bf16)
    pair_low = w_pairin.astype(bf16)
    side_a = jnp.dot(single, pair_low[0], preferred_element_type=f32)
    side_b = jnp.dot(single, pair_low[1], preferred_element_type=f32)
    pair = scores[:, :, None] * vecs[0] + side_a[:, None, :] + side_b[None, :, :]
    normal_one, scale_one = normalize(pair)
    pnorm = (normal_one * vecs[1]).astype(bf16)
    tri_low = w_tri.astype(bf16)
    proj = jnp.einsum("ijc,mcd->mijd", pnorm, tri_low[:5], preferred_element_type=f32)
    sig_left = jax.nn.sigmoid(proj[1])
    sig_right = jax.nn.sigmoid(proj[3])
    gate = jax.nn.sigmoid(proj[4])
    left = (sig_left * proj[0]).astype(bf16).astype(f32)
    right = (sig_right * proj[2]).astype(bf16).astype(f32)
    update = jnp.einsum("ikc,jkc->ijc", left * count[None, :, None], right, precision=highest)
    normal_two, scale_two = normalize(update)
    unorm = (normal_two * vecs[2]).astype(bf16)
    branch = jnp.einsum("ijc,cd->ijd", unorm, tri_low[5], preferred_element_type=f32)
    final = pair + gate * branch
    logit = jnp.einsum("ijc,c->ij", final, vecs[3], precision=highest)

    valid = key_ok * (resolved[0] > 0).astype(f32)
    weight = recycle[0].astype(f32) * valid[:, None] * valid[None, :]
    delta = coords[0][:, :, None] - coords[0][:, None, :]
    true_dist = jnp.sqrt(jnp.sum(delta * delta, 0))
    dist = dot32(dot32(onehot, jax.nn.softplus(logit)), onehot.T)
    diff = dist - true_dist
    root = jnp.sqrt(diff * diff + 1.0)
    loss_sum, loss_count = lax.psum(
        (jnp.sum(weight * (root - 1.0)), jnp.sum(weight)), "grp"
    )
    ddist = dot32(dot32(onehot.T, weight * diff / root), onehot)

    dlogit = ddist / loss_count * jax.nn.sigmoid(logit)
    grad_dist = jnp.einsum("ij,ijc->c", dlogit, final, precision=highest)
    dfinal = dlogit[:, :, None] * vecs[3]
    dbranch = (dfinal * gate).astype(bf16)
    dgate = dfinal * branch
    grad_out = jnp.einsum("ijc,ijd->cd", unorm, dbranch, preferred_element_type=f32)
    dunorm = jnp.einsum("ijd,cd->ijc", dbranch, tri_low[5], preferred_element_type=f32)
    grad_gain_two = jnp.einsum("ijc,ijc->c", dunorm, normal_two, precision=highest)
    dupdate = norm_back(normal_two, scale_two, dunorm * vecs[2])
    dleft = jnp.einsum("ijc,jkc->ikc", dupdate, right, precision=highest) * count[None, :, None]
    dright = jnp.einsum("ijc,ikc->jkc", dupdate, left, precision=highest) * count[None, :, None]
    dproj = jnp.stack(
        [
            dleft * sig_left,
            dleft * proj[0] * sig_left * (1.0 - sig_left),
            dright * sig_right,
            dright * proj[2] * sig_right * (1.0 - sig_right),
            dgate * gate * (1.0 - gate),
        ]
    ).astype(bf16)
    grad_proj = jnp.einsum("ijc,mijd->mcd", pnorm, dproj, preferred_element_type=f32)
    dpnorm = jnp.einsum("mijd,mcd->ijc", dproj, tri_low[:5], preferred_element_type=f32)
    grad_gain_one = jnp.einsum("ijc,ijc->c", dpnorm, normal_one, precision=highest)
    dpair = dfinal + norm_back(normal_one, scale_one, dpnorm * vecs[1])
    grad_scores = jnp.einsum("ij,ijc->c", scores, dpair, precision=highest)
    dside_a = jnp.sum(dpair, 1)
    dside_b = jnp.sum(dpair, 0)
    single32 = single.astype(f32)
    grad_pair = jnp.stack([dot32(single32.T, dside_a), dot32(single32.T, dside_b)])
    dsingle = dot32(dside_a, pair_low[0].astype(f32).T) + dot32(dside_b, pair_low[1].astype(f32).T)
    grad_node = dot32(frozen.astype(f32).T, dsingle)
    grad_tri = jnp.concatenate([grad_proj, grad_out[None]], 0)
    grad_vecs = jnp.stack([grad_scores, grad_gain_one, grad_gain_two, grad_dist])
    grad_in, grad_pairin, grad_tri, grad_vecs = lax.psum(
        (grad_node, grad_pair, grad_tri, grad_vecs), "grp"
    )
    new_row_in, new_col_in, new_in = factored(grad_in, w_in, row_in, col_in)
    new_row_pairin, new_col_pairin, new_pairin = factored(grad_pairin, w_pairin, row_pairin, col_pairin)
    new_row_tri, new_col_tri, new_tri = factored(grad_tri, w_tri, row_tri, col_tri)
    new_sq_vecs, new_vecs = unfactored(grad_vecs, vecs, sq_vecs)
    return (
        loss_sum, loss_count, grad_in, new_row_in, new_col_in, new_in, grad_pairin, new_row_pairin,
        new_col_pairin, new_pairin, grad_tri, new_row_tri, new_col_tri, new_tri, grad_vecs,
        new_sq_vecs, new_vecs,
    )


def solution(mesh):
    whole = P()
    in_specs = (
        P("grp", None), P("grp"), P("grp"), P("grp", None), P("grp", None, None), whole,
        P(None, None, "head"), whole, whole, P("head", None),
    ) + (whole,) * 11
    return jax.shard_map(
        shards, mesh=mesh, in_specs=in_specs, out_specs=(whole,) * 17, check_vma=False
    )
```

```python
import functools
import math

import jax
import jax.numpy as jnp
from jax import lax
from jax.experimental import pallas as pl
from jax.experimental.pallas import tpu as pltpu
from jax.sharding import PartitionSpec as P


STEP = 10
BETA = 1.0 - STEP ** (-0.8)
RATE = 0.3
MESH = pl.DeviceIdType.MESH
f32 = jnp.float32
bf16 = jnp.bfloat16
ROWS = 24
WIDE = 32


def dot(a, b):
    return jnp.dot(a, b, preferred_element_type=f32)


def dot_nt(a, b):
    return lax.dot_general(a, b, (((1,), (1,)), ((), ())), preferred_element_type=f32)


def dot_tn(a, b):
    return lax.dot_general(a, b, (((0,), (0,)), ((), ())), preferred_element_type=f32)


def silu(x):
    return x * jax.nn.sigmoid(x)


def mean_last(x):
    return jnp.mean(x, -1, keepdims=True)


def split(x, parts):
    out = []
    for _ in range(parts):
        part = x.astype(bf16)
        out.append(part)
        x = x - part.astype(f32)
    return out


def iota(shape, dim):
    return lax.broadcasted_iota(jnp.int32, shape, dim)


def tables_kernel(
    tokens_h, lengths_h, recycle_h, resolved_h, coords_h, embed_h, uv_h, qk_h, affine_h, out_h,
    w_in_h, w_pairin_h, w_tri_h, vecs_h,
    frozen_o, single_o, gtri_o, tail_o,
    tokens_v, lengths_s, recycle_s, resolved_v, coords_v, embed_v, uv_v, qk_v, affine_v, out_v,
    w_in_v, w_pairin_v, w_tri_v, vecs_v,
    emb, mixed, part, frozen_v, single_v, w_in_b, w_tri_b, cnt_b, true_d, cols,
    pair, sb, n1, s1, pnorm, proj, sig_l, sig_r, gate, left, right, upd, n2, s2, unorm,
    branch, final, dbranch, dwork, dleft, dright, dproj, stack_d, gtri_v, tail_v,
    load_sem, part_send, part_recv, peer_send, peer_recv, local_sem,
    *, heads, unit_chunk, col_chunk,
):
    grp = lax.axis_index("grp")
    head = lax.axis_index("head")
    other = 1 - grp
    seq = tokens_v.shape[1]
    units = uv_v.shape[2]
    width = emb.shape[1]
    chans = vecs_v.shape[1]
    vocab = embed_v.shape[0]
    n_unit = units // unit_chunk
    n_col = width // col_chunk

    loads = []

    def load(src, dst):
        copy = pltpu.make_async_copy(src, dst, load_sem.at[len(loads)])
        loads.append(copy)
        copy.start()
        return copy

    c_small = [
        load(embed_h, embed_v),
        load(tokens_h, tokens_v),
        load(lengths_h, lengths_s),
        load(recycle_h, recycle_s),
        load(affine_h, affine_v),
    ]
    c_qk = load(qk_h, qk_v)
    c_uv = []
    for c in range(n_unit):
        s = pl.ds(c * unit_chunk, unit_chunk)
        c_uv.append([load(uv_h.at[i, :, s], uv_v.at[i, :, s]) for i in range(2)])
    c_out = []
    for c in range(n_col):
        s = pl.ds(c * col_chunk, col_chunk)
        c_out.append(load(out_h.at[:, s], out_v.at[:, s]))
    c_pairs = [load(resolved_h, resolved_v), load(coords_h, coords_v)]
    c_par = [
        load(w_in_h, w_in_v),
        load(w_pairin_h, w_pairin_v),
        load(w_tri_h, w_tri_v),
        load(vecs_h, vecs_v),
    ]

    barrier = pltpu.get_barrier_semaphore()
    pl.semaphore_signal(barrier, inc=1, device_id={"grp": other}, device_id_type=MESH)
    for d in range(1, heads):
        peer = lax.rem(head + d, heads)
        pl.semaphore_signal(barrier, inc=1, device_id={"head": peer}, device_id_type=MESH)

    for c in c_small:
        c.wait()
    emb[...] = jnp.zeros_like(emb)
    emb[0:vocab, :] = embed_v[...].astype(f32)
    e = emb[...]
    centre = e - mean_last(e)
    normed = (centre * lax.rsqrt(mean_last(centre * centre) + 1e-05)).astype(bf16)

    length = lengths_s[0]
    recycle = recycle_s[0].astype(f32)
    tok = tokens_v[...]
    onehot = (iota((WIDE, seq), 0) == tok).astype(f32)
    key_ok = (iota((1, seq), 1) < length).astype(f32)
    one_b = onehot.astype(bf16)
    cnt_col = jnp.sum(onehot, -1, keepdims=True)
    cnt_b[...] = jnp.broadcast_to(cnt_col, (WIDE, chans))
    ones = jnp.ones((16, seq), bf16)
    cnt_row = dot_nt(ones, one_b)[0:1, :]
    key_row = dot_nt(ones, (onehot * key_ok).astype(bf16))[0:1, :]

    c_qk.wait()
    shared = silu(dot(normed, qk_v[...]))
    query = (shared * affine_v[0:1, :] + affine_v[1:2, :]).astype(bf16)
    keyed = (shared * affine_v[2:3, :] + affine_v[3:4, :]).astype(bf16)
    scores = dot_nt(query, keyed) / math.sqrt(qk_v.shape[1])
    masked = jnp.where(key_row > 0, scores, -1000000000.0)
    top = jnp.exp(masked - jnp.max(masked, -1, keepdims=True))
    attn = (top / jnp.sum(top * key_row, -1, keepdims=True)).astype(bf16).astype(f32)
    attn = jnp.concatenate(split(attn * key_row, 2), 0)

    for c in range(n_unit):
        s = slice(c * unit_chunk, (c + 1) * unit_chunk)
        c_uv[c][0].wait()
        ugate = silu(dot(normed, uv_v[0, :, s]))
        c_uv[c][1].wait()
        value = silu(dot(normed, uv_v[1, :, s])).astype(bf16)
        seen = dot(attn, value)
        mixed[:, s] = (ugate * (seen[0:WIDE] + seen[WIDE : 2 * WIDE])).astype(bf16)

    pl.semaphore_wait(barrier, heads)

    half = col_chunk // 2
    sends = []
    for c in range(n_col):
        s = slice(c * col_chunk, (c + 1) * col_chunk)
        c_out[c].wait()
        p = dot(mixed[...], out_v[:, s])
        part[head, c, :, 0:col_chunk] = p[0:16].astype(bf16)
        part[head, c, :, col_chunk : col_chunk + half] = jnp.concatenate(
            [p[16:24, 0:half], p[16:24, half:col_chunk]], 0
        ).astype(bf16)
        for d in range(1, heads):
            copy = pltpu.make_async_remote_copy(
                src_ref=part.at[head, c],
                dst_ref=part.at[head, c],
                send_sem=part_send.at[d - 1, c],
                recv_sem=part_recv.at[head, c],
                device_id={"head": lax.rem(head + d, heads)},
                device_id_type=MESH,
            )
            copy.start()
            sends.append(copy)

    for c in c_pairs + c_par:
        c.wait()
    w_in_b[...] = w_in_v[...].astype(bf16)
    for m in range(6):
        w_tri_b[:, m * chans : (m + 1) * chans] = w_tri_v[m].astype(bf16)
    valid = key_ok * (resolved_v[...] > 0).astype(f32)
    cols[...] = jnp.zeros_like(cols)
    cols[0:3, :] = coords_v[0]
    cols[3:4, :] = valid
    one_v = (onehot * valid).astype(bf16)
    weight_j = recycle * valid
    blk = 128
    n_blk = seq // blk
    places = []
    for b in range(n_blk):
        t = cols[:, b * blk : (b + 1) * blk].T
        places.append(t)
        d2 = None
        for k in range(3):
            delta = t[:, k : k + 1] - cols[k : k + 1, :]
            d2 = delta * delta if d2 is None else d2 + delta * delta
        true_d[b * blk : (b + 1) * blk, :] = jnp.sqrt(d2)
    n_valid = jnp.sum(valid, -1, keepdims=True)
    loss_count = recycle * n_valid * n_valid

    present = cnt_b[0:ROWS, :] > 0
    sc = jnp.where((cnt_row > 0) & (cnt_col > 0), scores, 0.0)[0:ROWS]

    for c in range(n_col):
        for d in range(1, heads):
            peer = lax.rem(head + d, heads)
            pltpu.make_async_remote_copy(
                src_ref=part.at[peer, c],
                dst_ref=part.at[peer, c],
                send_sem=part_send.at[d - 1, c],
                recv_sem=part_recv.at[peer, c],
                device_id={"head": peer},
                device_id_type=MESH,
            ).wait_recv()
        s = slice(c * col_chunk, (c + 1) * col_chunk)
        low = None
        for k in range(heads):
            a = part[k, c, :, 0:col_chunk].astype(f32)
            b = part[k, c, :, col_chunk : col_chunk + half].astype(f32)
            b = jnp.concatenate([b[0:8], b[8:16]], 1)
            low = [a, b] if low is None else [low[0] + a, low[1] + b]
        emb[0:16, s] += low[0]
        emb[16:24, s] += low[1]
    state = emb[0:ROWS, :]
    centre = state - mean_last(state)
    frozen = centre * lax.rsqrt(mean_last(centre * centre) + 1e-05)
    frozen_v[...] = jnp.concatenate([frozen, jnp.zeros((WIDE - ROWS, width), f32)], 0).astype(bf16)

    peers = []

    def give(src, dst):
        k = len(peers)
        away = pltpu.make_async_remote_copy(
            src_ref=src,
            dst_ref=dst,
            send_sem=peer_send.at[k],
            recv_sem=peer_recv.at[k],
            device_id={"grp": other},
            device_id_type=MESH,
        )
        away.start()
        here = pltpu.make_async_copy(src, dst, local_sem.at[k])
        here.start()
        peers.append((away, here))

    give(frozen_v, frozen_o.at[grp])
    single = dot(frozen_v[...], w_in_b[...]).astype(bf16)
    single_v[...] = single[0:ROWS].astype(f32)
    give(single_v, single_o.at[grp])
    side_a = dot(single, w_pairin_v[0].astype(bf16))[0:ROWS]
    side_b = dot(single, w_pairin_v[1].astype(bf16))[0:ROWS]
    side_a = jnp.where(present, side_a, 0.0)
    side_b = jnp.where(present, side_b, 0.0)
    v0 = vecs_v[0:1, :]
    v1 = vecs_v[1:2, :]
    v2 = vecs_v[2:3, :]
    v3 = vecs_v[3:4, :]
    v0c = v0 - mean_last(v0)
    side_ac = side_a - mean_last(side_a)
    side_bc = side_b - mean_last(side_b)

    n_chunk = ROWS // 2
    two = 2 * ROWS

    def rows(k):
        return slice(k * two, (k + 1) * two)

    def both(f, k):
        return jnp.concatenate([f(2 * k), f(2 * k + 1)], 0)

    for k in range(n_chunk):
        r = rows(k)
        sbk = both(lambda u: jnp.broadcast_to(sc[:, u : u + 1], (ROWS, chans)), k)
        sb[r] = sbk
        pair[r] = sbk * v0 + both(lambda u: side_a + side_b[u : u + 1, :], k)
        centre = sbk * v0c + both(lambda u: side_ac + side_bc[u : u + 1, :], k)
        scale = lax.rsqrt(mean_last(centre * centre) + 1e-05)
        normal = centre * scale
        n1[r] = normal
        s1[r] = jnp.broadcast_to(scale, (two, chans))
        pnorm[r] = (normal * v1).astype(bf16)
    proj[...] = dot(pnorm[...], w_tri_b[:, 0 : 5 * chans])
    for k in range(n_chunk):
        r = rows(k)
        sl = jax.nn.sigmoid(proj[r, chans : 2 * chans])
        sr = jax.nn.sigmoid(proj[r, 3 * chans : 4 * chans])
        sig_l[r] = sl
        sig_r[r] = sr
        left[r] = (sl * proj[r, 0:chans]).astype(bf16).astype(f32)
        right[r] = (sr * proj[r, 2 * chans : 3 * chans]).astype(bf16).astype(f32)
        gate[r] = jax.nn.sigmoid(proj[r, 4 * chans : 5 * chans])
        dwork[r] = left[r] * both(
            lambda u: jnp.broadcast_to(cnt_b[u : u + 1, :], (ROWS, chans)), k
        )

    def triangle(dst, moving, fixed, row_of, weighted):
        group = 4
        for a0 in range(0, ROWS, group):
            total = [None] * group
            for b in range(vocab):
                x = moving(b)
                for q in range(group):
                    y = x * fixed[pl.ds(row_of(a0 + q, b), 1), :]
                    total[q] = y if total[q] is None else total[q] + y
            for q in range(group):
                a = a0 + q
                t = total[q]
                if weighted:
                    t = t * cnt_b[a : a + 1, :]
                dst[a * ROWS : (a + 1) * ROWS, :] = t

    triangle(
        upd, lambda u: dwork[u * ROWS : (u + 1) * ROWS, :], right, lambda v, u: u * ROWS + v, False
    )
    for k in range(n_chunk):
        r = rows(k)
        x = upd[r]
        centre = x - mean_last(x)
        scale = lax.rsqrt(mean_last(centre * centre) + 1e-05)
        normal = centre * scale
        n2[r] = normal
        s2[r] = jnp.broadcast_to(scale, (two, chans))
        unorm[r] = (normal * v2).astype(bf16)
    branch[...] = dot(unorm[...], w_tri_b[:, 5 * chans : 6 * chans])
    lane = iota((ROWS, chans), 1)
    logit = jnp.zeros((ROWS, chans), f32)
    for k in range(n_chunk):
        r = rows(k)
        fin = pair[r] + gate[r] * branch[r]
        final[r] = fin
        col = jnp.sum(fin * v3, -1, keepdims=True)
        for q in range(2):
            logit = jnp.where(lane == 2 * k + q, col[q * ROWS : (q + 1) * ROWS], logit)

    dist = jnp.maximum(logit, 0.0) + jnp.log1p(jnp.exp(-jnp.abs(logit)))
    dist = jnp.concatenate([dist, jnp.zeros((WIDE - ROWS, chans), f32)], 0)
    for k, d in enumerate(split(dist, 3)):
        stack_d[k * WIDE : (k + 1) * WIDE, :] = d
    by_col = dot(stack_d[:, 0:WIDE], one_b).astype(bf16)
    one3 = jnp.concatenate([one_b, one_b, one_b], 0)
    loss_row = jnp.zeros((1, seq), f32)
    by_first = jnp.zeros((WIDE, seq), f32)
    for b in range(n_blk):
        s = slice(b * blk, (b + 1) * blk)
        diff = dot_tn(one3[:, s], by_col) - true_d[s, :]
        sq = diff * diff + 1.0
        inv = lax.rsqrt(sq)
        loss_row = loss_row + jnp.sum(
            places[b][:, 3:4] * (sq * inv - 1.0), 0, keepdims=True
        )
        for q in split(diff * inv, 2):
            by_first = by_first + dot(one_v[:, s], q)
    loss = jnp.sum(loss_row * weight_j, -1, keepdims=True)
    by_pair = dot_nt(jnp.concatenate(split(by_first * weight_j, 2), 0), one_b)
    by_pair = (by_pair[0:WIDE] + by_pair[WIDE : 2 * WIDE])[0:ROWS]
    dlogit = by_pair * jax.nn.sigmoid(logit)[:, 0:WIDE]

    g_dist = jnp.zeros((two, chans), f32)
    for k in range(n_chunk):
        r = rows(k)
        g = both(lambda u: jnp.broadcast_to(dlogit[:, u : u + 1], (ROWS, chans)), k)
        g_dist = g_dist + g * final[r]
        dfinal = g * v3
        gt = gate[r]
        pair[r] = dfinal
        dbranch[r] = (dfinal * gt).astype(bf16)
        dproj[r, 4 * chans : 5 * chans] = (dfinal * branch[r] * gt * (1.0 - gt)).astype(bf16)
    dwork[...] = dot_nt(dbranch[...], w_tri_b[:, 5 * chans : 6 * chans])
    gtri_v[5] = dot_tn(unorm[...], dbranch[...])
    give(gtri_v.at[5], gtri_o.at[grp, 5])
    gtri_v[4] = dot_tn(pnorm[...], dproj[:, 4 * chans : 5 * chans])
    give(gtri_v.at[4], gtri_o.at[grp, 4])
    g_two = jnp.zeros((two, chans), f32)
    for k in range(n_chunk):
        r = rows(k)
        dn = dwork[r]
        normal = n2[r]
        g_two = g_two + dn * normal
        dn = dn * v2
        upd[r] = s2[r] * (dn - mean_last(dn) - normal * mean_last(dn * normal))
    triangle(
        dleft, lambda v: upd[v * ROWS : (v + 1) * ROWS, :], right, lambda u, v: u * ROWS + v, True
    )
    for k in range(n_chunk):
        r = rows(k)
        d, sl = dleft[r], sig_l[r]
        dproj[r, 0:chans] = (d * sl).astype(bf16)
        dproj[r, chans : 2 * chans] = (d * proj[r, 0:chans] * sl * (1.0 - sl)).astype(bf16)
    for m in range(2):
        gtri_v[m] = dot_tn(pnorm[...], dproj[:, m * chans : (m + 1) * chans])
        give(gtri_v.at[m], gtri_o.at[grp, m])
    triangle(
        dright, lambda t: upd[pl.ds(t, ROWS, stride=ROWS), :], left, lambda u, t: u * ROWS + t, True
    )
    for k in range(n_chunk):
        r = rows(k)
        d, sr = dright[r], sig_r[r]
        dproj[r, 2 * chans : 3 * chans] = (d * sr).astype(bf16)
        dproj[r, 3 * chans : 4 * chans] = (
            d * proj[r, 2 * chans : 3 * chans] * sr * (1.0 - sr)
        ).astype(bf16)
    for m in range(2, 4):
        gtri_v[m] = dot_tn(pnorm[...], dproj[:, m * chans : (m + 1) * chans])
        give(gtri_v.at[m], gtri_o.at[grp, m])
    dwork[...] = dot_nt(dproj[...], w_tri_b[:, 0 : 5 * chans])
    g_one = jnp.zeros((two, chans), f32)
    g_score = jnp.zeros((two, chans), f32)
    d_a = jnp.zeros((ROWS, chans), f32)
    tail_v[...] = jnp.zeros_like(tail_v)
    for k in range(n_chunk):
        r = rows(k)
        dn = dwork[r]
        normal = n1[r]
        g_one = g_one + dn * normal
        dn = dn * v1
        dpair = pair[r] + s1[r] * (dn - mean_last(dn) - normal * mean_last(dn * normal))
        g_score = g_score + sb[r] * dpair
        d_a = d_a + dpair[0:ROWS] + dpair[ROWS:two]
        for q in range(2):
            tail_v[2 * k + q : 2 * k + q + 1, chans : 2 * chans] = jnp.sum(
                dpair[q * ROWS : (q + 1) * ROWS], 0, keepdims=True
            )
    tail_v[0:ROWS, 0:chans] = d_a
    for k, g in enumerate((g_score, g_one, g_two, g_dist)):
        tail_v[ROWS + k : ROWS + k + 1, 0:chans] = jnp.sum(g, 0, keepdims=True)
    tail_v[ROWS + 4 : ROWS + 5, 0:chans] = jnp.broadcast_to(loss, (1, chans))
    tail_v[ROWS + 5 : ROWS + 6, 0:chans] = jnp.broadcast_to(loss_count, (1, chans))
    give(tail_v, tail_o.at[grp])

    for c in sends:
        c.wait_send()
    for away, here in peers:
        away.wait()
        here.wait()


def update_kernel(
    frozen_h, single_h, gtri_h, tail_h, w_in_h, w_pairin_h, w_tri_h, vecs_h,
    row_in_h, col_in_h, row_pairin_h, col_pairin_h, row_tri_h, col_tri_h, sq_vecs_h,
    loss_o, count_o, g_in_o, row_in_o, col_in_o, new_in_o, g_pairin_o, row_pairin_o, col_pairin_o,
    new_pairin_o, g_tri_o, row_tri_o, col_tri_o, new_tri_o, g_vecs_o, sq_vecs_o, new_vecs_o,
    frozen_v, single_v, gtri_v, tail_v, w_in_v, w_pairin_v, w_tri_v, vecs_v,
    row_in_v, col_in_v, row_pairin_v, col_pairin_v, row_tri_v, col_tri_v, sq_vecs_v,
    loss_s, count_s, g_in, row_in_n, col_in_n, new_in, g_pairin, row_pairin_n, col_pairin_n,
    new_pairin, g_tri, row_tri_n, col_tri_n, new_tri, g_vecs, sq_vecs_n, new_vecs,
    ds_v, old_v, new_v, load_sem, store_sem,
):
    chans = vecs_v.shape[1]
    width, node = w_in_v.shape
    n_mat = w_tri_v.shape[0]
    loads = []

    def load(src, dst):
        copy = pltpu.make_async_copy(src, dst, load_sem.at[len(loads)])
        loads.append(copy)
        copy.start()
        return copy

    c_tail = load(tail_h, tail_v)
    c_pw = load(w_pairin_h, w_pairin_v)
    c_frozen = [
        load(frozen_h.at[i % 2], frozen_v.at[pl.ds(i * WIDE, WIDE)]) for i in range(4)
    ]
    c_single = load(single_h, single_v)
    c_gtri = load(gtri_h, gtri_v)
    c_small = [
        load(row_in_h, row_in_v), load(col_in_h, col_in_v), load(row_pairin_h, row_pairin_v),
        load(col_pairin_h, col_pairin_v), load(row_tri_h, row_tri_v), load(col_tri_h, col_tri_v),
        load(sq_vecs_h, sq_vecs_v), load(vecs_h, vecs_v),
    ]
    c_tri = load(w_tri_h, w_tri_v)
    c_in = load(w_in_h, w_in_v)
    stores = []

    def store(src, dst):
        copy = pltpu.make_async_copy(src, dst, store_sem.at[len(stores)])
        stores.append(copy)
        copy.start()

    c_tail.wait()
    totals = tail_v[0, ROWS : ROWS + 8, 0:chans] + tail_v[1, ROWS : ROWS + 8, 0:chans]
    loss_s[...] = totals[4:5, :]
    count_s[...] = totals[5:6, :]
    inv = 1.0 / totals[5:6, :]
    inv2 = jnp.concatenate([inv, inv], 1)
    d_side = [tail_v[i, 0:ROWS, :] * inv2 for i in range(2)]

    c_pw.wait()
    pads = jnp.zeros((WIDE - ROWS, node), f32)
    halves = [[], []]
    side_parts = []
    for i in range(2):
        parts = split(d_side[i], 2)
        side_parts.append(parts)
        st = jnp.concatenate([p.astype(f32) for p in parts], 0).astype(bf16)
        ds = dot_nt(st[:, 0:chans], w_pairin_v[0].astype(bf16)) + dot_nt(
            st[:, chans : 2 * chans], w_pairin_v[1].astype(bf16)
        )
        ds = ds[0:ROWS] + ds[ROWS : 2 * ROWS]
        for k, p in enumerate(split(ds, 2)):
            at = (2 * k + i) * WIDE
            ds_v[at : at + WIDE, :] = jnp.concatenate([p.astype(f32), pads], 0).astype(bf16)
    for c in c_frozen:
        c.wait()
    g_in[...] = dot_tn(frozen_v[...], ds_v[...])
    store(g_in, g_in_o)

    c_single.wait()
    sg = jnp.concatenate([single_v[0], single_v[1], single_v[0], single_v[1]], 0).astype(bf16)
    st = jnp.concatenate(
        [side_parts[i][k].astype(f32) for k in range(2) for i in range(2)], 0
    ).astype(bf16)
    for k in range(2):
        g_pairin[k] = dot_tn(sg, st[:, k * chans : (k + 1) * chans])
    store(g_pairin, g_pairin_o)

    c_gtri.wait()
    for m in range(n_mat):
        g_tri[m] = (gtri_v[0, m] + gtri_v[1, m]) * inv
    store(g_tri, g_tri_o)
    for c in c_small:
        c.wait()
    g_vecs[...] = totals[0:4, :] * inv
    store(g_vecs, g_vecs_o)

    n_in = width // chans
    n_pr = w_pairin_v.shape[1] // chans
    old_v[...] = jnp.zeros_like(old_v)
    for b in range(n_in):
        old_v[b : b + 1, :] = row_in_v[b : b + 1, :]
    at_pair = n_in
    for k in range(2):
        for b in range(n_pr):
            j = at_pair + k * n_pr + b
            old_v[j : j + 1, :] = row_pairin_v[k : k + 1, b * chans : (b + 1) * chans]
    at_tri = at_pair + 2 * n_pr
    old_v[at_tri : at_tri + n_mat, :] = row_tri_v[...]
    old = old_v[...].T
    lane = iota((chans, chans), 1)
    fresh = [jnp.zeros((chans, chans), f32)]

    def whole(x):
        return jnp.sum(jnp.sum(x, 0, keepdims=True), -1, keepdims=True)

    def adafactor(grad, weight, new, col_old, n_blk, at, n_cols, set_col):
        n_rows = n_blk * chans
        colsum = jnp.zeros((8, n_cols), f32)
        scaled = jnp.zeros((8, n_cols), f32)
        rowsum = jnp.zeros((chans, 1), f32)
        wsum = jnp.zeros((8, n_cols), f32)
        roots = []

        def fold(x):
            return jnp.sum(x.reshape(chans // 8, 8, n_cols), 0)

        for b in range(n_blk):
            s = slice(b * chans, (b + 1) * chans)
            g = grad(s)
            sq = g * g + 1e-30
            row = BETA * old[:, at + b : at + b + 1] + (1.0 - BETA) * mean_last(sq)
            fresh[0] = jnp.where(lane == at + b, row, fresh[0])
            rowsum = rowsum + row
            root = lax.rsqrt(row)
            roots.append(root)
            colsum = colsum + fold(sq)
            step = g * root
            scaled = scaled + fold(step * step)
            w = weight(s)
            wsum = wsum + fold(w * w)
        col = BETA * col_old + (1.0 - BETA) / n_rows * jnp.sum(colsum, 0, keepdims=True)
        set_col(col)
        row_mean = jnp.sum(rowsum, 0, keepdims=True) / n_rows
        size = n_rows * n_cols
        rms = jnp.sqrt(row_mean * jnp.sum(
            jnp.sum(scaled, 0, keepdims=True) / col, -1, keepdims=True
        ) / size)
        scale = jnp.maximum(0.001, jnp.sqrt(whole(wsum) / size))
        coef = RATE * scale / jnp.maximum(1.0, rms) * jnp.sqrt(row_mean)
        by_col = lax.rsqrt(col) * coef
        for b in range(n_blk):
            s = slice(b * chans, (b + 1) * chans)
            new(s, weight(s) - grad(s) * roots[b] * by_col)

    c_in.wait()
    n_half = col_in_v.shape[0]

    def set_in(col):
        for k in range(n_half):
            col_in_n[k : k + 1, :] = col[:, k * chans : (k + 1) * chans]

    def new_in_set(s, x):
        new_in[s, :] = x

    adafactor(
        lambda s: g_in[s, :], lambda s: w_in_v[s, :], new_in_set,
        jnp.concatenate([col_in_v[k : k + 1, :] for k in range(n_half)], 1), n_in, 0, node, set_in,
    )
    store(new_in, new_in_o)
    store(col_in_n, col_in_o)
    for k in range(2):
        def set_pair(col, k=k):
            col_pairin_n[k : k + 1, :] = col

        def new_pair(s, x, k=k):
            new_pairin[k, s, :] = x

        adafactor(
            lambda s, k=k: g_pairin[k, s, :], lambda s, k=k: w_pairin_v[k, s, :], new_pair,
            col_pairin_v[k : k + 1, :], n_pr, at_pair + k * n_pr, chans, set_pair,
        )
    store(new_pairin, new_pairin_o)
    store(col_pairin_n, col_pairin_o)
    c_tri.wait()
    for m in range(n_mat):
        def set_tri(col, m=m):
            col_tri_n[m : m + 1, :] = col

        def new_tri_set(s, x, m=m):
            new_tri[m, s, :] = x

        adafactor(
            lambda s, m=m: g_tri[m, s, :], lambda s, m=m: w_tri_v[m, s, :], new_tri_set,
            col_tri_v[m : m + 1, :], 1, at_tri + m, chans, set_tri,
        )
    store(new_tri, new_tri_o)
    store(col_tri_n, col_tri_o)
    new_v[...] = fresh[0].T
    for b in range(n_in):
        row_in_n[b : b + 1, :] = new_v[b : b + 1, :]
    for k in range(2):
        for b in range(n_pr):
            j = at_pair + k * n_pr + b
            row_pairin_n[k : k + 1, b * chans : (b + 1) * chans] = new_v[j : j + 1, :]
    row_tri_n[...] = new_v[at_tri : at_tri + n_mat, :]
    store(row_in_n, row_in_o)
    store(row_pairin_n, row_pairin_o)
    store(row_tri_n, row_tri_o)

    g = g_vecs[...]
    sq = BETA * sq_vecs_v[...] + (1.0 - BETA) * (g * g + 1e-30)
    sq_vecs_n[...] = sq
    step = g * lax.rsqrt(sq)
    step = step / jnp.maximum(1.0, jnp.sqrt(mean_last(step * step)))
    v = vecs_v[...]
    scale = jnp.maximum(0.001, jnp.sqrt(mean_last(v * v)))
    new_vecs[...] = v - RATE * scale * step
    store(sq_vecs_n, sq_vecs_o)
    store(new_vecs, new_vecs_o)
    store(loss_s, loss_o)
    store(count_s, count_o)
    for c in stores:
        c.wait()


def shards(
    tokens, lengths, recycle, resolved, coords, plm_embed, plm_uv, plm_qk, plm_affine, plm_out,
    w_in, w_pairin, w_tri, vecs, row_in, col_in, row_pairin, col_pairin, row_tri, col_tri, sq_vecs,
):
    heads = lax.axis_size("head")
    seq = tokens.shape[1]
    width = plm_embed.shape[1]
    units = plm_uv.shape[2]
    chans = vecs.shape[1]
    node = w_in.shape[1]
    unit_chunk = 256 if units % 256 == 0 else 128
    col_chunk = 256
    n_unit, n_col = units // unit_chunk, width // col_chunk
    anywhere = pl.BlockSpec(memory_space=pl.ANY)
    table = ROWS * ROWS

    def vm(*shape, dtype=f32):
        return pltpu.VMEM(shape, dtype)

    def like(x):
        return pltpu.VMEM(x.shape, x.dtype)

    operands = (
        tokens, lengths, recycle, resolved, coords, plm_embed, plm_uv, plm_qk, plm_affine, plm_out,
        w_in, w_pairin, w_tri, vecs,
    )
    scratch = [
        like(tokens), pltpu.SMEM((1,), jnp.int32), pltpu.SMEM((1,), jnp.int32), like(resolved),
        like(coords), like(plm_embed), like(plm_uv), like(plm_qk), like(plm_affine), like(plm_out),
        like(w_in), like(w_pairin), like(w_tri), like(vecs),
        vm(WIDE, width), vm(WIDE, units, dtype=bf16),
        vm(heads, n_col, 16, col_chunk + col_chunk // 2, dtype=bf16),
        vm(WIDE, width, dtype=bf16), vm(ROWS, node), vm(width, node, dtype=bf16),
        vm(chans, 6 * chans, dtype=bf16), vm(WIDE, chans), vm(seq, seq), vm(chans, seq),
        vm(table, chans), vm(table, chans), vm(table, chans), vm(table, chans),
        vm(table, chans, dtype=bf16), vm(table, 5 * chans), vm(table, chans), vm(table, chans),
        vm(table, chans), vm(table, chans), vm(table, chans), vm(table, chans), vm(table, chans),
        vm(table, chans), vm(table, chans, dtype=bf16),
        vm(table, chans), vm(table, chans), vm(table, chans, dtype=bf16), vm(table, chans),
        vm(table, chans), vm(table, chans), vm(table, 5 * chans, dtype=bf16),
        vm(3 * WIDE, chans, dtype=bf16), vm(6, chans, chans), vm(WIDE, 2 * chans),
        pltpu.SemaphoreType.DMA((12 + 2 * n_unit + n_col,)),
        pltpu.SemaphoreType.DMA((heads - 1, n_col)), pltpu.SemaphoreType.DMA((heads, n_col)),
        pltpu.SemaphoreType.DMA((9,)), pltpu.SemaphoreType.DMA((9,)), pltpu.SemaphoreType.DMA((9,)),
    ]
    sds = jax.ShapeDtypeStruct
    frozen, single, gtri, tail = pl.pallas_call(
        functools.partial(tables_kernel, heads=heads, unit_chunk=unit_chunk, col_chunk=col_chunk),
        out_shape=(
            sds((2, WIDE, width), bf16), sds((2, ROWS, node), f32), sds((2, 6, chans, chans), f32),
            sds((2, WIDE, 2 * chans), f32),
        ),
        in_specs=[anywhere] * len(operands),
        out_specs=[anywhere] * 4,
        scratch_shapes=scratch,
        compiler_params=pltpu.CompilerParams(
            collective_id=0, has_side_effects=True, vmem_limit_bytes=48 << 20
        ),
        name="tables",
    )(*operands)

    row_in2 = row_in.reshape(-1, chans)
    col_in2 = col_in.reshape(-1, chans)
    operands = (
        frozen, single, gtri, tail, w_in, w_pairin, w_tri, vecs, row_in2, col_in2, row_pairin,
        col_pairin, row_tri, col_tri, sq_vecs,
    )
    outs = (
        sds((1, chans), f32), sds((1, chans), f32), w_in, row_in2, col_in2, w_in, w_pairin,
        row_pairin, col_pairin, w_pairin, w_tri, row_tri, col_tri, w_tri, vecs, vecs, vecs,
    )
    outs = tuple(sds(x.shape, x.dtype) for x in outs)
    scratch = (
        [vm(4 * WIDE, width, dtype=bf16)] + [like(x) for x in operands[1:]] + [like(x) for x in outs]
        + [
            vm(4 * WIDE, node, dtype=bf16), vm(chans, chans), vm(chans, chans),
            pltpu.SemaphoreType.DMA((18,)), pltpu.SemaphoreType.DMA((17,)),
        ]
    )
    res = list(
        pl.pallas_call(
            update_kernel,
            out_shape=outs,
            in_specs=[anywhere] * len(operands),
            out_specs=[anywhere] * len(outs),
            scratch_shapes=scratch,
            compiler_params=pltpu.CompilerParams(vmem_limit_bytes=32 << 20),
            name="update",
        )(*operands)
    )
    res[0] = res[0][0, 0]
    res[1] = res[1][0, 0]
    res[3] = res[3].reshape(-1)
    res[4] = res[4].reshape(-1)
    return tuple(res)


def solution(mesh):
    whole = P()
    in_specs = (
        P("grp", None), P("grp"), P("grp"), P("grp", None), P("grp", None, None), whole,
        P(None, None, "head"), whole, whole, P("head", None),
    ) + (whole,) * 11
    return jax.shard_map(
        shards, mesh=mesh, in_specs=in_specs, out_specs=(whole,) * 17, check_vma=False
    )
```

```python
import functools
import math

import jax
import jax.numpy as jnp
from jax import lax
from jax.experimental import pallas as pl
from jax.experimental.pallas import tpu as pltpu
from jax.sharding import PartitionSpec as P


STEP = 10
BETA = 1.0 - STEP ** (-0.8)
RATE = 0.3
MESH = pl.DeviceIdType.MESH
f32 = jnp.float32
bf16 = jnp.bfloat16
ROWS = 24
WIDE = 32


def dot(a, b):
    return jnp.dot(a, b, preferred_element_type=f32)


def dot_nt(a, b):
    return lax.dot_general(a, b, (((1,), (1,)), ((), ())), preferred_element_type=f32)


def dot_tn(a, b):
    return lax.dot_general(a, b, (((0,), (0,)), ((), ())), preferred_element_type=f32)


def silu(x):
    return x * jax.nn.sigmoid(x)


def mean_last(x):
    return jnp.mean(x, -1, keepdims=True)


def split(x, parts):
    out = []
    for _ in range(parts):
        part = x.astype(bf16)
        out.append(part)
        x = x - part.astype(f32)
    return out


def iota(shape, dim):
    return lax.broadcasted_iota(jnp.int32, shape, dim)


def tables_kernel(
    tokens_h, lengths_s, recycle_s, resolved_h, coords_h, embed_h, uv_h, qk_h, affine_h, out_h,
    w_in_h, w_pairin_h, w_tri_h, vecs_h, row_in_h, row_pairin_h, row_tri_h,
    frozen_o, single_o, gtri_o, tail_o, old_o, scale_o,
    tokens_v, resolved_v, coords_v, embed_v, uv_v, qk_v, affine_v, out_v,
    w_in_v, w_pairin_v, w_tri_v, vecs_v, row_in_v, row_pairin_v, row_tri_v,
    emb, mixed, part, w_in_b, w_tri_b, cnt_b, true_d, cols,
    pair, sb, n1, s1, pnorm, proj, sig_l, sig_r, gate, left, right, upd, n2, s2, unorm,
    branch, final, dbranch, dwork, dleft, dright, dproj, stack_d, old_v,
    load_sem, part_send, part_recv, peer_send, peer_recv,
    *, heads, unit_chunk, depth_chunk,
):
    grp = lax.axis_index("grp")
    head = lax.axis_index("head")
    other = 1 - grp
    seq = tokens_v.shape[1]
    units = uv_v.shape[2]
    width = emb.shape[1]
    chans = vecs_v.shape[1]
    vocab = embed_v.shape[0]
    n_unit = units // unit_chunk
    n_depth = units // depth_chunk
    half = width // 2

    loads = []

    def load(src, dst):
        copy = pltpu.make_async_copy(src, dst, load_sem.at[len(loads)])
        loads.append(copy)
        copy.start()
        return copy

    c_small = [
        load(embed_h, embed_v),
        load(tokens_h, tokens_v),
        load(affine_h, affine_v),
    ]
    c_qk = load(qk_h, qk_v)
    c_uv = []
    for c in range(n_unit):
        s = pl.ds(c * unit_chunk, unit_chunk)
        c_uv.append([load(uv_h.at[i, :, s], uv_v.at[i, :, s]) for i in range(2)])
    c_out = []
    for c in range(n_depth):
        s = pl.ds(c * depth_chunk, depth_chunk)
        c_out.append(load(out_h.at[s], out_v.at[s]))
    c_pairs = [load(resolved_h, resolved_v), load(coords_h, coords_v)]
    c_par = [
        load(w_in_h, w_in_v),
        load(w_pairin_h, w_pairin_v),
        load(w_tri_h, w_tri_v),
        load(vecs_h, vecs_v),
        load(row_in_h, row_in_v),
        load(row_pairin_h, row_pairin_v),
        load(row_tri_h, row_tri_v),
    ]

    barrier = pltpu.get_barrier_semaphore()
    pl.semaphore_signal(barrier, inc=1, device_id={"grp": other}, device_id_type=MESH)
    for d in range(1, heads):
        peer = lax.rem(head + d, heads)
        pl.semaphore_signal(barrier, inc=1, device_id={"head": peer}, device_id_type=MESH)

    for c in c_small:
        c.wait()
    emb[...] = jnp.zeros_like(emb)
    emb[0:vocab, :] = embed_v[...].astype(f32)
    e = emb[...]
    centre = e - mean_last(e)
    normed = (centre * lax.rsqrt(mean_last(centre * centre) + 1e-05)).astype(bf16)

    length = lengths_s[0]
    recycle = recycle_s[0].astype(f32)
    tok = tokens_v[...]
    onehot = (iota((WIDE, seq), 0) == tok).astype(f32)
    key_ok = (iota((1, seq), 1) < length).astype(f32)
    one_b = onehot.astype(bf16)
    cnt_col = jnp.sum(onehot, -1, keepdims=True)
    cnt_b[...] = jnp.broadcast_to(cnt_col, (WIDE, chans))
    ones = jnp.ones((16, seq), bf16)
    cnt_row = dot_nt(ones, one_b)[0:1, :]
    key_row = dot_nt(ones, (onehot * key_ok).astype(bf16))[0:1, :]

    c_qk.wait()
    shared = silu(dot(normed, qk_v[...]))
    query = (shared * affine_v[0:1, :] + affine_v[1:2, :]).astype(bf16)
    keyed = (shared * affine_v[2:3, :] + affine_v[3:4, :]).astype(bf16)
    scores = dot_nt(query, keyed) / math.sqrt(qk_v.shape[1])
    masked = jnp.where(key_row > 0, scores, -1000000000.0)
    top = jnp.exp(masked - jnp.max(masked, -1, keepdims=True))
    attn = (top / jnp.sum(top * key_row, -1, keepdims=True)).astype(bf16).astype(f32)
    attn = jnp.concatenate(split(attn * key_row, 2), 0)

    for c in range(n_unit):
        s = slice(c * unit_chunk, (c + 1) * unit_chunk)
        c_uv[c][0].wait()
        ugate = silu(dot(normed, uv_v[0, :, s]))
        c_uv[c][1].wait()
        value = silu(dot(normed, uv_v[1, :, s])).astype(bf16)
        seen = dot(attn, value)
        mixed[:, s] = (ugate * (seen[0:WIDE] + seen[WIDE : 2 * WIDE])).astype(bf16)

    pl.semaphore_wait(barrier, heads)

    p = None
    for c in range(n_depth):
        s = slice(c * depth_chunk, (c + 1) * depth_chunk)
        c_out[c].wait()
        q = dot(mixed[:, s], out_v[s, :])
        p = q if p is None else p + q
    part[head, :, 0:width] = p[0:16].astype(bf16)
    part[head, :, width : width + half] = jnp.concatenate(
        [p[16:24, 0:half], p[16:24, half:width]], 0
    ).astype(bf16)
    sends = []
    for d in range(1, heads):
        copy = pltpu.make_async_remote_copy(
            src_ref=part.at[head],
            dst_ref=part.at[head],
            send_sem=part_send.at[d - 1],
            recv_sem=part_recv.at[head],
            device_id={"head": lax.rem(head + d, heads)},
            device_id_type=MESH,
        )
        copy.start()
        sends.append(copy)

    for c in c_pairs + c_par:
        c.wait()
    w_in_b[...] = w_in_v[...].astype(bf16)
    for m in range(6):
        w_tri_b[:, m * chans : (m + 1) * chans] = w_tri_v[m].astype(bf16)
    valid = key_ok * (resolved_v[...] > 0).astype(f32)
    cols[...] = jnp.zeros_like(cols)
    for k in range(3):
        cols[k : k + 1, :] = coords_v[k]
    cols[3:4, :] = valid
    one_v = (onehot * valid).astype(bf16)
    weight_j = recycle * valid
    blk = 128
    n_blk = seq // blk
    places = []
    for b in range(n_blk):
        t = cols[:, b * blk : (b + 1) * blk].T
        places.append(t)
        d2 = None
        for k in range(3):
            delta = t[:, k : k + 1] - cols[k : k + 1, :]
            d2 = delta * delta if d2 is None else d2 + delta * delta
        true_d[b * blk : (b + 1) * blk, :] = jnp.sqrt(d2)
    n_valid = jnp.sum(valid, -1, keepdims=True)
    loss_count = recycle * n_valid * n_valid

    present = cnt_b[0:ROWS, :] > 0
    sc = jnp.where((cnt_row > 0) & (cnt_col > 0), scores, 0.0)[0:ROWS]

    n_in = width // chans
    n_pr = w_pairin_v.shape[1] // chans
    at_tri = n_in + 2 * n_pr
    old_v[...] = jnp.zeros_like(old_v)
    old_v[0:n_in, :] = row_in_v[...]
    for k in range(2):
        for b in range(n_pr):
            j = n_in + k * n_pr + b
            old_v[j : j + 1, :] = row_pairin_v[k : k + 1, b * chans : (b + 1) * chans]
    old_v[at_tri : at_tri + 6, :] = row_tri_v[...]
    old = BETA * old_v[...].T
    for k in range(at_tri + 6):
        old_o[k * chans : (k + 1) * chans, :] = jnp.broadcast_to(old[:, k : k + 1], (chans, chans))
    scale_o[...] = jnp.zeros_like(scale_o)
    mats = [w_in_v] + [w_pairin_v.at[k] for k in range(2)] + [w_tri_v.at[m] for m in range(6)]
    for k, w in enumerate(mats):
        x = w[...]
        x = jnp.sum(jnp.sum(x * x, 0, keepdims=True), -1, keepdims=True) / (w.shape[0] * w.shape[1])
        x = RATE * jnp.maximum(0.001, jnp.sqrt(x))
        scale_o[k : k + 1, :] = jnp.broadcast_to(x, (1, chans))

    for d in range(1, heads):
        peer = lax.rem(head + d, heads)
        pltpu.make_async_remote_copy(
            src_ref=part.at[peer],
            dst_ref=part.at[peer],
            send_sem=part_send.at[d - 1],
            recv_sem=part_recv.at[peer],
            device_id={"head": peer},
            device_id_type=MESH,
        ).wait_recv()
    low = None
    for k in range(heads):
        a = part[k, :, 0:width].astype(f32)
        b = part[k, :, width : width + half].astype(f32)
        b = jnp.concatenate([b[0:8], b[8:16]], 1)
        low = [a, b] if low is None else [low[0] + a, low[1] + b]
    emb[0:16, :] += low[0]
    emb[16:24, :] += low[1]
    state = emb[0:ROWS, :]
    centre = state - mean_last(state)
    frozen = centre * lax.rsqrt(mean_last(centre * centre) + 1e-05)
    frozen = jnp.concatenate([frozen, jnp.zeros((WIDE - ROWS, width), f32)], 0).astype(bf16)
    frozen_o[grp] = frozen

    peers = []

    def give(ref):
        k = len(peers)
        copy = pltpu.make_async_remote_copy(
            src_ref=ref,
            dst_ref=ref,
            send_sem=peer_send.at[k],
            recv_sem=peer_recv.at[k],
            device_id={"grp": other},
            device_id_type=MESH,
        )
        copy.start()
        peers.append(copy)

    give(frozen_o.at[grp])
    single = dot(frozen, w_in_b[...]).astype(bf16)
    single_o[grp] = single[0:ROWS].astype(f32)
    give(single_o.at[grp])
    side_a = dot(single, w_pairin_v[0].astype(bf16))[0:ROWS]
    side_b = dot(single, w_pairin_v[1].astype(bf16))[0:ROWS]
    side_a = jnp.where(present, side_a, 0.0)
    side_b = jnp.where(present, side_b, 0.0)
    v0 = vecs_v[0:1, :]
    v1 = vecs_v[1:2, :]
    v2 = vecs_v[2:3, :]
    v3 = vecs_v[3:4, :]
    v0c = v0 - mean_last(v0)
    side_ac = side_a - mean_last(side_a)
    side_bc = side_b - mean_last(side_b)

    n_chunk = ROWS // 2
    two = 2 * ROWS

    def rows(k):
        return slice(k * two, (k + 1) * two)

    def both(f, k):
        return jnp.concatenate([f(2 * k), f(2 * k + 1)], 0)

    for k in range(n_chunk):
        r = rows(k)
        sbk = both(lambda u: jnp.broadcast_to(sc[:, u : u + 1], (ROWS, chans)), k)
        sb[r] = sbk
        pair[r] = sbk * v0 + both(lambda u: side_a + side_b[u : u + 1, :], k)
        centre = sbk * v0c + both(lambda u: side_ac + side_bc[u : u + 1, :], k)
        scale = lax.rsqrt(mean_last(centre * centre) + 1e-05)
        normal = centre * scale
        n1[r] = normal
        s1[r] = jnp.broadcast_to(scale, (two, chans))
        pnorm[r] = (normal * v1).astype(bf16)
    proj[...] = dot(pnorm[...], w_tri_b[:, 0 : 5 * chans])
    for k in range(n_chunk):
        r = rows(k)
        sl = jax.nn.sigmoid(proj[r, chans : 2 * chans])
        sr = jax.nn.sigmoid(proj[r, 3 * chans : 4 * chans])
        sig_l[r] = sl
        sig_r[r] = sr
        left[r] = (sl * proj[r, 0:chans]).astype(bf16).astype(f32)
        right[r] = (sr * proj[r, 2 * chans : 3 * chans]).astype(bf16).astype(f32)
        gate[r] = jax.nn.sigmoid(proj[r, 4 * chans : 5 * chans])
        dwork[r] = left[r] * both(
            lambda u: jnp.broadcast_to(cnt_b[u : u + 1, :], (ROWS, chans)), k
        )

    def triangle(dst, moving, fixed, row_of, weighted):
        group = 4
        for a0 in range(0, ROWS, group):
            total = [None] * group
            for b in range(vocab):
                x = moving(b)
                for q in range(group):
                    y = x * fixed[pl.ds(row_of(a0 + q, b), 1), :]
                    total[q] = y if total[q] is None else total[q] + y
            for q in range(group):
                a = a0 + q
                t = total[q]
                if weighted:
                    t = t * cnt_b[a : a + 1, :]
                dst[a * ROWS : (a + 1) * ROWS, :] = t

    triangle(
        upd, lambda u: dwork[u * ROWS : (u + 1) * ROWS, :], right, lambda v, u: u * ROWS + v, False
    )
    for k in range(n_chunk):
        r = rows(k)
        x = upd[r]
        centre = x - mean_last(x)
        scale = lax.rsqrt(mean_last(centre * centre) + 1e-05)
        normal = centre * scale
        n2[r] = normal
        s2[r] = jnp.broadcast_to(scale, (two, chans))
        unorm[r] = (normal * v2).astype(bf16)
    branch[...] = dot(unorm[...], w_tri_b[:, 5 * chans : 6 * chans])
    lane = iota((ROWS, chans), 1)
    logit = jnp.zeros((ROWS, chans), f32)
    for k in range(n_chunk):
        r = rows(k)
        fin = pair[r] + gate[r] * branch[r]
        final[r] = fin
        col = jnp.sum(fin * v3, -1, keepdims=True)
        for q in range(2):
            logit = jnp.where(lane == 2 * k + q, col[q * ROWS : (q + 1) * ROWS], logit)

    dist = jnp.maximum(logit, 0.0) + jnp.log1p(jnp.exp(-jnp.abs(logit)))
    dist = jnp.concatenate([dist, jnp.zeros((WIDE - ROWS, chans), f32)], 0)
    for k, d in enumerate(split(dist, 3)):
        stack_d[k * WIDE : (k + 1) * WIDE, :] = d
    by_col = dot(stack_d[:, 0:WIDE], one_b).astype(bf16)
    one3 = jnp.concatenate([one_b, one_b, one_b], 0)
    loss_row = jnp.zeros((1, seq), f32)
    by_first = jnp.zeros((WIDE, seq), f32)
    for b in range(n_blk):
        s = slice(b * blk, (b + 1) * blk)
        diff = dot_tn(one3[:, s], by_col) - true_d[s, :]
        sq = diff * diff + 1.0
        inv = lax.rsqrt(sq)
        loss_row = loss_row + jnp.sum(
            places[b][:, 3:4] * (sq * inv - 1.0), 0, keepdims=True
        )
        for q in split(diff * inv, 2):
            by_first = by_first + dot(one_v[:, s], q)
    loss = jnp.sum(loss_row * weight_j, -1, keepdims=True)
    by_pair = dot_nt(jnp.concatenate(split(by_first * weight_j, 2), 0), one_b)
    by_pair = (by_pair[0:WIDE] + by_pair[WIDE : 2 * WIDE])[0:ROWS]
    dlogit = by_pair * jax.nn.sigmoid(logit)[:, 0:WIDE]

    g_dist = jnp.zeros((two, chans), f32)
    for k in range(n_chunk):
        r = rows(k)
        g = both(lambda u: jnp.broadcast_to(dlogit[:, u : u + 1], (ROWS, chans)), k)
        g_dist = g_dist + g * final[r]
        dfinal = g * v3
        gt = gate[r]
        pair[r] = dfinal
        dbranch[r] = (dfinal * gt).astype(bf16)
        dproj[r, 4 * chans : 5 * chans] = (dfinal * branch[r] * gt * (1.0 - gt)).astype(bf16)
    dwork[...] = dot_nt(dbranch[...], w_tri_b[:, 5 * chans : 6 * chans])
    gtri_o[grp, 5] = dot_tn(unorm[...], dbranch[...])
    give(gtri_o.at[grp, 5])
    gtri_o[grp, 4] = dot_tn(pnorm[...], dproj[:, 4 * chans : 5 * chans])
    give(gtri_o.at[grp, 4])
    g_two = jnp.zeros((two, chans), f32)
    for k in range(n_chunk):
        r = rows(k)
        dn = dwork[r]
        normal = n2[r]
        g_two = g_two + dn * normal
        dn = dn * v2
        upd[r] = s2[r] * (dn - mean_last(dn) - normal * mean_last(dn * normal))
    triangle(
        dleft, lambda v: upd[v * ROWS : (v + 1) * ROWS, :], right, lambda u, v: u * ROWS + v, True
    )
    for k in range(n_chunk):
        r = rows(k)
        d, sl = dleft[r], sig_l[r]
        dproj[r, 0:chans] = (d * sl).astype(bf16)
        dproj[r, chans : 2 * chans] = (d * proj[r, 0:chans] * sl * (1.0 - sl)).astype(bf16)
    for m in range(2):
        gtri_o[grp, m] = dot_tn(pnorm[...], dproj[:, m * chans : (m + 1) * chans])
        give(gtri_o.at[grp, m])
    triangle(
        dright, lambda t: upd[pl.ds(t, ROWS, stride=ROWS), :], left, lambda u, t: u * ROWS + t, True
    )
    for k in range(n_chunk):
        r = rows(k)
        d, sr = dright[r], sig_r[r]
        dproj[r, 2 * chans : 3 * chans] = (d * sr).astype(bf16)
        dproj[r, 3 * chans : 4 * chans] = (
            d * proj[r, 2 * chans : 3 * chans] * sr * (1.0 - sr)
        ).astype(bf16)
    for m in range(2, 4):
        gtri_o[grp, m] = dot_tn(pnorm[...], dproj[:, m * chans : (m + 1) * chans])
        give(gtri_o.at[grp, m])
    dwork[...] = dot_nt(dproj[...], w_tri_b[:, 0 : 5 * chans])
    g_one = jnp.zeros((two, chans), f32)
    g_score = jnp.zeros((two, chans), f32)
    d_a = jnp.zeros((ROWS, chans), f32)
    tail_o[grp] = jnp.zeros((WIDE, 2 * chans), f32)
    for k in range(n_chunk):
        r = rows(k)
        dn = dwork[r]
        normal = n1[r]
        g_one = g_one + dn * normal
        dn = dn * v1
        dpair = pair[r] + s1[r] * (dn - mean_last(dn) - normal * mean_last(dn * normal))
        g_score = g_score + sb[r] * dpair
        d_a = d_a + dpair[0:ROWS] + dpair[ROWS:two]
        for q in range(2):
            tail_o[grp, 2 * k + q : 2 * k + q + 1, chans : 2 * chans] = jnp.sum(
                dpair[q * ROWS : (q + 1) * ROWS], 0, keepdims=True
            )
    tail_o[grp, 0:ROWS, 0:chans] = d_a
    for k, g in enumerate((g_score, g_one, g_two, g_dist)):
        tail_o[grp, ROWS + k : ROWS + k + 1, 0:chans] = jnp.sum(g, 0, keepdims=True)
    tail_o[grp, ROWS + 4 : ROWS + 5, 0:chans] = jnp.broadcast_to(loss, (1, chans))
    tail_o[grp, ROWS + 5 : ROWS + 6, 0:chans] = jnp.broadcast_to(loss_count, (1, chans))
    give(tail_o.at[grp])

    for c in sends:
        c.wait_send()
    for c in peers:
        c.wait()


def update_kernel(
    frozen_v, single_v, gtri_v, tail_v, old_v, scale_v, w_in_v, w_pairin_v, w_tri_v, vecs_v,
    row_in_v, col_in_v, row_pairin_v, col_pairin_v, row_tri_v, col_tri_v, sq_vecs_v,
    loss_o, count_o, g_in_o, row_in_o, col_in_o, new_in_o, g_pairin_o, row_pairin_o, col_pairin_o,
    new_pairin_o, g_tri_o, row_tri_o, col_tri_o, new_tri_o, g_vecs_o, sq_vecs_o, new_vecs_o,
    loss_s, count_s, g_in, row_in_n, col_in_n, new_in, g_pairin, row_pairin_n, col_pairin_n,
    new_pairin, g_tri, row_tri_n, col_tri_n, new_tri, g_vecs, sq_vecs_n, new_vecs,
    ds_v, sq_in, sq_rest, sum_in, sum_rest, store_sem,
):
    chans = vecs_v.shape[1]
    width, node = w_in_v.shape
    n_mat = w_tri_v.shape[0]
    stores = []

    def store(src, dst):
        copy = pltpu.make_async_copy(src, dst, store_sem.at[len(stores)])
        stores.append(copy)
        copy.start()

    totals = tail_v[0, ROWS : ROWS + 8, 0:chans] + tail_v[1, ROWS : ROWS + 8, 0:chans]
    inv = 1.0 / totals[5:6, :]
    inv2 = jnp.concatenate([inv, inv], 1)
    d_side = [tail_v[i, 0:ROWS, :] * inv2 for i in range(2)]

    pads = jnp.zeros((WIDE - ROWS, node), f32)
    side_parts = []
    for i in range(2):
        parts = split(d_side[i], 2)
        side_parts.append(parts)
        st = jnp.concatenate([p.astype(f32) for p in parts], 0).astype(bf16)
        ds = dot_nt(st[:, 0:chans], w_pairin_v[0].astype(bf16)) + dot_nt(
            st[:, chans : 2 * chans], w_pairin_v[1].astype(bf16)
        )
        ds = ds[0:ROWS] + ds[ROWS : 2 * ROWS]
        for k, p in enumerate(split(ds, 2)):
            at = (2 * k + i) * WIDE
            ds_v[at : at + WIDE, :] = jnp.concatenate([p.astype(f32), pads], 0).astype(bf16)
    fz = jnp.concatenate([frozen_v[0], frozen_v[1], frozen_v[0], frozen_v[1]], 0)
    g_in[...] = dot_tn(fz, ds_v[...])
    store(g_in, g_in_o)

    sg = jnp.concatenate([single_v[0], single_v[1], single_v[0], single_v[1]], 0).astype(bf16)
    st = jnp.concatenate(
        [side_parts[i][k].astype(f32) for k in range(2) for i in range(2)], 0
    ).astype(bf16)
    for k in range(2):
        g_pairin[k] = dot_tn(sg, st[:, k * chans : (k + 1) * chans])
    store(g_pairin, g_pairin_o)
    for m in range(n_mat):
        g_tri[m] = (gtri_v[0, m] + gtri_v[1, m]) * inv
    store(g_tri, g_tri_o)
    loss_s[...] = totals[4:5, :]
    count_s[...] = totals[5:6, :]
    g_vecs[...] = totals[0:4, :] * inv
    store(loss_s, loss_o)
    store(count_s, count_o)
    store(g_vecs, g_vecs_o)

    blk = chans
    n_in = width // blk
    n_pr = w_pairin_v.shape[1] // blk
    at_tri = 2 * n_pr
    for b in range(n_in):
        g = g_in[b * blk : (b + 1) * blk, :]
        sq_in[b * blk : (b + 1) * blk, :] = (g * g).astype(bf16)
    for k in range(2):
        for b in range(n_pr):
            g = g_pairin[k, b * blk : (b + 1) * blk, :]
            j = k * n_pr + b
            sq_rest[j * blk : (j + 1) * blk, :] = (g * g).astype(bf16)
    for m in range(n_mat):
        g = g_tri[m]
        j = at_tri + m
        sq_rest[j * blk : (j + 1) * blk, :] = (g * g).astype(bf16)
    sum_in[...] = dot(sq_in[...], jnp.ones((node, chans), bf16))
    sum_rest[...] = dot(sq_rest[...], jnp.ones((chans, chans), bf16))
    lane_in = dot_nt(jnp.ones((16, node), bf16), sq_in[...])[0:1]
    lane_rest = dot_nt(jnp.ones((16, chans), bf16), sq_rest[...])[0:1]

    def fresh(old, total, n):
        return BETA * old + ((1.0 - BETA) / n * total + (1.0 - BETA) * 1e-30)

    for b in range(n_in):
        row_in_n[b : b + 1, :] = fresh(
            row_in_v[b : b + 1, :], lane_in[:, b * blk : (b + 1) * blk], node
        )
    for k in range(2):
        s = slice(k * n_pr * blk, (k + 1) * n_pr * blk)
        row_pairin_n[k : k + 1, :] = fresh(row_pairin_v[k : k + 1, :], lane_rest[:, s], chans)
    for m in range(n_mat):
        s = slice((at_tri + m) * blk, (at_tri + m + 1) * blk)
        row_tri_n[m : m + 1, :] = fresh(row_tri_v[m : m + 1, :], lane_rest[:, s], chans)
    store(row_in_n, row_in_o)
    store(row_pairin_n, row_pairin_o)
    store(row_tri_n, row_tri_o)

    def fold(x):
        return jnp.sum(x.reshape(blk // 8, 8, x.shape[1]), 0)

    def adafactor(grad, weight, new, col_old, col_new, sums, old_at, n_blk, which, n_cols):
        n_rows = n_blk * blk
        halves = n_cols // chans
        col_sum = [jnp.zeros((8, chans), f32)] * halves
        scaled = [jnp.zeros((8, chans), f32)] * halves
        row_sum = jnp.zeros((8, chans), f32)
        for b in range(n_blk):
            s = slice(b * blk, (b + 1) * blk)
            o = slice((old_at + b) * blk, (old_at + b + 1) * blk)
            t = sums[0][(sums[1] + b) * blk : (sums[1] + b + 1) * blk, :]
            row = old_v[o, :] + ((1.0 - BETA) / n_cols * t + (1.0 - BETA) * 1e-30)
            row_sum = row_sum + fold(row)
            root = lax.rsqrt(row)
            for h in range(halves):
                c = slice(h * chans, (h + 1) * chans)
                g = grad[s, c]
                step = g * root
                new[s, c] = step
                col_sum[h] = col_sum[h] + fold(g * g)
                scaled[h] = scaled[h] + fold(step * step)
        row_mean = jnp.sum(row_sum, 0, keepdims=True) / n_rows
        power = jnp.zeros((1, chans), f32)
        by_col = []
        for h in range(halves):
            col = fresh(col_old(h), jnp.sum(col_sum[h], 0, keepdims=True), n_rows)
            col_new(h, col)
            power = power + jnp.sum(scaled[h], 0, keepdims=True) / col
            by_col.append(lax.rsqrt(col))
        rms = jnp.sqrt(row_mean * jnp.sum(power, -1, keepdims=True) / (n_rows * n_cols))
        coef = scale_v[which : which + 1, :] * jnp.sqrt(row_mean) / jnp.maximum(1.0, rms)
        for b in range(n_blk):
            s = slice(b * blk, (b + 1) * blk)
            for h in range(halves):
                c = slice(h * chans, (h + 1) * chans)
                new[s, c] = weight[s, c] - new[s, c] * (by_col[h] * coef)

    def put(ref, k):
        def put_col(h, col):
            at = k if k is not None else h
            ref[at : at + 1, :] = col

        return put_col

    adafactor(
        g_in, w_in_v, new_in, lambda h: col_in_v[h : h + 1, :], put(col_in_n, None), (sum_in, 0), 0,
        n_in, 0, node,
    )
    store(new_in, new_in_o)
    store(col_in_n, col_in_o)
    for k in range(2):
        adafactor(
            g_pairin.at[k], w_pairin_v.at[k], new_pairin.at[k],
            lambda h, k=k: col_pairin_v[k : k + 1, :], put(col_pairin_n, k),
            (sum_rest, k * n_pr), n_in + k * n_pr, n_pr, 1 + k, chans,
        )
    store(new_pairin, new_pairin_o)
    store(col_pairin_n, col_pairin_o)
    for m in range(n_mat):
        adafactor(
            g_tri.at[m], w_tri_v.at[m], new_tri.at[m],
            lambda h, m=m: col_tri_v[m : m + 1, :], put(col_tri_n, m),
            (sum_rest, at_tri + m), n_in + at_tri + m, 1, 3 + m, chans,
        )
    store(new_tri, new_tri_o)
    store(col_tri_n, col_tri_o)

    g = g_vecs[...]
    sq = BETA * sq_vecs_v[...] + (1.0 - BETA) * (g * g + 1e-30)
    sq_vecs_n[...] = sq
    step = g * lax.rsqrt(sq)
    step = step / jnp.maximum(1.0, jnp.sqrt(mean_last(step * step)))
    v = vecs_v[...]
    scale = jnp.maximum(0.001, jnp.sqrt(mean_last(v * v)))
    new_vecs[...] = v - RATE * scale * step
    store(sq_vecs_n, sq_vecs_o)
    store(new_vecs, new_vecs_o)
    for c in stores:
        c.wait()


def shards(
    tokens, lengths, recycle, resolved, coords, plm_embed, plm_uv, plm_qk, plm_affine, plm_out,
    w_in, w_pairin, w_tri, vecs, row_in, col_in, row_pairin, col_pairin, row_tri, col_tri, sq_vecs,
):
    heads = lax.axis_size("head")
    seq = tokens.shape[1]
    width = plm_embed.shape[1]
    units = plm_uv.shape[2]
    chans = vecs.shape[1]
    node = w_in.shape[1]
    unit_chunk = 256 if units % 256 == 0 else 128
    depth_chunk = units // 2 if units % 256 == 0 else units
    n_unit, n_depth = units // unit_chunk, units // depth_chunk
    anywhere = pl.BlockSpec(memory_space=pl.ANY)
    inside = pl.BlockSpec(memory_space=pltpu.VMEM)
    table = ROWS * ROWS

    def vm(*shape, dtype=f32):
        return pltpu.VMEM(shape, dtype)

    def like(x):
        return pltpu.VMEM(x.shape, x.dtype)

    coords = jnp.transpose(coords, (1, 0, 2))
    row_in2 = row_in.reshape(-1, chans)
    col_in2 = col_in.reshape(-1, chans)
    operands = (
        tokens, lengths, recycle, resolved, coords, plm_embed, plm_uv, plm_qk, plm_affine, plm_out,
        w_in, w_pairin, w_tri, vecs, row_in2, row_pairin, row_tri,
    )
    scratch = [
        like(tokens), like(resolved),
        like(coords), like(plm_embed), like(plm_uv), like(plm_qk), like(plm_affine), like(plm_out),
        like(w_in), like(w_pairin), like(w_tri), like(vecs), like(row_in2), like(row_pairin),
        like(row_tri), vm(WIDE, width), vm(WIDE, units, dtype=bf16),
        vm(heads, 16, width + width // 2, dtype=bf16), vm(width, node, dtype=bf16),
        vm(chans, 6 * chans, dtype=bf16), vm(WIDE, chans), vm(seq, seq), vm(chans, seq),
        vm(table, chans), vm(table, chans), vm(table, chans), vm(table, chans),
        vm(table, chans, dtype=bf16), vm(table, 5 * chans), vm(table, chans), vm(table, chans),
        vm(table, chans), vm(table, chans), vm(table, chans), vm(table, chans), vm(table, chans),
        vm(table, chans), vm(table, chans, dtype=bf16),
        vm(table, chans), vm(table, chans), vm(table, chans, dtype=bf16), vm(table, chans),
        vm(table, chans), vm(table, chans), vm(table, 5 * chans, dtype=bf16),
        vm(3 * WIDE, chans, dtype=bf16), vm(chans, chans),
        pltpu.SemaphoreType.DMA((13 + 2 * n_unit + n_depth,)),
        pltpu.SemaphoreType.DMA((heads - 1,)), pltpu.SemaphoreType.DMA((heads,)),
        pltpu.SemaphoreType.DMA((9,)), pltpu.SemaphoreType.DMA((9,)),
    ]
    operands = tuple(
        x if x.size == 1 else pltpu.with_memory_space_constraint(x, pltpu.HBM) for x in operands
    )
    sds = jax.ShapeDtypeStruct
    n_blk = width // chans + 2 * (node // chans) + 6
    made = pl.pallas_call(
        functools.partial(tables_kernel, heads=heads, unit_chunk=unit_chunk, depth_chunk=depth_chunk),
        out_shape=(
            sds((2, WIDE, width), bf16), sds((2, ROWS, node), f32), sds((2, 6, chans, chans), f32),
            sds((2, WIDE, 2 * chans), f32), sds((n_blk * chans, chans), f32), sds((16, chans), f32),
        ),
        in_specs=[
            pl.BlockSpec(memory_space=pltpu.SMEM) if x.size == 1 else anywhere for x in operands
        ],
        out_specs=[inside] * 6,
        scratch_shapes=scratch,
        compiler_params=pltpu.CompilerParams(
            collective_id=0, has_side_effects=True, vmem_limit_bytes=48 << 20
        ),
        name="tables",
    )(*operands)

    operands = tuple(made) + (
        w_in, w_pairin, w_tri, vecs, row_in2, col_in2, row_pairin,
        col_pairin, row_tri, col_tri, sq_vecs,
    )
    outs = (
        sds((1, chans), f32), sds((1, chans), f32), w_in, row_in2, col_in2, w_in, w_pairin,
        row_pairin, col_pairin, w_pairin, w_tri, row_tri, col_tri, w_tri, vecs, vecs, vecs,
    )
    outs = tuple(sds(x.shape, x.dtype) for x in outs)
    scratch = (
        [like(x) for x in outs]
        + [
            vm(4 * WIDE, node, dtype=bf16), vm(width, node, dtype=bf16),
            vm((n_blk - width // chans) * chans, chans, dtype=bf16), vm(width, chans),
            vm((n_blk - width // chans) * chans, chans),
            pltpu.SemaphoreType.DMA((17,)),
        ]
    )
    res = list(
        pl.pallas_call(
            update_kernel,
            out_shape=outs,
            in_specs=[inside] * len(operands),
            out_specs=[anywhere] * len(outs),
            scratch_shapes=scratch,
            compiler_params=pltpu.CompilerParams(vmem_limit_bytes=32 << 20),
            name="update",
        )(*operands)
    )
    res[0] = res[0][0, 0]
    res[1] = res[1][0, 0]
    res[3] = res[3].reshape(-1)
    res[4] = res[4].reshape(-1)
    return tuple(res)


def solution(mesh):
    whole = P()
    in_specs = (
        P("grp", None), P("grp"), P("grp"), P("grp", None), P("grp", None, None), whole,
        P(None, None, "head"), whole, whole, P("head", None),
    ) + (whole,) * 11
    return jax.shard_map(
        shards, mesh=mesh, in_specs=in_specs, out_specs=(whole,) * 17, check_vma=False
    )
```

```python
import functools
import math

import jax
import jax.numpy as jnp
from jax import lax
from jax.experimental import pallas as pl
from jax.experimental.pallas import tpu as pltpu
from jax.sharding import PartitionSpec as P


STEP = 10
BETA = 1.0 - STEP ** (-0.8)
RATE = 0.3
MESH = pl.DeviceIdType.MESH
f32 = jnp.float32
bf16 = jnp.bfloat16
ROWS = 24
WIDE = 32


def dot(a, b):
    return jnp.dot(a, b, preferred_element_type=f32)


def dot_nt(a, b):
    return lax.dot_general(a, b, (((1,), (1,)), ((), ())), preferred_element_type=f32)


def dot_tn(a, b):
    return lax.dot_general(a, b, (((0,), (0,)), ((), ())), preferred_element_type=f32)


def silu(x):
    return x * jax.nn.sigmoid(x)


def mean_last(x):
    return jnp.mean(x, -1, keepdims=True)


def split(x, parts):
    out = []
    for _ in range(parts):
        part = x.astype(bf16)
        out.append(part)
        x = x - part.astype(f32)
    return out


def iota(shape, dim):
    return lax.broadcasted_iota(jnp.int32, shape, dim)


def tables_kernel(
    tokens_h, lengths_s, recycle_s, resolved_h, coords_h, embed_h, uv_h, qk_h, affine_h, out_h,
    w_in_h, w_pairin_h, w_tri_h, vecs_h, row_in_h, col_in_h, row_pairin_h, col_pairin_h, row_tri_h,
    col_tri_h, sq_vecs_h,
    frozen_o, single_o, gtri_o, tail_o, old_o, scale_o,
    w_in_v, w_pairin_v, w_tri_v, vecs_v, row_in_v, col_in_v, row_pairin_v, col_pairin_v, row_tri_v,
    col_tri_v, sq_vecs_v,
    tokens_v, resolved_v, coords_v, embed_v, uv_v, qk_v, affine_v, out_v,
    emb, gate_x, value_x, part, w_in_b, w_tri_b, cnt_b, true_d, cols,
    pair, sb, n1, s1, pnorm, proj, sig_l, sig_r, gate, left, right, upd, n2, s2, unorm,
    branch, final, dbranch, dwork, dleft, dright, dproj, stack_d, old_v,
    load_sem, part_send, part_recv, unit_send, unit_recv, peer_send, peer_recv,
    *, heads, shared_by, unit_part,
):
    grp = lax.axis_index("grp")
    head = lax.axis_index("head")
    other = 1 - grp
    seq = tokens_v.shape[1]
    width = emb.shape[1]
    chans = vecs_v.shape[1]
    vocab = embed_v.shape[0]
    half = width // 2

    loads = []

    def load(src, dst):
        copy = pltpu.make_async_copy(src, dst, load_sem.at[len(loads)])
        loads.append(copy)
        copy.start()
        return copy

    c_small = [
        load(embed_h, embed_v),
        load(tokens_h, tokens_v),
        load(affine_h, affine_v),
    ]
    mine = grp if shared_by == 2 else 0
    at_mine = pl.multiple_of(mine * unit_part, 128)
    c_value = load(uv_h.at[1, :, pl.ds(at_mine, unit_part)], uv_v.at[1])
    c_qk = load(qk_h, qk_v)
    c_gate = load(uv_h.at[0, :, pl.ds(at_mine, unit_part)], uv_v.at[0])
    c_out = []
    for k in range(shared_by):
        at = pl.multiple_of(lax.rem(mine + k, shared_by) * unit_part, 128)
        c_out.append(load(out_h.at[pl.ds(at, unit_part)], out_v.at[k]))
    c_pairs = [load(resolved_h, resolved_v), load(coords_h, coords_v)]
    c_par = [
        load(w_in_h, w_in_v),
        load(w_pairin_h, w_pairin_v),
        load(w_tri_h, w_tri_v),
        load(vecs_h, vecs_v),
        load(row_in_h, row_in_v),
        load(row_pairin_h, row_pairin_v),
        load(row_tri_h, row_tri_v),
        load(col_in_h, col_in_v),
        load(col_pairin_h, col_pairin_v),
        load(col_tri_h, col_tri_v),
        load(sq_vecs_h, sq_vecs_v),
    ]

    barrier = pltpu.get_barrier_semaphore()
    pl.semaphore_signal(barrier, inc=1, device_id={"grp": other}, device_id_type=MESH)
    for d in range(1, heads):
        peer = lax.rem(head + d, heads)
        pl.semaphore_signal(barrier, inc=1, device_id={"head": peer}, device_id_type=MESH)

    for c in c_small:
        c.wait()
    emb[...] = jnp.zeros_like(emb)
    emb[0:vocab, :] = embed_v[...].astype(f32)
    e = emb[...]
    centre = e - mean_last(e)
    normed = (centre * lax.rsqrt(mean_last(centre * centre) + 1e-05)).astype(bf16)

    length = lengths_s[0]
    recycle = recycle_s[0].astype(f32)
    tok = tokens_v[...]
    onehot = (iota((WIDE, seq), 0) == tok).astype(f32)
    key_ok = (iota((1, seq), 1) < length).astype(f32)
    one_b = onehot.astype(bf16)
    cnt_col = jnp.sum(onehot, -1, keepdims=True)
    cnt_b[...] = jnp.broadcast_to(cnt_col, (WIDE, chans))
    ones = jnp.ones((16, seq), bf16)
    cnt_row = dot_nt(ones, one_b)[0:1, :]
    key_row = dot_nt(ones, (onehot * key_ok).astype(bf16))[0:1, :]

    pl.semaphore_wait(barrier, heads)
    unit_sends = []

    def swap(ref, k):
        copy = pltpu.make_async_remote_copy(
            src_ref=ref.at[0],
            dst_ref=ref.at[1],
            send_sem=unit_send.at[k],
            recv_sem=unit_recv.at[k],
            device_id={"grp": other},
            device_id_type=MESH,
        )
        copy.start()
        unit_sends.append(copy)

    c_value.wait()
    value_x[0] = silu(dot(normed, uv_v[1])).astype(bf16)
    if shared_by == 2:
        swap(value_x, 0)
    c_qk.wait()
    shared = silu(dot(normed, qk_v[...]))
    query = (shared * affine_v[0:1, :] + affine_v[1:2, :]).astype(bf16)
    keyed = (shared * affine_v[2:3, :] + affine_v[3:4, :]).astype(bf16)
    scores = dot_nt(query, keyed) / math.sqrt(qk_v.shape[1])
    masked = jnp.where(key_row > 0, scores, -1000000000.0)
    top = jnp.exp(masked - jnp.max(masked, -1, keepdims=True))
    attn = (top / jnp.sum(top * key_row, -1, keepdims=True)).astype(bf16).astype(f32)
    attn = jnp.concatenate(split(attn * key_row, 2), 0)

    c_gate.wait()
    ugate = silu(dot(normed, uv_v[0]))
    gate_x[0] = ugate[0:ROWS]
    if shared_by == 2:
        swap(gate_x, 1)

    p = None
    for k in range(shared_by):
        if k == 1:
            for c in unit_sends:
                c.wait_recv()
        seen = dot(attn, value_x[k])
        seen = seen[0:ROWS] + seen[WIDE : WIDE + ROWS]
        mixed = jnp.concatenate([gate_x[k] * seen, jnp.zeros((WIDE - ROWS, unit_part), f32)], 0)
        c_out[k].wait()
        q = dot(mixed.astype(bf16), out_v[k])
        p = q if p is None else p + q
    part[head, :, 0:width] = p[0:16].astype(bf16)
    part[head, :, width : width + half] = jnp.concatenate(
        [p[16:24, 0:half], p[16:24, half:width]], 0
    ).astype(bf16)
    sends = []
    for d in range(1, heads):
        copy = pltpu.make_async_remote_copy(
            src_ref=part.at[head],
            dst_ref=part.at[head],
            send_sem=part_send.at[d - 1],
            recv_sem=part_recv.at[head],
            device_id={"head": lax.rem(head + d, heads)},
            device_id_type=MESH,
        )
        copy.start()
        sends.append(copy)

    for c in c_pairs + c_par:
        c.wait()
    w_in_b[...] = w_in_v[...].astype(bf16)
    for m in range(6):
        w_tri_b[:, m * chans : (m + 1) * chans] = w_tri_v[m].astype(bf16)
    valid = key_ok * (resolved_v[...] > 0).astype(f32)
    cols[...] = jnp.zeros_like(cols)
    for k in range(3):
        cols[k : k + 1, :] = coords_v[k]
    cols[3:4, :] = valid
    one_v = (onehot * valid).astype(bf16)
    weight_j = recycle * valid
    blk = 128
    n_blk = seq // blk
    places = []
    for b in range(n_blk):
        t = cols[:, b * blk : (b + 1) * blk].T
        places.append(t)
        d2 = None
        for k in range(3):
            delta = t[:, k : k + 1] - cols[k : k + 1, :]
            d2 = delta * delta if d2 is None else d2 + delta * delta
        true_d[b * blk : (b + 1) * blk, :] = jnp.sqrt(d2)
    n_valid = jnp.sum(valid, -1, keepdims=True)
    loss_count = recycle * n_valid * n_valid

    present = cnt_b[0:ROWS, :] > 0
    sc = jnp.where((cnt_row > 0) & (cnt_col > 0), scores, 0.0)[0:ROWS]

    n_in = width // chans
    n_pr = w_pairin_v.shape[1] // chans
    at_tri = n_in + 2 * n_pr
    old_v[...] = jnp.zeros_like(old_v)
    old_v[0:n_in, :] = row_in_v[...]
    for k in range(2):
        for b in range(n_pr):
            j = n_in + k * n_pr + b
            old_v[j : j + 1, :] = row_pairin_v[k : k + 1, b * chans : (b + 1) * chans]
    old_v[at_tri : at_tri + 6, :] = row_tri_v[...]
    old = BETA * old_v[...].T
    for k in range(at_tri + 6):
        old_o[k * chans : (k + 1) * chans, :] = jnp.broadcast_to(old[:, k : k + 1], (chans, chans))
    scale_o[...] = jnp.zeros_like(scale_o)
    mats = [w_in_v] + [w_pairin_v.at[k] for k in range(2)] + [w_tri_v.at[m] for m in range(6)]
    for k, w in enumerate(mats):
        x = w[...]
        x = jnp.sum(jnp.sum(x * x, 0, keepdims=True), -1, keepdims=True) / (w.shape[0] * w.shape[1])
        x = RATE * jnp.maximum(0.001, jnp.sqrt(x))
        scale_o[k : k + 1, :] = jnp.broadcast_to(x, (1, chans))

    for d in range(1, heads):
        peer = lax.rem(head + d, heads)
        pltpu.make_async_remote_copy(
            src_ref=part.at[peer],
            dst_ref=part.at[peer],
            send_sem=part_send.at[d - 1],
            recv_sem=part_recv.at[peer],
            device_id={"head": peer},
            device_id_type=MESH,
        ).wait_recv()
    low = None
    for k in range(heads):
        a = part[k, :, 0:width].astype(f32)
        b = part[k, :, width : width + half].astype(f32)
        b = jnp.concatenate([b[0:8], b[8:16]], 1)
        low = [a, b] if low is None else [low[0] + a, low[1] + b]
    emb[0:16, :] += low[0]
    emb[16:24, :] += low[1]
    state = emb[0:ROWS, :]
    centre = state - mean_last(state)
    frozen = centre * lax.rsqrt(mean_last(centre * centre) + 1e-05)
    frozen = jnp.concatenate([frozen, jnp.zeros((WIDE - ROWS, width), f32)], 0).astype(bf16)
    frozen_o[grp] = frozen

    peers = []

    def give(ref):
        k = len(peers)
        copy = pltpu.make_async_remote_copy(
            src_ref=ref,
            dst_ref=ref,
            send_sem=peer_send.at[k],
            recv_sem=peer_recv.at[k],
            device_id={"grp": other},
            device_id_type=MESH,
        )
        copy.start()
        peers.append(copy)

    give(frozen_o.at[grp])
    single = dot(frozen, w_in_b[...]).astype(bf16)
    single_o[grp] = single[0:ROWS].astype(f32)
    give(single_o.at[grp])
    side_a = dot(single, w_pairin_v[0].astype(bf16))[0:ROWS]
    side_b = dot(single, w_pairin_v[1].astype(bf16))[0:ROWS]
    side_a = jnp.where(present, side_a, 0.0)
    side_b = jnp.where(present, side_b, 0.0)
    v0 = vecs_v[0:1, :]
    v1 = vecs_v[1:2, :]
    v2 = vecs_v[2:3, :]
    v3 = vecs_v[3:4, :]
    v0c = v0 - mean_last(v0)
    side_ac = side_a - mean_last(side_a)
    side_bc = side_b - mean_last(side_b)

    n_chunk = ROWS // 2
    two = 2 * ROWS

    def rows(k):
        return slice(k * two, (k + 1) * two)

    def both(f, k):
        return jnp.concatenate([f(2 * k), f(2 * k + 1)], 0)

    for k in range(n_chunk):
        r = rows(k)
        sbk = both(lambda u: jnp.broadcast_to(sc[:, u : u + 1], (ROWS, chans)), k)
        sb[r] = sbk
        pair[r] = sbk * v0 + both(lambda u: side_a + side_b[u : u + 1, :], k)
        centre = sbk * v0c + both(lambda u: side_ac + side_bc[u : u + 1, :], k)
        scale = lax.rsqrt(mean_last(centre * centre) + 1e-05)
        normal = centre * scale
        n1[r] = normal
        s1[r] = jnp.broadcast_to(scale, (two, chans))
        pnorm[r] = (normal * v1).astype(bf16)
    proj[...] = dot(pnorm[...], w_tri_b[:, 0 : 5 * chans])
    for k in range(n_chunk):
        r = rows(k)
        sl = jax.nn.sigmoid(proj[r, chans : 2 * chans])
        sr = jax.nn.sigmoid(proj[r, 3 * chans : 4 * chans])
        sig_l[r] = sl
        sig_r[r] = sr
        left[r] = (sl * proj[r, 0:chans]).astype(bf16).astype(f32)
        right[r] = (sr * proj[r, 2 * chans : 3 * chans]).astype(bf16).astype(f32)
        gate[r] = jax.nn.sigmoid(proj[r, 4 * chans : 5 * chans])
        dwork[r] = left[r] * both(
            lambda u: jnp.broadcast_to(cnt_b[u : u + 1, :], (ROWS, chans)), k
        )

    def triangle(dst, moving, fixed, row_of, weighted):
        group = 4
        for a0 in range(0, ROWS, group):
            total = [None] * group
            for b in range(vocab):
                x = moving(b)
                for q in range(group):
                    y = x * fixed[pl.ds(row_of(a0 + q, b), 1), :]
                    total[q] = y if total[q] is None else total[q] + y
            for q in range(group):
                a = a0 + q
                t = total[q]
                if weighted:
                    t = t * cnt_b[a : a + 1, :]
                dst[a * ROWS : (a + 1) * ROWS, :] = t

    triangle(
        upd, lambda u: dwork[u * ROWS : (u + 1) * ROWS, :], right, lambda v, u: u * ROWS + v, False
    )
    for k in range(n_chunk):
        r = rows(k)
        x = upd[r]
        centre = x - mean_last(x)
        scale = lax.rsqrt(mean_last(centre * centre) + 1e-05)
        normal = centre * scale
        n2[r] = normal
        s2[r] = jnp.broadcast_to(scale, (two, chans))
        unorm[r] = (normal * v2).astype(bf16)
    branch[...] = dot(unorm[...], w_tri_b[:, 5 * chans : 6 * chans])
    lane = iota((ROWS, chans), 1)
    logit = jnp.zeros((ROWS, chans), f32)
    for k in range(n_chunk):
        r = rows(k)
        fin = pair[r] + gate[r] * branch[r]
        final[r] = fin
        col = jnp.sum(fin * v3, -1, keepdims=True)
        for q in range(2):
            logit = jnp.where(lane == 2 * k + q, col[q * ROWS : (q + 1) * ROWS], logit)

    dist = jnp.maximum(logit, 0.0) + jnp.log1p(jnp.exp(-jnp.abs(logit)))
    dist = jnp.concatenate([dist, jnp.zeros((WIDE - ROWS, chans), f32)], 0)
    for k, d in enumerate(split(dist, 3)):
        stack_d[k * WIDE : (k + 1) * WIDE, :] = d
    by_col = dot(stack_d[:, 0:WIDE], one_b).astype(bf16)
    one3 = jnp.concatenate([one_b, one_b, one_b], 0)
    loss_row = jnp.zeros((1, seq), f32)
    by_first = jnp.zeros((WIDE, seq), f32)
    for b in range(n_blk):
        s = slice(b * blk, (b + 1) * blk)
        diff = dot_tn(one3[:, s], by_col) - true_d[s, :]
        sq = diff * diff + 1.0
        inv = lax.rsqrt(sq)
        loss_row = loss_row + jnp.sum(
            places[b][:, 3:4] * (sq * inv - 1.0), 0, keepdims=True
        )
        for q in split(diff * inv, 2):
            by_first = by_first + dot(one_v[:, s], q)
    loss = jnp.sum(loss_row * weight_j, -1, keepdims=True)
    by_pair = dot_nt(jnp.concatenate(split(by_first * weight_j, 2), 0), one_b)
    by_pair = (by_pair[0:WIDE] + by_pair[WIDE : 2 * WIDE])[0:ROWS]
    dlogit = by_pair * jax.nn.sigmoid(logit)[:, 0:WIDE]

    g_dist = jnp.zeros((two, chans), f32)
    for k in range(n_chunk):
        r = rows(k)
        g = both(lambda u: jnp.broadcast_to(dlogit[:, u : u + 1], (ROWS, chans)), k)
        g_dist = g_dist + g * final[r]
        dfinal = g * v3
        gt = gate[r]
        pair[r] = dfinal
        dbranch[r] = (dfinal * gt).astype(bf16)
        dproj[r, 4 * chans : 5 * chans] = (dfinal * branch[r] * gt * (1.0 - gt)).astype(bf16)
    dwork[...] = dot_nt(dbranch[...], w_tri_b[:, 5 * chans : 6 * chans])
    gtri_o[grp, 5] = dot_tn(unorm[...], dbranch[...])
    give(gtri_o.at[grp, 5])
    gtri_o[grp, 4] = dot_tn(pnorm[...], dproj[:, 4 * chans : 5 * chans])
    give(gtri_o.at[grp, 4])
    g_two = jnp.zeros((two, chans), f32)
    for k in range(n_chunk):
        r = rows(k)
        dn = dwork[r]
        normal = n2[r]
        g_two = g_two + dn * normal
        dn = dn * v2
        upd[r] = s2[r] * (dn - mean_last(dn) - normal * mean_last(dn * normal))
    triangle(
        dleft, lambda v: upd[v * ROWS : (v + 1) * ROWS, :], right, lambda u, v: u * ROWS + v, True
    )
    for k in range(n_chunk):
        r = rows(k)
        d, sl = dleft[r], sig_l[r]
        dproj[r, 0:chans] = (d * sl).astype(bf16)
        dproj[r, chans : 2 * chans] = (d * proj[r, 0:chans] * sl * (1.0 - sl)).astype(bf16)
    for m in range(2):
        gtri_o[grp, m] = dot_tn(pnorm[...], dproj[:, m * chans : (m + 1) * chans])
        give(gtri_o.at[grp, m])
    triangle(
        dright, lambda t: upd[pl.ds(t, ROWS, stride=ROWS), :], left, lambda u, t: u * ROWS + t, True
    )
    for k in range(n_chunk):
        r = rows(k)
        d, sr = dright[r], sig_r[r]
        dproj[r, 2 * chans : 3 * chans] = (d * sr).astype(bf16)
        dproj[r, 3 * chans : 4 * chans] = (
            d * proj[r, 2 * chans : 3 * chans] * sr * (1.0 - sr)
        ).astype(bf16)
    for m in range(2, 4):
        gtri_o[grp, m] = dot_tn(pnorm[...], dproj[:, m * chans : (m + 1) * chans])
        give(gtri_o.at[grp, m])
    dwork[...] = dot_nt(dproj[...], w_tri_b[:, 0 : 5 * chans])
    g_one = jnp.zeros((two, chans), f32)
    g_score = jnp.zeros((two, chans), f32)
    d_a = jnp.zeros((ROWS, chans), f32)
    tail_o[grp] = jnp.zeros((WIDE, 2 * chans), f32)
    for k in range(n_chunk):
        r = rows(k)
        dn = dwork[r]
        normal = n1[r]
        g_one = g_one + dn * normal
        dn = dn * v1
        dpair = pair[r] + s1[r] * (dn - mean_last(dn) - normal * mean_last(dn * normal))
        g_score = g_score + sb[r] * dpair
        d_a = d_a + dpair[0:ROWS] + dpair[ROWS:two]
        for q in range(2):
            tail_o[grp, 2 * k + q : 2 * k + q + 1, chans : 2 * chans] = jnp.sum(
                dpair[q * ROWS : (q + 1) * ROWS], 0, keepdims=True
            )
    tail_o[grp, 0:ROWS, 0:chans] = d_a
    for k, g in enumerate((g_score, g_one, g_two, g_dist)):
        tail_o[grp, ROWS + k : ROWS + k + 1, 0:chans] = jnp.sum(g, 0, keepdims=True)
    tail_o[grp, ROWS + 4 : ROWS + 5, 0:chans] = jnp.broadcast_to(loss, (1, chans))
    tail_o[grp, ROWS + 5 : ROWS + 6, 0:chans] = jnp.broadcast_to(loss_count, (1, chans))
    give(tail_o.at[grp])

    for c in sends + unit_sends:
        c.wait_send()
    for c in peers:
        c.wait()


def update_kernel(
    frozen_v, single_v, gtri_v, tail_v, old_v, scale_v, w_in_v, w_pairin_v, w_tri_v, vecs_v,
    row_in_v, col_in_v, row_pairin_v, col_pairin_v, row_tri_v, col_tri_v, sq_vecs_v,
    loss_o, count_o, g_in_o, row_in_o, col_in_o, new_in_o, g_pairin_o, row_pairin_o, col_pairin_o,
    new_pairin_o, g_tri_o, row_tri_o, col_tri_o, new_tri_o, g_vecs_o, sq_vecs_o, new_vecs_o,
    loss_s, count_s, g_in, row_in_n, col_in_n, new_in, g_pairin, row_pairin_n, col_pairin_n,
    new_pairin, g_tri, row_tri_n, col_tri_n, new_tri, g_vecs, sq_vecs_n, new_vecs,
    ds_v, sq_in, sq_rest, sum_in, sum_rest, store_sem,
):
    chans = vecs_v.shape[1]
    width, node = w_in_v.shape
    n_mat = w_tri_v.shape[0]
    stores = []

    def store(src, dst):
        copy = pltpu.make_async_copy(src, dst, store_sem.at[len(stores)])
        stores.append(copy)
        copy.start()

    totals = tail_v[0, ROWS : ROWS + 8, 0:chans] + tail_v[1, ROWS : ROWS + 8, 0:chans]
    inv = 1.0 / totals[5:6, :]
    inv2 = jnp.concatenate([inv, inv], 1)
    d_side = [tail_v[i, 0:ROWS, :] * inv2 for i in range(2)]

    pads = jnp.zeros((WIDE - ROWS, node), f32)
    side_parts = []
    for i in range(2):
        parts = split(d_side[i], 2)
        side_parts.append(parts)
        st = jnp.concatenate([p.astype(f32) for p in parts], 0).astype(bf16)
        ds = dot_nt(st[:, 0:chans], w_pairin_v[0].astype(bf16)) + dot_nt(
            st[:, chans : 2 * chans], w_pairin_v[1].astype(bf16)
        )
        ds = ds[0:ROWS] + ds[ROWS : 2 * ROWS]
        for k, p in enumerate(split(ds, 2)):
            at = (2 * k + i) * WIDE
            ds_v[at : at + WIDE, :] = jnp.concatenate([p.astype(f32), pads], 0).astype(bf16)
    fz = jnp.concatenate([frozen_v[0], frozen_v[1], frozen_v[0], frozen_v[1]], 0)
    g_in[...] = dot_tn(fz, ds_v[...])
    store(g_in, g_in_o)

    sg = jnp.concatenate([single_v[0], single_v[1], single_v[0], single_v[1]], 0).astype(bf16)
    st = jnp.concatenate(
        [side_parts[i][k].astype(f32) for k in range(2) for i in range(2)], 0
    ).astype(bf16)
    for k in range(2):
        g_pairin[k] = dot_tn(sg, st[:, k * chans : (k + 1) * chans])
    store(g_pairin, g_pairin_o)
    for m in range(n_mat):
        g_tri[m] = (gtri_v[0, m] + gtri_v[1, m]) * inv
    store(g_tri, g_tri_o)
    loss_s[...] = totals[4:5, :]
    count_s[...] = totals[5:6, :]
    g_vecs[...] = totals[0:4, :] * inv
    store(loss_s, loss_o)
    store(count_s, count_o)
    store(g_vecs, g_vecs_o)

    blk = chans
    n_in = width // blk
    n_pr = w_pairin_v.shape[1] // blk
    at_tri = 2 * n_pr
    for b in range(n_in):
        g = g_in[b * blk : (b + 1) * blk, :]
        sq_in[b * blk : (b + 1) * blk, :] = (g * g).astype(bf16)
    for k in range(2):
        for b in range(n_pr):
            g = g_pairin[k, b * blk : (b + 1) * blk, :]
            j = k * n_pr + b
            sq_rest[j * blk : (j + 1) * blk, :] = (g * g).astype(bf16)
    for m in range(n_mat):
        g = g_tri[m]
        j = at_tri + m
        sq_rest[j * blk : (j + 1) * blk, :] = (g * g).astype(bf16)
    sum_in[...] = dot(sq_in[...], jnp.ones((node, chans), bf16))
    sum_rest[...] = dot(sq_rest[...], jnp.ones((chans, chans), bf16))
    lane_in = dot_nt(jnp.ones((16, node), bf16), sq_in[...])[0:1]
    lane_rest = dot_nt(jnp.ones((16, chans), bf16), sq_rest[...])[0:1]

    def fresh(old, total, n):
        return BETA * old + ((1.0 - BETA) / n * total + (1.0 - BETA) * 1e-30)

    for b in range(n_in):
        row_in_n[b : b + 1, :] = fresh(
            row_in_v[b : b + 1, :], lane_in[:, b * blk : (b + 1) * blk], node
        )
    for k in range(2):
        s = slice(k * n_pr * blk, (k + 1) * n_pr * blk)
        row_pairin_n[k : k + 1, :] = fresh(row_pairin_v[k : k + 1, :], lane_rest[:, s], chans)
    for m in range(n_mat):
        s = slice((at_tri + m) * blk, (at_tri + m + 1) * blk)
        row_tri_n[m : m + 1, :] = fresh(row_tri_v[m : m + 1, :], lane_rest[:, s], chans)
    store(row_in_n, row_in_o)
    store(row_pairin_n, row_pairin_o)
    store(row_tri_n, row_tri_o)

    def fold(x):
        return jnp.sum(x.reshape(blk // 8, 8, x.shape[1]), 0)

    def adafactor(grad, weight, new, col_old, col_new, sums, old_at, n_blk, which, n_cols):
        n_rows = n_blk * blk
        halves = n_cols // chans
        col_sum = [jnp.zeros((8, chans), f32)] * halves
        scaled = [jnp.zeros((8, chans), f32)] * halves
        row_sum = jnp.zeros((8, chans), f32)
        for b in range(n_blk):
            s = slice(b * blk, (b + 1) * blk)
            o = slice((old_at + b) * blk, (old_at + b + 1) * blk)
            t = sums[0][(sums[1] + b) * blk : (sums[1] + b + 1) * blk, :]
            row = old_v[o, :] + ((1.0 - BETA) / n_cols * t + (1.0 - BETA) * 1e-30)
            row_sum = row_sum + fold(row)
            root = lax.rsqrt(row)
            for h in range(halves):
                c = slice(h * chans, (h + 1) * chans)
                g = grad[s, c]
                step = g * root
                new[s, c] = step
                col_sum[h] = col_sum[h] + fold(g * g)
                scaled[h] = scaled[h] + fold(step * step)
        row_mean = jnp.sum(row_sum, 0, keepdims=True) / n_rows
        power = jnp.zeros((1, chans), f32)
        by_col = []
        for h in range(halves):
            col = fresh(col_old(h), jnp.sum(col_sum[h], 0, keepdims=True), n_rows)
            col_new(h, col)
            power = power + jnp.sum(scaled[h], 0, keepdims=True) / col
            by_col.append(lax.rsqrt(col))
        rms = jnp.sqrt(row_mean * jnp.sum(power, -1, keepdims=True) / (n_rows * n_cols))
        coef = scale_v[which : which + 1, :] * jnp.sqrt(row_mean) / jnp.maximum(1.0, rms)
        for b in range(n_blk):
            s = slice(b * blk, (b + 1) * blk)
            for h in range(halves):
                c = slice(h * chans, (h + 1) * chans)
                new[s, c] = weight[s, c] - new[s, c] * (by_col[h] * coef)

    def put(ref, k):
        def put_col(h, col):
            at = k if k is not None else h
            ref[at : at + 1, :] = col

        return put_col

    adafactor(
        g_in, w_in_v, new_in, lambda h: col_in_v[h : h + 1, :], put(col_in_n, None), (sum_in, 0), 0,
        n_in, 0, node,
    )
    store(new_in, new_in_o)
    store(col_in_n, col_in_o)
    for k in range(2):
        adafactor(
            g_pairin.at[k], w_pairin_v.at[k], new_pairin.at[k],
            lambda h, k=k: col_pairin_v[k : k + 1, :], put(col_pairin_n, k),
            (sum_rest, k * n_pr), n_in + k * n_pr, n_pr, 1 + k, chans,
        )
    store(new_pairin, new_pairin_o)
    store(col_pairin_n, col_pairin_o)
    for m in range(n_mat):
        adafactor(
            g_tri.at[m], w_tri_v.at[m], new_tri.at[m],
            lambda h, m=m: col_tri_v[m : m + 1, :], put(col_tri_n, m),
            (sum_rest, at_tri + m), n_in + at_tri + m, 1, 3 + m, chans,
        )
    store(new_tri, new_tri_o)
    store(col_tri_n, col_tri_o)

    g = g_vecs[...]
    sq = BETA * sq_vecs_v[...] + (1.0 - BETA) * (g * g + 1e-30)
    sq_vecs_n[...] = sq
    step = g * lax.rsqrt(sq)
    step = step / jnp.maximum(1.0, jnp.sqrt(mean_last(step * step)))
    v = vecs_v[...]
    scale = jnp.maximum(0.001, jnp.sqrt(mean_last(v * v)))
    new_vecs[...] = v - RATE * scale * step
    store(sq_vecs_n, sq_vecs_o)
    store(new_vecs, new_vecs_o)
    for c in stores:
        c.wait()


def shards(
    tokens, lengths, recycle, resolved, coords, plm_embed, plm_uv, plm_qk, plm_affine, plm_out,
    w_in, w_pairin, w_tri, vecs, row_in, col_in, row_pairin, col_pairin, row_tri, col_tri, sq_vecs,
):
    heads = lax.axis_size("head")
    seq = tokens.shape[1]
    width = plm_embed.shape[1]
    units = plm_uv.shape[2]
    chans = vecs.shape[1]
    node = w_in.shape[1]
    shared_by = 2 if units % 256 == 0 else 1
    unit_part = units // shared_by
    anywhere = pl.BlockSpec(memory_space=pl.ANY)
    inside = pl.BlockSpec(memory_space=pltpu.VMEM)
    table = ROWS * ROWS

    def vm(*shape, dtype=f32):
        return pltpu.VMEM(shape, dtype)

    def like(x):
        return pltpu.VMEM(x.shape, x.dtype)

    coords = jnp.transpose(coords, (1, 0, 2))
    row_in2 = row_in.reshape(-1, chans)
    col_in2 = col_in.reshape(-1, chans)
    operands = (
        tokens, lengths, recycle, resolved, coords, plm_embed, plm_uv, plm_qk, plm_affine, plm_out,
        w_in, w_pairin, w_tri, vecs, row_in2, col_in2, row_pairin, col_pairin, row_tri, col_tri, sq_vecs,
    )
    kept = operands[10:]
    scratch = [
        like(tokens), like(resolved),
        like(coords), like(plm_embed), vm(2, width, unit_part, dtype=bf16), like(plm_qk),
        like(plm_affine), vm(shared_by, unit_part, width, dtype=bf16),
        vm(WIDE, width), vm(shared_by, ROWS, unit_part), vm(shared_by, WIDE, unit_part, dtype=bf16),
        vm(heads, 16, width + width // 2, dtype=bf16), vm(width, node, dtype=bf16),
        vm(chans, 6 * chans, dtype=bf16), vm(WIDE, chans), vm(seq, seq), vm(chans, seq),
        vm(table, chans), vm(table, chans), vm(table, chans), vm(table, chans),
        vm(table, chans, dtype=bf16), vm(table, 5 * chans), vm(table, chans), vm(table, chans),
        vm(table, chans), vm(table, chans), vm(table, chans), vm(table, chans), vm(table, chans),
        vm(table, chans), vm(table, chans, dtype=bf16),
        vm(table, chans), vm(table, chans), vm(table, chans, dtype=bf16), vm(table, chans),
        vm(table, chans), vm(table, chans), vm(table, 5 * chans, dtype=bf16),
        vm(3 * WIDE, chans, dtype=bf16), vm(chans, chans),
        pltpu.SemaphoreType.DMA((19 + shared_by,)),
        pltpu.SemaphoreType.DMA((heads - 1,)), pltpu.SemaphoreType.DMA((heads,)),
        pltpu.SemaphoreType.DMA((2,)), pltpu.SemaphoreType.DMA((2,)),
        pltpu.SemaphoreType.DMA((9,)), pltpu.SemaphoreType.DMA((9,)),
    ]
    operands = tuple(
        x if x.size == 1 else pltpu.with_memory_space_constraint(x, pltpu.HBM) for x in operands
    )
    sds = jax.ShapeDtypeStruct
    n_blk = width // chans + 2 * (node // chans) + 6
    made = pl.pallas_call(
        functools.partial(tables_kernel, heads=heads, shared_by=shared_by, unit_part=unit_part),
        out_shape=(
            sds((2, WIDE, width), bf16), sds((2, ROWS, node), f32), sds((2, 6, chans, chans), f32),
            sds((2, WIDE, 2 * chans), f32), sds((n_blk * chans, chans), f32), sds((16, chans), f32),
        )
        + tuple(sds(x.shape, x.dtype) for x in kept),
        in_specs=[
            pl.BlockSpec(memory_space=pltpu.SMEM) if x.size == 1 else anywhere for x in operands
        ],
        out_specs=[inside] * (6 + len(kept)),
        scratch_shapes=scratch,
        compiler_params=pltpu.CompilerParams(
            collective_id=0, has_side_effects=True, vmem_limit_bytes=48 << 20
        ),
        name="tables",
    )(*operands)

    operands = tuple(made)
    outs = (
        sds((1, chans), f32), sds((1, chans), f32), w_in, row_in2, col_in2, w_in, w_pairin,
        row_pairin, col_pairin, w_pairin, w_tri, row_tri, col_tri, w_tri, vecs, vecs, vecs,
    )
    outs = tuple(sds(x.shape, x.dtype) for x in outs)
    scratch = (
        [like(x) for x in outs]
        + [
            vm(4 * WIDE, node, dtype=bf16), vm(width, node, dtype=bf16),
            vm((n_blk - width // chans) * chans, chans, dtype=bf16), vm(width, chans),
            vm((n_blk - width // chans) * chans, chans),
            pltpu.SemaphoreType.DMA((17,)),
        ]
    )
    res = list(
        pl.pallas_call(
            update_kernel,
            out_shape=outs,
            in_specs=[inside] * len(operands),
            out_specs=[anywhere] * len(outs),
            scratch_shapes=scratch,
            compiler_params=pltpu.CompilerParams(vmem_limit_bytes=32 << 20),
            name="update",
        )(*operands)
    )
    res[0] = res[0][0, 0]
    res[1] = res[1][0, 0]
    res[3] = res[3].reshape(-1)
    res[4] = res[4].reshape(-1)
    return tuple(res)


def solution(mesh):
    whole = P()
    in_specs = (
        P("grp", None), P("grp"), P("grp"), P("grp", None), P("grp", None, None), whole,
        P(None, None, "head"), whole, whole, P("head", None),
    ) + (whole,) * 11
    return jax.shard_map(
        shards, mesh=mesh, in_specs=in_specs, out_specs=(whole,) * 17, check_vma=False
    )
```

```python
import functools
import math

import jax
import jax.numpy as jnp
from jax import lax
from jax.experimental import pallas as pl
from jax.experimental.pallas import tpu as pltpu
from jax.sharding import PartitionSpec as P


STEP = 10
ORDER = (0, 1, 4, 2, 3)
BETA = 1.0 - STEP ** (-0.8)
RATE = 0.3
MESH = pl.DeviceIdType.MESH
f32 = jnp.float32
bf16 = jnp.bfloat16
ROWS = 24
WIDE = 32


def dot(a, b):
    return jnp.dot(a, b, preferred_element_type=f32)


def dot_nt(a, b):
    return lax.dot_general(a, b, (((1,), (1,)), ((), ())), preferred_element_type=f32)


def dot_tn(a, b):
    return lax.dot_general(a, b, (((0,), (0,)), ((), ())), preferred_element_type=f32)


def silu(x):
    return x * jax.nn.sigmoid(x)


def mean_last(x):
    return jnp.mean(x, -1, keepdims=True)


def split(x, parts):
    out = []
    for _ in range(parts):
        part = x.astype(bf16)
        out.append(part)
        x = x - part.astype(f32)
    return out


def iota(shape, dim):
    return lax.broadcasted_iota(jnp.int32, shape, dim)


def tables_kernel(
    tokens_h, lengths_s, recycle_s, resolved_h, coords_h, embed_h, uv_h, qk_h, affine_h, out_h,
    w_in_h, w_pairin_h, w_tri_h, vecs_h, row_in_h, col_in_h, row_pairin_h, col_pairin_h, row_tri_h,
    col_tri_h, sq_vecs_h,
    frozen_o, single_o, gtri_o, tail_o, old_o, scale_o,
    w_in_v, w_pairin_v, w_tri_v, vecs_v, row_in_v, col_in_v, row_pairin_v, col_pairin_v, row_tri_v,
    col_tri_v, sq_vecs_v,
    tokens_v, resolved_v, coords_v, embed_v, uv_v, qk_v, affine_v, out_v,
    emb, gate_x, value_x, partial_v, part, w_in_b, w_pair_b, w_tri_b, cnt_b, true_d, cols,
    pair, sb, n1, s1, pnorm, proj, sig_l, sig_r, gate, left, right, upd, n2, s2, unorm,
    branch, final, dbranch, left_n, gated_b, dunorm, dpnorm, dlast, dleft, dright, dproj, stack_d,
    old_v, one_t,
    load_sem, part_send, part_recv, unit_send, unit_recv, peer_send, peer_recv,
    *, heads, shared_by, unit_part,
):
    grp = lax.axis_index("grp")
    head = lax.axis_index("head")
    other = 1 - grp
    seq = tokens_v.shape[1]
    width = emb.shape[1]
    chans = vecs_v.shape[1]
    vocab = embed_v.shape[0]
    half = width // 2
    quarter = width // 4

    loads = []

    def load(src, dst):
        copy = pltpu.make_async_copy(src, dst, load_sem.at[len(loads)])
        loads.append(copy)
        copy.start()
        return copy

    c_small = [
        load(embed_h, embed_v),
        load(tokens_h, tokens_v),
        load(affine_h, affine_v),
    ]
    mine = grp if shared_by == 2 else 0
    at_mine = pl.multiple_of(mine * unit_part, 128)
    c_qk = load(qk_h, qk_v)
    c_gate = load(uv_h.at[0, :, pl.ds(at_mine, unit_part)], uv_v.at[0])
    c_value = load(uv_h.at[1, :, pl.ds(at_mine, unit_part)], uv_v.at[1])
    c_out = []
    for k in range(shared_by):
        at = pl.multiple_of(lax.rem(mine + k, shared_by) * unit_part, 128)
        c_out.append(load(out_h.at[pl.ds(at, unit_part)], out_v.at[k]))
    c_pairs = [load(resolved_h, resolved_v), load(coords_h, coords_v)]
    c_par = [
        load(w_in_h, w_in_v),
        load(w_pairin_h, w_pairin_v),
        load(w_tri_h, w_tri_v),
        load(vecs_h, vecs_v),
        load(row_in_h, row_in_v),
        load(row_pairin_h, row_pairin_v),
        load(row_tri_h, row_tri_v),
        load(col_in_h, col_in_v),
        load(col_pairin_h, col_pairin_v),
        load(col_tri_h, col_tri_v),
        load(sq_vecs_h, sq_vecs_v),
    ]

    barrier = pltpu.get_barrier_semaphore()
    pl.semaphore_signal(barrier, inc=1, device_id={"grp": other}, device_id_type=MESH)
    for d in range(1, heads):
        peer = lax.rem(head + d, heads)
        pl.semaphore_signal(barrier, inc=1, device_id={"head": peer}, device_id_type=MESH)

    for c in c_small:
        c.wait()
    emb[...] = jnp.zeros_like(emb)
    emb[0:vocab, :] = embed_v[...].astype(f32)
    e = emb[...]
    centre = e - mean_last(e)
    normed = (centre * lax.rsqrt(mean_last(centre * centre) + 1e-05)).astype(bf16)

    length = lengths_s[0]
    recycle = recycle_s[0].astype(f32)
    tok = tokens_v[...]
    onehot = (iota((WIDE, seq), 0) == tok).astype(f32)
    key_ok = (iota((1, seq), 1) < length).astype(f32)
    one_b = onehot.astype(bf16)
    cnt_col = jnp.sum(onehot, -1, keepdims=True)
    cnt_b[...] = jnp.broadcast_to(cnt_col, (WIDE, chans))
    ones = jnp.ones((16, seq), bf16)
    cnt_row = dot_nt(ones, one_b)[0:1, :]
    key_row = dot_nt(ones, (onehot * key_ok).astype(bf16))[0:1, :]

    pl.semaphore_wait(barrier, heads)
    unit_sends = []

    def swap(ref, k):
        copy = pltpu.make_async_remote_copy(
            src_ref=ref.at[0],
            dst_ref=ref.at[1],
            send_sem=unit_send.at[k],
            recv_sem=unit_recv.at[k],
            device_id={"grp": other},
            device_id_type=MESH,
        )
        copy.start()
        unit_sends.append(copy)

    c_qk.wait()
    shared = silu(dot(normed, qk_v[...]))
    query = (shared * affine_v[0:1, :] + affine_v[1:2, :]).astype(bf16)
    keyed = (shared * affine_v[2:3, :] + affine_v[3:4, :]).astype(bf16)
    scores = dot_nt(query, keyed) / math.sqrt(qk_v.shape[1])
    masked = jnp.where(key_row > 0, scores, -1000000000.0)
    top = jnp.exp(masked - jnp.max(masked, -1, keepdims=True))
    attn = (top / jnp.sum(top * key_row, -1, keepdims=True)).astype(bf16).astype(f32)
    attn = jnp.concatenate(split(attn * key_row, 2), 0)

    c_gate.wait()
    ugate = silu(dot(normed, uv_v[0]))
    gate_x[0] = ugate[0:ROWS]
    if shared_by == 2:
        swap(gate_x, 0)
    c_value.wait()
    value_x[0] = silu(dot(normed, uv_v[1])).astype(bf16)
    if shared_by == 2:
        swap(value_x, 1)

    def mix(k):
        seen = dot(attn, value_x[k])
        seen = seen[0:ROWS] + seen[WIDE : WIDE + ROWS]
        return (gate_x[k] * seen).astype(bf16)

    mixed = mix(0)
    c_out[0].wait()
    if shared_by == 2:
        partial_v[...] = dot(mixed, out_v[0])
        for c in unit_sends:
            c.wait_recv()
        mixed = mix(1)
        c_out[1].wait()
    sends = []
    for n in range(2):
        s = slice(n * half, (n + 1) * half)
        p = dot(mixed, out_v[shared_by - 1, :, s])
        if shared_by == 2:
            p = p + partial_v[:, s]
        part[head, n, :, 0:half] = p[0:16].astype(bf16)
        part[head, n, :, half : half + quarter] = jnp.concatenate(
            [p[16:24, 0:quarter], p[16:24, quarter:half]], 0
        ).astype(bf16)
        for d in range(1, heads):
            copy = pltpu.make_async_remote_copy(
                src_ref=part.at[head, n],
                dst_ref=part.at[head, n],
                send_sem=part_send.at[d - 1, n],
                recv_sem=part_recv.at[head, n],
                device_id={"head": lax.rem(head + d, heads)},
                device_id_type=MESH,
            )
            copy.start()
            sends.append(copy)

    for c in c_pairs + c_par:
        c.wait()
    w_in_b[...] = w_in_v[...].astype(bf16)
    for k in range(2):
        w_pair_b[:, k * chans : (k + 1) * chans] = w_pairin_v[k].astype(bf16)
    v0 = vecs_v[0:1, :]
    v1 = vecs_v[1:2, :]
    v2 = vecs_v[2:3, :]
    v3 = vecs_v[3:4, :]
    gain_one = vecs_v[...].T[:, 1:2]
    gain_two = vecs_v[...].T[:, 2:3]
    for k, m in enumerate(ORDER + (5,)):
        c = slice(k * chans, (k + 1) * chans)
        w = w_tri_v[m].astype(bf16)
        w_tri_b[0:chans, c] = w
        w = w.astype(f32) * (gain_two if m == 5 else gain_one)
        w = jnp.sum(w, 0, keepdims=True) * (1.0 / chans)
        w_tri_b[chans : 2 * chans, c] = jnp.broadcast_to(w, (chans, chans)).astype(bf16)
    valid = key_ok * (resolved_v[...] > 0).astype(f32)
    cols[...] = jnp.zeros_like(cols)
    for k in range(3):
        cols[k : k + 1, :] = coords_v[k]
    cols[3:4, :] = valid
    cols[4:5, :] = tok.astype(f32)
    one_v = (onehot * valid).astype(bf16)
    weight_j = recycle * valid
    blk = 128
    n_blk = seq // blk
    places = []
    for b in range(n_blk):
        t = cols[:, b * blk : (b + 1) * blk].T
        hot = lax.bitwise_and(iota((blk, chans), 1), WIDE - 1) == t[:, 4:5].astype(jnp.int32)
        hot = hot & (iota((blk, chans), 1) < 3 * WIDE)
        one_t[b * blk : (b + 1) * blk, :] = hot.astype(f32).astype(bf16)
        places.append(t)
        d2 = None
        for k in range(3):
            delta = t[:, k : k + 1] - cols[k : k + 1, :]
            d2 = delta * delta if d2 is None else d2 + delta * delta
        true_d[b * blk : (b + 1) * blk, :] = jnp.sqrt(d2)
    n_valid = jnp.sum(valid, -1, keepdims=True)
    loss_count = recycle * n_valid * n_valid

    present = cnt_b[0:ROWS, :] > 0
    sc = jnp.where((cnt_row > 0) & (cnt_col > 0), scores, 0.0)[0:ROWS]

    n_chunk = ROWS // 2
    two = 2 * ROWS

    def rows(k):
        return slice(k * two, (k + 1) * two)

    def both(f, k):
        return jnp.concatenate([f(2 * k), f(2 * k + 1)], 0)

    v0c = v0 - mean_last(v0)
    for k in range(n_chunk):
        r = rows(k)
        sbk = both(lambda u: jnp.broadcast_to(sc[:, u : u + 1], (ROWS, chans)), k)
        sb[r] = sbk
        pair[r] = sbk * v0
        n1[r] = sbk * v0c
    lane = iota((ROWS, chans), 1)
    score_logit = jnp.sum(v0 * v3, -1, keepdims=True) * jnp.concatenate(
        [sc, jnp.zeros((ROWS, chans - WIDE), f32)], 1
    )

    n_in = width // chans
    n_pr = w_pairin_v.shape[1] // chans
    at_tri = n_in + 2 * n_pr
    old_v[...] = jnp.zeros_like(old_v)
    old_v[0:n_in, :] = row_in_v[...]
    for k in range(2):
        for b in range(n_pr):
            j = n_in + k * n_pr + b
            old_v[j : j + 1, :] = row_pairin_v[k : k + 1, b * chans : (b + 1) * chans]
    old_v[at_tri : at_tri + 6, :] = row_tri_v[...]
    old = BETA * old_v[...].T
    for k in range(at_tri + 6):
        old_o[k * chans : (k + 1) * chans, :] = jnp.broadcast_to(old[:, k : k + 1], (chans, chans))
    scale_o[...] = jnp.zeros_like(scale_o)
    mats = [w_in_v] + [w_pairin_v.at[k] for k in range(2)] + [w_tri_v.at[m] for m in range(6)]
    for k, w in enumerate(mats):
        x = w[...]
        x = jnp.sum(jnp.sum(x * x, 0, keepdims=True), -1, keepdims=True) / (w.shape[0] * w.shape[1])
        x = RATE * jnp.maximum(0.001, jnp.sqrt(x))
        scale_o[k : k + 1, :] = jnp.broadcast_to(x, (1, chans))

    for n in range(2):
        for d in range(1, heads):
            peer = lax.rem(head + d, heads)
            pltpu.make_async_remote_copy(
                src_ref=part.at[peer, n],
                dst_ref=part.at[peer, n],
                send_sem=part_send.at[d - 1, n],
                recv_sem=part_recv.at[peer, n],
                device_id={"head": peer},
                device_id_type=MESH,
            ).wait_recv()
    for n in range(2):
        s = slice(n * half, (n + 1) * half)
        low = None
        for k in range(heads):
            a = part[k, n, :, 0:half].astype(f32)
            b = part[k, n, :, half : half + quarter].astype(f32)
            b = jnp.concatenate([b[0:8], b[8:16]], 1)
            low = [a, b] if low is None else [low[0] + a, low[1] + b]
        emb[0:16, s] += low[0]
        emb[16:24, s] += low[1]
    state = emb[0:ROWS, :]
    centre = state - mean_last(state)
    frozen = centre * lax.rsqrt(mean_last(centre * centre) + 1e-05)
    frozen = jnp.concatenate([frozen, jnp.zeros((WIDE - ROWS, width), f32)], 0).astype(bf16)
    frozen_o[grp] = frozen

    peers = []

    def give(ref):
        k = len(peers)
        copy = pltpu.make_async_remote_copy(
            src_ref=ref,
            dst_ref=ref,
            send_sem=peer_send.at[k],
            recv_sem=peer_recv.at[k],
            device_id={"grp": other},
            device_id_type=MESH,
        )
        copy.start()
        peers.append(copy)

    give(frozen_o.at[grp])
    single = dot(frozen, w_in_b[...]).astype(bf16)
    single_o[grp] = single[0:ROWS].astype(f32)
    give(single_o.at[grp])
    side = dot(single, w_pair_b[...])[0:ROWS]
    side_a = jnp.where(present, side[:, 0:chans], 0.0)
    side_b = jnp.where(present, side[:, chans : 2 * chans], 0.0)
    side_ac = side_a - mean_last(side_a)
    side_bc = side_b - mean_last(side_b)

    own = iota((ROWS, chans), 0) == lane
    logit_b = jnp.sum(
        jnp.where(own, jnp.sum(side_b * v3, -1, keepdims=True), 0.0), 0, keepdims=True
    )
    logit = score_logit + jnp.sum(side_a * v3, -1, keepdims=True) + logit_b
    for k in range(n_chunk):
        r = rows(k)
        pair[r] = pair[r] + both(lambda u: side_a + side_b[u : u + 1, :], k)
        centre = n1[r] + both(lambda u: side_ac + side_bc[u : u + 1, :], k)
        scale = lax.rsqrt(mean_last(centre * centre) + 1e-05)
        normal = centre * scale
        n1[r] = normal
        s1[r] = jnp.broadcast_to(scale, (two, chans))
        pnorm[r] = (normal * v1).astype(bf16)
    proj[...] = dot(pnorm[...], w_tri_b[0:chans, 0 : 5 * chans])
    for k in range(n_chunk):
        r = rows(k)
        sl = jax.nn.sigmoid(proj[r, chans : 2 * chans])
        sr = jax.nn.sigmoid(proj[r, 4 * chans : 5 * chans])
        sig_l[r] = sl
        sig_r[r] = sr
        left[r] = (sl * proj[r, 0:chans]).astype(bf16).astype(f32)
        right[r] = (sr * proj[r, 3 * chans : 4 * chans]).astype(bf16).astype(f32)
        gate[r] = jax.nn.sigmoid(proj[r, 2 * chans : 3 * chans])
        left_n[r] = left[r] * both(
            lambda u: jnp.broadcast_to(cnt_b[u : u + 1, :], (ROWS, chans)), k
        )

    def triangle(dst, moving, fixed, row_of, weighted):
        group = 4
        for a0 in range(0, ROWS, group):
            total = [None] * group
            for b in range(vocab):
                x = moving(b)
                for q in range(group):
                    y = x * fixed[pl.ds(row_of(a0 + q, b), 1), :]
                    total[q] = y if total[q] is None else total[q] + y
            for q in range(group):
                a = a0 + q
                t = total[q]
                if weighted:
                    t = t * cnt_b[a : a + 1, :]
                dst[a * ROWS : (a + 1) * ROWS, :] = t

    triangle(
        upd, lambda u: left_n[u * ROWS : (u + 1) * ROWS, :], right, lambda v, u: u * ROWS + v, False
    )
    for k in range(n_chunk):
        r = rows(k)
        x = upd[r]
        centre = x - mean_last(x)
        scale = lax.rsqrt(mean_last(centre * centre) + 1e-05)
        normal = centre * scale
        n2[r] = normal
        s2[r] = jnp.broadcast_to(scale, (two, chans))
        unorm[r] = (normal * v2).astype(bf16)
    branch[...] = dot(unorm[...], w_tri_b[0:chans, 5 * chans : 6 * chans])
    gated = jnp.zeros((ROWS, chans), f32)
    for k in range(n_chunk):
        r = rows(k)
        move = gate[r] * branch[r]
        final[r] = pair[r] + move
        col = jnp.sum(move * v3, -1, keepdims=True)
        gated_b[r] = jnp.broadcast_to(col, (two, chans))
        for q in range(2):
            gated = jnp.where(lane == 2 * k + q, col[q * ROWS : (q + 1) * ROWS], gated)
    logit = logit + gated

    dist = jnp.maximum(logit, 0.0) + jnp.log1p(jnp.exp(-jnp.abs(logit)))
    dist = jnp.concatenate([dist, jnp.zeros((WIDE - ROWS, chans), f32)], 0)
    for k, d in enumerate(split(dist, 3)):
        stack_d[k * WIDE : (k + 1) * WIDE, :] = d
    by_col = dot(stack_d[:, 0:WIDE], one_b).astype(bf16)
    for k in range(n_chunk):
        r = rows(k)
        sl, sr, gt = sig_l[r], sig_r[r], gate[r]
        proj[r, 0:chans] = proj[r, 0:chans] * sl * (1.0 - sl)
        proj[r, 3 * chans : 4 * chans] = proj[r, 3 * chans : 4 * chans] * sr * (1.0 - sr)
        gt3 = gt * v3
        proj[r, 2 * chans : 3 * chans] = gt3 * (1.0 - gt) * branch[r]
        gate[r] = gt3
    loss_row = jnp.zeros((1, seq), f32)
    by_first = jnp.zeros((WIDE, seq), f32)
    for b in range(n_blk):
        s = slice(b * blk, (b + 1) * blk)
        diff = dot(one_t[s, 0 : 3 * WIDE], by_col) - true_d[s, :]
        sq = diff * diff + 1.0
        inv = lax.rsqrt(sq)
        loss_row = loss_row + jnp.sum(
            places[b][:, 3:4] * (sq * inv - 1.0), 0, keepdims=True
        )
        by_first = by_first + dot(one_v[:, s], (diff * inv).astype(bf16))
    loss = jnp.sum(loss_row * weight_j, -1, keepdims=True)
    by_pair = dot_nt(jnp.concatenate(split(by_first * weight_j, 2), 0), one_b)
    by_pair = (by_pair[0:WIDE] + by_pair[WIDE : 2 * WIDE])[0:ROWS]
    dlogit = by_pair * jax.nn.sigmoid(logit)[:, 0:WIDE]

    g_dist = jnp.zeros((two, chans), f32)
    for k in range(n_chunk):
        r = rows(k)
        g = both(lambda u: jnp.broadcast_to(dlogit[:, u : u + 1], (ROWS, chans)), k)
        g_dist = g_dist + g * final[r]
        dfinal = g * v3
        pair[r] = dfinal
        dbranch[r] = (g * gate[r]).astype(bf16)
        dproj[r, 2 * chans : 3 * chans] = (g * proj[r, 2 * chans : 3 * chans]).astype(bf16)
        gated_b[r] = g * gated_b[r] * (1.0 / chans)
    dunorm[...] = dot_nt(dbranch[...], w_tri_b[:, 5 * chans : 6 * chans])
    gtri_o[grp, 5] = dot_tn(unorm[...], dbranch[...])
    gtri_o[grp, 4] = dot_tn(pnorm[...], dproj[:, 2 * chans : 3 * chans])
    give(gtri_o.at[grp, pl.ds(4, 2)])
    g_two = jnp.zeros((two, chans), f32)
    for k in range(n_chunk):
        r = rows(k)
        dn = dunorm[r, 0:chans]
        normal = n2[r]
        g_two = g_two + dn * normal
        upd[r] = s2[r] * (dn * v2 - dunorm[r, chans : 2 * chans] - normal * gated_b[r])
    triangle(
        dleft, lambda v: upd[v * ROWS : (v + 1) * ROWS, :], right, lambda u, v: u * ROWS + v, True
    )
    for k in range(n_chunk):
        r = rows(k)
        d, sl = dleft[r], sig_l[r]
        dproj[r, 0:chans] = (d * sl).astype(bf16)
        dproj[r, chans : 2 * chans] = (d * proj[r, 0:chans]).astype(bf16)
    dpnorm[...] = dot_nt(dproj[:, 0 : 3 * chans], w_tri_b[:, 0 : 3 * chans])
    g = dot_tn(pnorm[...], dproj[:, 0 : 2 * chans])
    gtri_o[grp, 0] = g[:, 0:chans]
    gtri_o[grp, 1] = g[:, chans : 2 * chans]
    give(gtri_o.at[grp, pl.ds(0, 2)])
    triangle(
        dright, lambda t: upd[pl.ds(t, ROWS, stride=ROWS), :], left, lambda u, t: u * ROWS + t, True
    )
    for k in range(n_chunk):
        r = rows(k)
        d, sr = dright[r], sig_r[r]
        dproj[r, 3 * chans : 4 * chans] = (d * sr).astype(bf16)
        dproj[r, 4 * chans : 5 * chans] = (d * proj[r, 3 * chans : 4 * chans]).astype(bf16)
    dlast[...] = dot_nt(dproj[:, 3 * chans : 5 * chans], w_tri_b[:, 3 * chans : 5 * chans])
    g = dot_tn(pnorm[...], dproj[:, 3 * chans : 5 * chans])
    gtri_o[grp, 2] = g[:, 0:chans]
    gtri_o[grp, 3] = g[:, chans : 2 * chans]
    give(gtri_o.at[grp, pl.ds(2, 2)])
    g_one = jnp.zeros((two, chans), f32)
    g_score = jnp.zeros((two, chans), f32)
    d_a = jnp.zeros((ROWS, chans), f32)
    tail_o[grp] = jnp.zeros((WIDE, 2 * chans), f32)
    for k in range(n_chunk):
        r = rows(k)
        dn = dpnorm[r, 0:chans] + dlast[r, 0:chans]
        mean = dpnorm[r, chans : 2 * chans] + dlast[r, chans : 2 * chans]
        normal = n1[r]
        along = dn * normal
        g_one = g_one + along
        dpair = pair[r] + s1[r] * (dn * v1 - mean - normal * mean_last(along * v1))
        g_score = g_score + sb[r] * dpair
        d_a = d_a + dpair[0:ROWS] + dpair[ROWS:two]
        for q in range(2):
            tail_o[grp, 2 * k + q : 2 * k + q + 1, chans : 2 * chans] = jnp.sum(
                dpair[q * ROWS : (q + 1) * ROWS], 0, keepdims=True
            )
    tail_o[grp, 0:ROWS, 0:chans] = d_a
    for k, g in enumerate((g_score, g_one, g_two, g_dist)):
        tail_o[grp, ROWS + k : ROWS + k + 1, 0:chans] = jnp.sum(g, 0, keepdims=True)
    tail_o[grp, ROWS + 4 : ROWS + 5, 0:chans] = jnp.broadcast_to(loss, (1, chans))
    tail_o[grp, ROWS + 5 : ROWS + 6, 0:chans] = jnp.broadcast_to(loss_count, (1, chans))
    give(tail_o.at[grp])

    for c in sends + unit_sends:
        c.wait_send()
    for c in peers:
        c.wait()


def update_kernel(
    frozen_v, single_v, gtri_v, tail_v, old_v, scale_v, w_in_v, w_pairin_v, w_tri_v, vecs_v,
    row_in_v, col_in_v, row_pairin_v, col_pairin_v, row_tri_v, col_tri_v, sq_vecs_v,
    loss_o, count_o, g_in_o, row_in_o, col_in_o, new_in_o, g_pairin_o, row_pairin_o, col_pairin_o,
    new_pairin_o, g_tri_o, row_tri_o, col_tri_o, new_tri_o, g_vecs_o, sq_vecs_o, new_vecs_o,
    loss_s, count_s, g_in, row_in_n, col_in_n, new_in, g_pairin, row_pairin_n, col_pairin_n,
    new_pairin, g_tri, row_tri_n, col_tri_n, new_tri, g_vecs, sq_vecs_n, new_vecs,
    ds_v, sq_in, sq_rest, sum_in, sum_rest, store_sem,
):
    chans = vecs_v.shape[1]
    width, node = w_in_v.shape
    n_mat = w_tri_v.shape[0]
    stores = []

    def store(src, dst):
        copy = pltpu.make_async_copy(src, dst, store_sem.at[len(stores)])
        stores.append(copy)
        copy.start()

    totals = tail_v[0, ROWS : ROWS + 8, 0:chans] + tail_v[1, ROWS : ROWS + 8, 0:chans]
    inv = 1.0 / totals[5:6, :]
    inv2 = jnp.concatenate([inv, inv], 1)
    d_side = [tail_v[i, 0:ROWS, :] * inv2 for i in range(2)]

    pads = jnp.zeros((WIDE - ROWS, node), f32)
    side_parts = []
    for i in range(2):
        parts = split(d_side[i], 2)
        side_parts.append(parts)
        st = jnp.concatenate([p.astype(f32) for p in parts], 0).astype(bf16)
        ds = dot_nt(st[:, 0:chans], w_pairin_v[0].astype(bf16)) + dot_nt(
            st[:, chans : 2 * chans], w_pairin_v[1].astype(bf16)
        )
        ds = ds[0:ROWS] + ds[ROWS : 2 * ROWS]
        for k, p in enumerate(split(ds, 2)):
            at = (2 * k + i) * WIDE
            ds_v[at : at + WIDE, :] = jnp.concatenate([p.astype(f32), pads], 0).astype(bf16)
    fz = jnp.concatenate([frozen_v[0], frozen_v[1], frozen_v[0], frozen_v[1]], 0)
    g_in[...] = dot_tn(fz, ds_v[...])
    store(g_in, g_in_o)

    sg = jnp.concatenate([single_v[0], single_v[1], single_v[0], single_v[1]], 0).astype(bf16)
    st = jnp.concatenate(
        [side_parts[i][k].astype(f32) for k in range(2) for i in range(2)], 0
    ).astype(bf16)
    for k in range(2):
        g_pairin[k] = dot_tn(sg, st[:, k * chans : (k + 1) * chans])
    store(g_pairin, g_pairin_o)
    for m in range(n_mat):
        g_tri[m] = (gtri_v[0, m] + gtri_v[1, m]) * inv
    store(g_tri, g_tri_o)
    loss_s[...] = totals[4:5, :]
    count_s[...] = totals[5:6, :]
    g_vecs[...] = totals[0:4, :] * inv
    store(loss_s, loss_o)
    store(count_s, count_o)
    store(g_vecs, g_vecs_o)

    blk = chans
    n_in = width // blk
    n_pr = w_pairin_v.shape[1] // blk
    at_tri = 2 * n_pr
    for b in range(n_in):
        g = g_in[b * blk : (b + 1) * blk, :]
        sq_in[b * blk : (b + 1) * blk, :] = (g * g).astype(bf16)
    for k in range(2):
        for b in range(n_pr):
            g = g_pairin[k, b * blk : (b + 1) * blk, :]
            j = k * n_pr + b
            sq_rest[j * blk : (j + 1) * blk, :] = (g * g).astype(bf16)
    for m in range(n_mat):
        g = g_tri[m]
        j = at_tri + m
        sq_rest[j * blk : (j + 1) * blk, :] = (g * g).astype(bf16)
    sum_in[...] = dot(sq_in[...], jnp.ones((node, chans), bf16))
    sum_rest[...] = dot(sq_rest[...], jnp.ones((chans, chans), bf16))
    lane_in = dot_nt(jnp.ones((16, node), bf16), sq_in[...])[0:1]
    lane_rest = dot_nt(jnp.ones((16, chans), bf16), sq_rest[...])[0:1]

    def fresh(old, total, n):
        return BETA * old + ((1.0 - BETA) / n * total + (1.0 - BETA) * 1e-30)

    for b in range(n_in):
        row_in_n[b : b + 1, :] = fresh(
            row_in_v[b : b + 1, :], lane_in[:, b * blk : (b + 1) * blk], node
        )
    for k in range(2):
        s = slice(k * n_pr * blk, (k + 1) * n_pr * blk)
        row_pairin_n[k : k + 1, :] = fresh(row_pairin_v[k : k + 1, :], lane_rest[:, s], chans)
    for m in range(n_mat):
        s = slice((at_tri + m) * blk, (at_tri + m + 1) * blk)
        row_tri_n[m : m + 1, :] = fresh(row_tri_v[m : m + 1, :], lane_rest[:, s], chans)
    store(row_in_n, row_in_o)
    store(row_pairin_n, row_pairin_o)
    store(row_tri_n, row_tri_o)

    def fold(x):
        return jnp.sum(x.reshape(blk // 8, 8, x.shape[1]), 0)

    def adafactor(grad, weight, new, col_old, col_new, sums, old_at, n_blk, which, n_cols):
        n_rows = n_blk * blk
        halves = n_cols // chans
        col_sum = [jnp.zeros((8, chans), f32)] * halves
        scaled = [jnp.zeros((8, chans), f32)] * halves
        row_sum = jnp.zeros((8, chans), f32)
        for b in range(n_blk):
            s = slice(b * blk, (b + 1) * blk)
            o = slice((old_at + b) * blk, (old_at + b + 1) * blk)
            t = sums[0][(sums[1] + b) * blk : (sums[1] + b + 1) * blk, :]
            row = old_v[o, :] + ((1.0 - BETA) / n_cols * t + (1.0 - BETA) * 1e-30)
            row_sum = row_sum + fold(row)
            root = lax.rsqrt(row)
            for h in range(halves):
                c = slice(h * chans, (h + 1) * chans)
                g = grad[s, c]
                step = g * root
                new[s, c] = step
                col_sum[h] = col_sum[h] + fold(g * g)
                scaled[h] = scaled[h] + fold(step * step)
        row_mean = jnp.sum(row_sum, 0, keepdims=True) / n_rows
        power = jnp.zeros((1, chans), f32)
        by_col = []
        for h in range(halves):
            col = fresh(col_old(h), jnp.sum(col_sum[h], 0, keepdims=True), n_rows)
            col_new(h, col)
            power = power + jnp.sum(scaled[h], 0, keepdims=True) / col
            by_col.append(lax.rsqrt(col))
        rms = jnp.sqrt(row_mean * jnp.sum(power, -1, keepdims=True) / (n_rows * n_cols))
        coef = scale_v[which : which + 1, :] * jnp.sqrt(row_mean) / jnp.maximum(1.0, rms)
        for b in range(n_blk):
            s = slice(b * blk, (b + 1) * blk)
            for h in range(halves):
                c = slice(h * chans, (h + 1) * chans)
                new[s, c] = weight[s, c] - new[s, c] * (by_col[h] * coef)

    def put(ref, k):
        def put_col(h, col):
            at = k if k is not None else h
            ref[at : at + 1, :] = col

        return put_col

    adafactor(
        g_in, w_in_v, new_in, lambda h: col_in_v[h : h + 1, :], put(col_in_n, None), (sum_in, 0), 0,
        n_in, 0, node,
    )
    store(new_in, new_in_o)
    store(col_in_n, col_in_o)
    for k in range(2):
        adafactor(
            g_pairin.at[k], w_pairin_v.at[k], new_pairin.at[k],
            lambda h, k=k: col_pairin_v[k : k + 1, :], put(col_pairin_n, k),
            (sum_rest, k * n_pr), n_in + k * n_pr, n_pr, 1 + k, chans,
        )
    store(new_pairin, new_pairin_o)
    store(col_pairin_n, col_pairin_o)
    for m in range(n_mat):
        adafactor(
            g_tri.at[m], w_tri_v.at[m], new_tri.at[m],
            lambda h, m=m: col_tri_v[m : m + 1, :], put(col_tri_n, m),
            (sum_rest, at_tri + m), n_in + at_tri + m, 1, 3 + m, chans,
        )
    store(new_tri, new_tri_o)
    store(col_tri_n, col_tri_o)

    g = g_vecs[...]
    sq = BETA * sq_vecs_v[...] + (1.0 - BETA) * (g * g + 1e-30)
    sq_vecs_n[...] = sq
    step = g * lax.rsqrt(sq)
    step = step / jnp.maximum(1.0, jnp.sqrt(mean_last(step * step)))
    v = vecs_v[...]
    scale = jnp.maximum(0.001, jnp.sqrt(mean_last(v * v)))
    new_vecs[...] = v - RATE * scale * step
    store(sq_vecs_n, sq_vecs_o)
    store(new_vecs, new_vecs_o)
    for c in stores:
        c.wait()


def shards(
    tokens, lengths, recycle, resolved, coords, plm_embed, plm_uv, plm_qk, plm_affine, plm_out,
    w_in, w_pairin, w_tri, vecs, row_in, col_in, row_pairin, col_pairin, row_tri, col_tri, sq_vecs,
):
    heads = lax.axis_size("head")
    seq = tokens.shape[1]
    width = plm_embed.shape[1]
    units = plm_uv.shape[2]
    chans = vecs.shape[1]
    node = w_in.shape[1]
    shared_by = 2 if units % 256 == 0 else 1
    unit_part = units // shared_by
    anywhere = pl.BlockSpec(memory_space=pl.ANY)
    inside = pl.BlockSpec(memory_space=pltpu.VMEM)
    table = ROWS * ROWS

    def vm(*shape, dtype=f32):
        return pltpu.VMEM(shape, dtype)

    def like(x):
        return pltpu.VMEM(x.shape, x.dtype)

    coords = jnp.transpose(coords, (1, 0, 2))
    row_in2 = row_in.reshape(-1, chans)
    col_in2 = col_in.reshape(-1, chans)
    operands = (
        tokens, lengths, recycle, resolved, coords, plm_embed, plm_uv, plm_qk, plm_affine, plm_out,
        w_in, w_pairin, w_tri, vecs, row_in2, col_in2, row_pairin, col_pairin, row_tri, col_tri, sq_vecs,
    )
    kept = operands[10:]
    scratch = [
        like(tokens), like(resolved),
        like(coords), like(plm_embed), vm(2, width, unit_part, dtype=bf16), like(plm_qk),
        like(plm_affine), vm(shared_by, unit_part, width, dtype=bf16),
        vm(WIDE, width), vm(shared_by, ROWS, unit_part), vm(shared_by, WIDE, unit_part, dtype=bf16),
        vm(ROWS, width), vm(heads, 2, 16, width // 2 + width // 4, dtype=bf16),
        vm(width, node, dtype=bf16), vm(node, 2 * chans, dtype=bf16),
        vm(2 * chans, 6 * chans, dtype=bf16), vm(WIDE, chans), vm(seq, seq), vm(chans, seq),
        vm(table, chans), vm(table, chans), vm(table, chans), vm(table, chans),
        vm(table, chans, dtype=bf16), vm(table, 5 * chans), vm(table, chans), vm(table, chans),
        vm(table, chans), vm(table, chans), vm(table, chans), vm(table, chans), vm(table, chans),
        vm(table, chans), vm(table, chans, dtype=bf16),
        vm(table, chans), vm(table, chans), vm(table, chans, dtype=bf16), vm(table, chans),
        vm(table, chans), vm(table, 2 * chans), vm(table, 2 * chans), vm(table, 2 * chans),
        vm(table, chans), vm(table, chans), vm(table, 5 * chans, dtype=bf16),
        vm(3 * WIDE, chans, dtype=bf16), vm(chans, chans), vm(seq, chans, dtype=bf16),
        pltpu.SemaphoreType.DMA((19 + shared_by,)),
        pltpu.SemaphoreType.DMA((heads - 1, 2)), pltpu.SemaphoreType.DMA((heads, 2)),
        pltpu.SemaphoreType.DMA((2,)), pltpu.SemaphoreType.DMA((2,)),
        pltpu.SemaphoreType.DMA((6,)), pltpu.SemaphoreType.DMA((6,)),
    ]
    operands = tuple(
        x if x.size == 1 else pltpu.with_memory_space_constraint(x, pltpu.HBM) for x in operands
    )
    sds = jax.ShapeDtypeStruct
    n_blk = width // chans + 2 * (node // chans) + 6
    made = pl.pallas_call(
        functools.partial(tables_kernel, heads=heads, shared_by=shared_by, unit_part=unit_part),
        out_shape=(
            sds((2, WIDE, width), bf16), sds((2, ROWS, node), f32), sds((2, 6, chans, chans), f32),
            sds((2, WIDE, 2 * chans), f32), sds((n_blk * chans, chans), f32), sds((16, chans), f32),
        )
        + tuple(sds(x.shape, x.dtype) for x in kept),
        in_specs=[
            pl.BlockSpec(memory_space=pltpu.SMEM) if x.size == 1 else anywhere for x in operands
        ],
        out_specs=[inside] * (6 + len(kept)),
        scratch_shapes=scratch,
        compiler_params=pltpu.CompilerParams(
            collective_id=0, has_side_effects=True, vmem_limit_bytes=48 << 20
        ),
        name="tables",
    )(*operands)

    operands = tuple(made)
    outs = (
        sds((1, chans), f32), sds((1, chans), f32), w_in, row_in2, col_in2, w_in, w_pairin,
        row_pairin, col_pairin, w_pairin, w_tri, row_tri, col_tri, w_tri, vecs, vecs, vecs,
    )
    outs = tuple(sds(x.shape, x.dtype) for x in outs)
    scratch = (
        [like(x) for x in outs]
        + [
            vm(4 * WIDE, node, dtype=bf16), vm(width, node, dtype=bf16),
            vm((n_blk - width // chans) * chans, chans, dtype=bf16), vm(width, chans),
            vm((n_blk - width // chans) * chans, chans),
            pltpu.SemaphoreType.DMA((17,)),
        ]
    )
    res = list(
        pl.pallas_call(
            update_kernel,
            out_shape=outs,
            in_specs=[inside] * len(operands),
            out_specs=[anywhere] * len(outs),
            scratch_shapes=scratch,
            compiler_params=pltpu.CompilerParams(vmem_limit_bytes=32 << 20),
            name="update",
        )(*operands)
    )
    res[0] = res[0][0, 0]
    res[1] = res[1][0, 0]
    res[3] = res[3].reshape(-1)
    res[4] = res[4].reshape(-1)
    return tuple(res)


def solution(mesh):
    whole = P()
    in_specs = (
        P("grp", None), P("grp"), P("grp"), P("grp", None), P("grp", None, None), whole,
        P(None, None, "head"), whole, whole, P("head", None),
    ) + (whole,) * 11
    return jax.shard_map(
        shards, mesh=mesh, in_specs=in_specs, out_specs=(whole,) * 17, check_vma=False
    )
```

```python
import functools
import math

import jax
import jax.numpy as jnp
from jax import lax
from jax.experimental import pallas as pl
from jax.experimental.pallas import tpu as pltpu
from jax.sharding import PartitionSpec as P


STEP = 10
ORDER = (0, 1, 4, 2, 3)
BETA = 1.0 - STEP ** (-0.8)
RATE = 0.3
MESH = pl.DeviceIdType.MESH
f32 = jnp.float32
bf16 = jnp.bfloat16
ROWS = 24
WIDE = 32


def dot(a, b):
    return jnp.dot(a, b, preferred_element_type=f32)


def dot_nt(a, b):
    return lax.dot_general(a, b, (((1,), (1,)), ((), ())), preferred_element_type=f32)


def dot_tn(a, b):
    return lax.dot_general(a, b, (((0,), (0,)), ((), ())), preferred_element_type=f32)


def silu(x):
    return x * jax.nn.sigmoid(x)


def mean_last(x):
    return jnp.mean(x, -1, keepdims=True)


def split(x, parts):
    out = []
    for _ in range(parts):
        part = x.astype(bf16)
        out.append(part)
        x = x - part.astype(f32)
    return out


def iota(shape, dim):
    return lax.broadcasted_iota(jnp.int32, shape, dim)


def fresh(old, total, n):
    return BETA * old + ((1.0 - BETA) / n * total + (1.0 - BETA) * 1e-30)


def fold(x):
    return jnp.sum(x.reshape(x.shape[0] // 8, 8, x.shape[1]), 0)


def adafactor(grad, weight, new, col_old, col_new, sums, old, scale):
    n_rows, n_cols = grad.shape
    chans = old.shape[1]
    blk = chans
    halves = n_cols // chans
    col_sum = [jnp.zeros((8, chans), f32)] * halves
    scaled = [jnp.zeros((8, chans), f32)] * halves
    row_sum = jnp.zeros((8, chans), f32)
    for b in range(n_rows // blk):
        s = slice(b * blk, (b + 1) * blk)
        row = old[s, :] + ((1.0 - BETA) / n_cols * sums[s, :] + (1.0 - BETA) * 1e-30)
        row_sum = row_sum + fold(row)
        root = lax.rsqrt(row)
        for h in range(halves):
            c = slice(h * chans, (h + 1) * chans)
            g = grad[s, c]
            step = g * root
            new[s, c] = step
            col_sum[h] = col_sum[h] + fold(g * g)
            scaled[h] = scaled[h] + fold(step * step)
    row_mean = jnp.sum(row_sum, 0, keepdims=True) / n_rows
    power = jnp.zeros((1, chans), f32)
    by_col = []
    for h in range(halves):
        col = fresh(col_old(h), jnp.sum(col_sum[h], 0, keepdims=True), n_rows)
        col_new(h, col)
        power = power + jnp.sum(scaled[h], 0, keepdims=True) / col
        by_col.append(lax.rsqrt(col))
    rms = jnp.sqrt(row_mean * jnp.sum(power, -1, keepdims=True) / (n_rows * n_cols))
    coef = scale * jnp.sqrt(row_mean) / jnp.maximum(1.0, rms)
    by_col = [x * coef for x in by_col]

    def second(b, carry):
        s = pl.ds(b * blk, blk)
        for h in range(halves):
            c = slice(h * chans, (h + 1) * chans)
            new[s, c] = weight[s, c] - new[s, c] * by_col[h]
        return carry

    if n_rows == blk:
        second(0, 0)
    else:
        lax.fori_loop(0, n_rows // blk, second, 0)


def tables_kernel(
    tokens_h, lengths_s, recycle_s, resolved_h, coords_h, embed_h, uv_h, qk_h, affine_h, out_h,
    w_in_h, w_pairin_h, w_tri_h, vecs_h, row_in_h, col_in_h, row_pairin_h, col_pairin_h, row_tri_h,
    col_tri_h, sq_vecs_h,
    frozen_o, single_o, tail_o, old_o, scale_o, g_tri_o, new_tri_o, row_tri_o, col_tri_o,
    w_in_v, w_pairin_v, w_tri_v, vecs_v, row_in_v, col_in_v, row_pairin_v, col_pairin_v, row_tri_v,
    col_tri_v, sq_vecs_v,
    tokens_v, resolved_v, coords_v, embed_v, uv_v, qk_v, affine_v, out_v,
    emb, gate_x, value_x, partial_v, part, w_in_b, w_pair_b, w_tri_b, cnt_b, true_d, cols,
    pair, sb, n1, s1, pnorm, proj, sig_l, sig_r, gate, left, right, upd, n2, s2, unorm,
    branch, final, dbranch, left_n, gated_b, dunorm, dpnorm, dlast, dleft, dright, dproj,
    old_v, one_t, gtri_x, sq_tri, sum_tri,
    load_sem, part_send, part_recv, unit_send, unit_recv, peer_send, peer_recv,
    *, heads, shared_by, unit_part,
):
    grp = lax.axis_index("grp")
    head = lax.axis_index("head")
    other = 1 - grp
    seq = tokens_v.shape[1]
    width = emb.shape[1]
    chans = vecs_v.shape[1]
    vocab = embed_v.shape[0]
    half = width // 2
    quarter = width // 4

    loads = []

    def load(src, dst):
        copy = pltpu.make_async_copy(src, dst, load_sem.at[len(loads)])
        loads.append(copy)
        copy.start()
        return copy

    c_small = [
        load(embed_h, embed_v),
        load(tokens_h, tokens_v),
        load(affine_h, affine_v),
    ]
    mine = grp if shared_by == 2 else 0
    at_mine = pl.multiple_of(mine * unit_part, 128)
    c_gate = load(uv_h.at[0, :, pl.ds(at_mine, unit_part)], uv_v.at[0])
    c_value = load(uv_h.at[1, :, pl.ds(at_mine, unit_part)], uv_v.at[1])
    c_qk = load(qk_h, qk_v)
    c_out = []
    for k in range(shared_by):
        at = pl.multiple_of(lax.rem(mine + k, shared_by) * unit_part, 128)
        c_out.append(load(out_h.at[pl.ds(at, unit_part)], out_v.at[k]))
    c_pairs = [load(resolved_h, resolved_v), load(coords_h, coords_v)]
    c_par = [
        load(w_in_h, w_in_v),
        load(w_pairin_h, w_pairin_v),
        load(w_tri_h, w_tri_v),
        load(vecs_h, vecs_v),
        load(row_in_h, row_in_v),
        load(row_pairin_h, row_pairin_v),
        load(row_tri_h, row_tri_v),
        load(col_in_h, col_in_v),
        load(col_pairin_h, col_pairin_v),
        load(col_tri_h, col_tri_v),
        load(sq_vecs_h, sq_vecs_v),
    ]

    barrier = pltpu.get_barrier_semaphore()
    pl.semaphore_signal(barrier, inc=1, device_id={"grp": other}, device_id_type=MESH)
    for d in range(1, heads):
        peer = lax.rem(head + d, heads)
        pl.semaphore_signal(barrier, inc=1, device_id={"head": peer}, device_id_type=MESH)

    for c in c_small:
        c.wait()
    emb[...] = jnp.zeros_like(emb)
    emb[0:vocab, :] = embed_v[...].astype(f32)
    e = emb[...]
    centre = e - mean_last(e)
    normed = (centre * lax.rsqrt(mean_last(centre * centre) + 1e-05)).astype(bf16)

    length = lengths_s[0]
    recycle = recycle_s[0].astype(f32)
    tok = tokens_v[...]
    onehot = (iota((WIDE, seq), 0) == tok).astype(f32)
    key_ok = (iota((1, seq), 1) < length).astype(f32)
    one_b = onehot.astype(bf16)
    cnt_col = jnp.sum(onehot, -1, keepdims=True)
    cnt_b[...] = jnp.broadcast_to(cnt_col, (WIDE, chans))
    ones = jnp.ones((16, seq), bf16)
    cnt_row = dot_nt(ones, one_b)[0:1, :]
    key_row = dot_nt(ones, (onehot * key_ok).astype(bf16))[0:1, :]

    pl.semaphore_wait(barrier, heads)
    unit_sends = []

    def swap(ref, k):
        copy = pltpu.make_async_remote_copy(
            src_ref=ref.at[0],
            dst_ref=ref.at[1],
            send_sem=unit_send.at[k],
            recv_sem=unit_recv.at[k],
            device_id={"grp": other},
            device_id_type=MESH,
        )
        copy.start()
        unit_sends.append(copy)

    c_gate.wait()
    ugate = silu(dot(normed, uv_v[0]))
    gate_x[0] = ugate[0:ROWS]
    if shared_by == 2:
        swap(gate_x, 0)
    c_value.wait()
    value_x[0] = silu(dot(normed, uv_v[1])).astype(bf16)
    if shared_by == 2:
        swap(value_x, 1)

    c_qk.wait()
    shared = silu(dot(normed, qk_v[...]))
    query = (shared * affine_v[0:1, :] + affine_v[1:2, :]).astype(bf16)
    keyed = (shared * affine_v[2:3, :] + affine_v[3:4, :]).astype(bf16)
    scores = dot_nt(query, keyed) / math.sqrt(qk_v.shape[1])
    masked = jnp.where(key_row > 0, scores, -1000000000.0)
    top = jnp.exp(masked - jnp.max(masked, -1, keepdims=True))
    attn = (top / jnp.sum(top * key_row, -1, keepdims=True)).astype(bf16).astype(f32)
    attn = jnp.concatenate(split(attn * key_row, 2), 0)

    def mix(k):
        seen = dot(attn, value_x[k])
        seen = seen[0:ROWS] + seen[WIDE : WIDE + ROWS]
        return (gate_x[k] * seen).astype(bf16)

    mixed = mix(0)
    c_out[0].wait()
    if shared_by == 2:
        partial_v[...] = dot(mixed, out_v[0])
        for c in unit_sends:
            c.wait_recv()
        mixed = mix(1)
        c_out[1].wait()
    sends = []
    for n in range(2):
        s = slice(n * half, (n + 1) * half)
        p = dot(mixed, out_v[shared_by - 1, :, s])
        if shared_by == 2:
            p = p + partial_v[:, s]
        part[head, n, :, 0:half] = p[0:16].astype(bf16)
        part[head, n, :, half : half + quarter] = jnp.concatenate(
            [p[16:24, 0:quarter], p[16:24, quarter:half]], 0
        ).astype(bf16)
        for d in range(1, heads):
            copy = pltpu.make_async_remote_copy(
                src_ref=part.at[head, n],
                dst_ref=part.at[head, n],
                send_sem=part_send.at[d - 1, n],
                recv_sem=part_recv.at[head, n],
                device_id={"head": lax.rem(head + d, heads)},
                device_id_type=MESH,
            )
            copy.start()
            sends.append(copy)

    for c in c_pairs + c_par:
        c.wait()
    w_in_b[...] = w_in_v[...].astype(bf16)
    for k in range(2):
        w_pair_b[:, k * chans : (k + 1) * chans] = w_pairin_v[k].astype(bf16)
    v0 = vecs_v[0:1, :]
    v1 = vecs_v[1:2, :]
    v2 = vecs_v[2:3, :]
    v3 = vecs_v[3:4, :]
    gain_one = vecs_v[...].T[:, 1:2]
    gain_two = vecs_v[...].T[:, 2:3]
    for k, m in enumerate(ORDER + (5,)):
        c = slice(k * chans, (k + 1) * chans)
        w = w_tri_v[m].astype(bf16)
        w_tri_b[0:chans, c] = w
        w = w.astype(f32) * (gain_two if m == 5 else gain_one)
        w = jnp.sum(w, 0, keepdims=True) * (1.0 / chans)
        w_tri_b[chans : 2 * chans, c] = jnp.broadcast_to(w, (chans, chans)).astype(bf16)
    valid = key_ok * (resolved_v[...] > 0).astype(f32)
    cols[...] = jnp.zeros_like(cols)
    for k in range(3):
        cols[k : k + 1, :] = coords_v[k]
    cols[3:4, :] = valid
    cols[4:5, :] = tok.astype(f32)
    one_v = (onehot * valid).astype(bf16)
    weight_j = recycle * valid
    blk = 128
    n_blk = seq // blk
    places = []
    for b in range(n_blk):
        t = cols[:, b * blk : (b + 1) * blk].T
        hot = lax.bitwise_and(iota((blk, chans), 1), WIDE - 1) == t[:, 4:5].astype(jnp.int32)
        hot = hot & (iota((blk, chans), 1) < 3 * WIDE)
        one_t[b * blk : (b + 1) * blk, :] = hot.astype(f32).astype(bf16)
        places.append(t)
        d2 = None
        for k in range(3):
            delta = t[:, k : k + 1] - cols[k : k + 1, :]
            d2 = delta * delta if d2 is None else d2 + delta * delta
        true_d[b * blk : (b + 1) * blk, :] = jnp.sqrt(d2)
    n_valid = jnp.sum(valid, -1, keepdims=True)
    loss_count = recycle * n_valid * n_valid

    present = cnt_b[0:ROWS, :] > 0
    sc = jnp.where((cnt_row > 0) & (cnt_col > 0), scores, 0.0)[0:ROWS]

    n_chunk = ROWS // 2
    two = 2 * ROWS

    def rows(k):
        return slice(k * two, (k + 1) * two)

    def both(f, k):
        return jnp.concatenate([f(2 * k), f(2 * k + 1)], 0)

    v0c = v0 - mean_last(v0)
    for k in range(n_chunk):
        r = rows(k)
        sbk = both(lambda u: jnp.broadcast_to(sc[:, u : u + 1], (ROWS, chans)), k)
        sb[r] = sbk
        pair[r] = sbk * v0
        n1[r] = sbk * v0c
    lane = iota((ROWS, chans), 1)
    score_logit = jnp.sum(v0 * v3, -1, keepdims=True) * jnp.concatenate(
        [sc, jnp.zeros((ROWS, chans - WIDE), f32)], 1
    )

    n_in = width // chans
    n_pr = w_pairin_v.shape[1] // chans
    at_tri = n_in + 2 * n_pr
    old_v[...] = jnp.zeros_like(old_v)
    old_v[0:n_in, :] = row_in_v[...]
    for k in range(2):
        for b in range(n_pr):
            j = n_in + k * n_pr + b
            old_v[j : j + 1, :] = row_pairin_v[k : k + 1, b * chans : (b + 1) * chans]
    old_v[at_tri : at_tri + 6, :] = row_tri_v[...]
    old = BETA * old_v[...].T
    for k in range(at_tri + 6):
        old_o[k * chans : (k + 1) * chans, :] = jnp.broadcast_to(old[:, k : k + 1], (chans, chans))
    scale_o[...] = jnp.zeros_like(scale_o)
    mats = [w_in_v] + [w_pairin_v.at[k] for k in range(2)] + [w_tri_v.at[m] for m in range(6)]
    for k, w in enumerate(mats):
        x = w[...]
        x = jnp.sum(jnp.sum(x * x, 0, keepdims=True), -1, keepdims=True) / (w.shape[0] * w.shape[1])
        x = RATE * jnp.maximum(0.001, jnp.sqrt(x))
        scale_o[k : k + 1, :] = jnp.broadcast_to(x, (1, chans))

    for n in range(2):
        for d in range(1, heads):
            peer = lax.rem(head + d, heads)
            pltpu.make_async_remote_copy(
                src_ref=part.at[peer, n],
                dst_ref=part.at[peer, n],
                send_sem=part_send.at[d - 1, n],
                recv_sem=part_recv.at[peer, n],
                device_id={"head": peer},
                device_id_type=MESH,
            ).wait_recv()
    for n in range(2):
        s = slice(n * half, (n + 1) * half)
        low = None
        for k in range(heads):
            a = part[k, n, :, 0:half].astype(f32)
            b = part[k, n, :, half : half + quarter].astype(f32)
            b = jnp.concatenate([b[0:8], b[8:16]], 1)
            low = [a, b] if low is None else [low[0] + a, low[1] + b]
        emb[0:16, s] += low[0]
        emb[16:24, s] += low[1]
    state = emb[0:ROWS, :]
    centre = state - mean_last(state)
    frozen = centre * lax.rsqrt(mean_last(centre * centre) + 1e-05)
    frozen = jnp.concatenate([frozen, jnp.zeros((WIDE - ROWS, width), f32)], 0).astype(bf16)
    frozen_o[grp] = frozen

    peers = []

    def give(ref):
        k = len(peers)
        copy = pltpu.make_async_remote_copy(
            src_ref=ref,
            dst_ref=ref,
            send_sem=peer_send.at[k],
            recv_sem=peer_recv.at[k],
            device_id={"grp": other},
            device_id_type=MESH,
        )
        copy.start()
        peers.append(copy)
        return copy

    give(frozen_o.at[grp])
    single = dot(frozen, w_in_b[...]).astype(bf16)
    single_o[grp] = jnp.concatenate(
        [single[0:ROWS].astype(f32), jnp.broadcast_to(loss_count, (8, single.shape[1]))], 0
    )
    c_single = give(single_o.at[grp])
    side = dot(single, w_pair_b[...])[0:ROWS]
    side_a = jnp.where(present, side[:, 0:chans], 0.0)
    side_b = jnp.where(present, side[:, chans : 2 * chans], 0.0)
    side_ac = side_a - mean_last(side_a)
    side_bc = side_b - mean_last(side_b)

    own = iota((ROWS, chans), 0) == lane
    logit_b = jnp.sum(
        jnp.where(own, jnp.sum(side_b * v3, -1, keepdims=True), 0.0), 0, keepdims=True
    )
    logit = score_logit + jnp.sum(side_a * v3, -1, keepdims=True) + logit_b
    for k in range(n_chunk):
        r = rows(k)
        pair[r] = pair[r] + both(lambda u: side_a + side_b[u : u + 1, :], k)
        centre = n1[r] + both(lambda u: side_ac + side_bc[u : u + 1, :], k)
        scale = lax.rsqrt(mean_last(centre * centre) + 1e-05)
        normal = centre * scale
        n1[r] = normal
        s1[r] = jnp.broadcast_to(scale, (two, chans))
        pnorm[r] = (normal * v1).astype(bf16)
    proj[...] = dot(pnorm[...], w_tri_b[0:chans, 0 : 5 * chans])
    for k in range(n_chunk):
        r = rows(k)
        sl = jax.nn.sigmoid(proj[r, chans : 2 * chans])
        sr = jax.nn.sigmoid(proj[r, 4 * chans : 5 * chans])
        sig_l[r] = sl
        sig_r[r] = sr
        left[r] = (sl * proj[r, 0:chans]).astype(bf16).astype(f32)
        right[r] = (sr * proj[r, 3 * chans : 4 * chans]).astype(bf16).astype(f32)
        gate[r] = jax.nn.sigmoid(proj[r, 2 * chans : 3 * chans])
        left_n[r] = left[r] * both(
            lambda u: jnp.broadcast_to(cnt_b[u : u + 1, :], (ROWS, chans)), k
        )

    def triangle(dst, moving, fixed, row_of, weighted):
        group = 4
        for a0 in range(0, ROWS, group):
            total = [None] * group
            for b in range(vocab):
                x = moving(b)
                for q in range(group):
                    y = x * fixed[pl.ds(row_of(a0 + q, b), 1), :]
                    total[q] = y if total[q] is None else total[q] + y
            for q in range(group):
                a = a0 + q
                t = total[q]
                if weighted:
                    t = t * cnt_b[a : a + 1, :]
                dst[a * ROWS : (a + 1) * ROWS, :] = t

    triangle(
        upd, lambda u: left_n[u * ROWS : (u + 1) * ROWS, :], right, lambda v, u: u * ROWS + v, False
    )
    for k in range(n_chunk):
        r = rows(k)
        x = upd[r]
        centre = x - mean_last(x)
        scale = lax.rsqrt(mean_last(centre * centre) + 1e-05)
        normal = centre * scale
        n2[r] = normal
        s2[r] = jnp.broadcast_to(scale, (two, chans))
        unorm[r] = (normal * v2).astype(bf16)
    branch[...] = dot(unorm[...], w_tri_b[0:chans, 5 * chans : 6 * chans])
    gated = jnp.zeros((ROWS, chans), f32)
    for k in range(n_chunk):
        r = rows(k)
        move = gate[r] * branch[r]
        final[r] = pair[r] + move
        col = jnp.sum(move * v3, -1, keepdims=True)
        gated_b[r] = jnp.broadcast_to(col, (two, chans))
        for q in range(2):
            gated = jnp.where(lane == 2 * k + q, col[q * ROWS : (q + 1) * ROWS], gated)
    logit = logit + gated

    dist = jnp.maximum(logit, 0.0) + jnp.log(1.0 + jnp.exp(-jnp.abs(logit)))
    dist = jnp.concatenate([dist, jnp.zeros((WIDE - ROWS, chans), f32)], 0)
    dist = jnp.concatenate(split(dist, 3), 0)
    by_col = dot(dist[:, 0:WIDE], one_b).astype(bf16)
    for k in range(n_chunk):
        r = rows(k)
        sl, sr, gt = sig_l[r], sig_r[r], gate[r]
        proj[r, 0:chans] = proj[r, 0:chans] * sl * (1.0 - sl)
        proj[r, 3 * chans : 4 * chans] = proj[r, 3 * chans : 4 * chans] * sr * (1.0 - sr)
        gt3 = gt * v3
        proj[r, 2 * chans : 3 * chans] = gt3 * (1.0 - gt) * branch[r]
        gate[r] = gt3
    loss_row = jnp.zeros((1, seq), f32)
    by_first = jnp.zeros((WIDE, seq), f32)
    for b in range(n_blk):
        s = slice(b * blk, (b + 1) * blk)
        diff = dot(one_t[s, 0 : 3 * WIDE], by_col) - true_d[s, :]
        sq = diff * diff + 1.0
        inv = lax.rsqrt(sq)
        loss_row = loss_row + jnp.sum(
            places[b][:, 3:4] * (sq * inv - 1.0), 0, keepdims=True
        )
        by_first = by_first + dot(one_v[:, s], (diff * inv).astype(bf16))
    loss = jnp.sum(loss_row * weight_j, -1, keepdims=True)
    by_pair = dot_nt(jnp.concatenate(split(by_first * weight_j, 2), 0), one_b)
    by_pair = (by_pair[0:WIDE] + by_pair[WIDE : 2 * WIDE])[0:ROWS]
    dlogit = by_pair * jax.nn.sigmoid(logit)[:, 0:WIDE]

    g_dist = jnp.zeros((two, chans), f32)
    for k in range(n_chunk):
        r = rows(k)
        g = both(lambda u: jnp.broadcast_to(dlogit[:, u : u + 1], (ROWS, chans)), k)
        g_dist = g_dist + g * final[r]
        dfinal = g * v3
        pair[r] = dfinal
        dbranch[r] = (g * gate[r]).astype(bf16)
        dproj[r, 2 * chans : 3 * chans] = (g * proj[r, 2 * chans : 3 * chans]).astype(bf16)
        gated_b[r] = g * gated_b[r] * (1.0 / chans)
    dunorm[...] = dot_nt(dbranch[...], w_tri_b[:, 5 * chans : 6 * chans])
    gtri_x[grp, 5] = dot_tn(unorm[...], dbranch[...])
    gtri_x[grp, 4] = dot_tn(pnorm[...], dproj[:, 2 * chans : 3 * chans])
    c_pair = [give(gtri_x.at[grp, pl.ds(4, 2)])]
    g_two = jnp.zeros((two, chans), f32)
    for k in range(n_chunk):
        r = rows(k)
        dn = dunorm[r, 0:chans]
        normal = n2[r]
        g_two = g_two + dn * normal
        upd[r] = s2[r] * (dn * v2 - dunorm[r, chans : 2 * chans] - normal * gated_b[r])
    triangle(
        dleft, lambda v: upd[v * ROWS : (v + 1) * ROWS, :], right, lambda u, v: u * ROWS + v, True
    )
    for k in range(n_chunk):
        r = rows(k)
        d, sl = dleft[r], sig_l[r]
        dproj[r, 0:chans] = (d * sl).astype(bf16)
        dproj[r, chans : 2 * chans] = (d * proj[r, 0:chans]).astype(bf16)
    dpnorm[...] = dot_nt(dproj[:, 0 : 3 * chans], w_tri_b[:, 0 : 3 * chans])
    g = dot_tn(pnorm[...], dproj[:, 0 : 2 * chans])
    gtri_x[grp, 0] = g[:, 0:chans]
    gtri_x[grp, 1] = g[:, chans : 2 * chans]
    c_pair.append(give(gtri_x.at[grp, pl.ds(0, 2)]))
    triangle(
        dright, lambda t: upd[pl.ds(t, ROWS, stride=ROWS), :], left, lambda u, t: u * ROWS + t, True
    )
    for k in range(n_chunk):
        r = rows(k)
        d, sr = dright[r], sig_r[r]
        dproj[r, 3 * chans : 4 * chans] = (d * sr).astype(bf16)
        dproj[r, 4 * chans : 5 * chans] = (d * proj[r, 3 * chans : 4 * chans]).astype(bf16)
    dlast[...] = dot_nt(dproj[:, 3 * chans : 5 * chans], w_tri_b[:, 3 * chans : 5 * chans])
    g = dot_tn(pnorm[...], dproj[:, 3 * chans : 5 * chans])
    gtri_x[grp, 2] = g[:, 0:chans]
    gtri_x[grp, 3] = g[:, chans : 2 * chans]
    c_pair.append(give(gtri_x.at[grp, pl.ds(2, 2)]))
    g_one = jnp.zeros((two, chans), f32)
    g_score = jnp.zeros((two, chans), f32)
    d_a = jnp.zeros((ROWS, chans), f32)
    tail_o[grp] = jnp.zeros((WIDE, 2 * chans), f32)
    for k in range(n_chunk):
        r = rows(k)
        dn = dpnorm[r, 0:chans] + dlast[r, 0:chans]
        mean = dpnorm[r, chans : 2 * chans] + dlast[r, chans : 2 * chans]
        normal = n1[r]
        along = dn * normal
        g_one = g_one + along
        dpair = pair[r] + s1[r] * (dn * v1 - mean - normal * mean_last(along * v1))
        g_score = g_score + sb[r] * dpair
        d_a = d_a + dpair[0:ROWS] + dpair[ROWS:two]
        for q in range(2):
            tail_o[grp, 2 * k + q : 2 * k + q + 1, chans : 2 * chans] = jnp.sum(
                dpair[q * ROWS : (q + 1) * ROWS], 0, keepdims=True
            )
    tail_o[grp, 0:ROWS, 0:chans] = d_a
    for k, g in enumerate((g_score, g_one, g_two, g_dist)):
        tail_o[grp, ROWS + k : ROWS + k + 1, 0:chans] = jnp.sum(g, 0, keepdims=True)
    tail_o[grp, ROWS + 4 : ROWS + 5, 0:chans] = jnp.broadcast_to(loss, (1, chans))
    tail_o[grp, ROWS + 5 : ROWS + 6, 0:chans] = jnp.broadcast_to(loss_count, (1, chans))
    c_tail = give(tail_o.at[grp])

    c_single.wait_recv()
    inv = 1.0 / (
        single_o[0, ROWS : ROWS + 1, 0:chans] + single_o[1, ROWS : ROWS + 1, 0:chans]
    )
    for pairs in ((0, 1), (2,)):
        mats = []
        for k in pairs:
            c_pair[k].wait_recv()
            first = (4, 0, 2)[k]
            mats += [first, first + 1]
        for m in mats:
            g = (gtri_x[0, m] + gtri_x[1, m]) * inv
            g_tri_o[m] = g
            sq_tri[m * chans : (m + 1) * chans, :] = (g * g).astype(bf16)
        for m in mats:
            r = slice(m * chans, (m + 1) * chans)
            sum_tri[r, :] = dot(sq_tri[r, :], jnp.ones((chans, chans), bf16))
        for m in mats:
            total = sum_tri[m * chans : (m + 1) * chans, :].T[0:1, :]
            row_tri_o[m : m + 1, :] = fresh(row_tri_v[m : m + 1, :], total, chans)

            def put_col(h, col, m=m):
                col_tri_o[m : m + 1, :] = col

            adafactor(
                g_tri_o.at[m], w_tri_v.at[m], new_tri_o.at[m],
                lambda h, m=m: col_tri_v[m : m + 1, :], put_col,
                sum_tri.at[pl.ds(m * chans, chans)],
                old_o.at[pl.ds((at_tri + m) * chans, chans)],
                scale_o[3 + m : 4 + m, :],
            )

    for c in sends + unit_sends + peers:
        c.wait_send()
    for c in peers:
        if c is not c_single and all(c is not x for x in c_pair):
            c.wait_recv()


def update_kernel(
    frozen_v, single_v, tail_v, old_v, scale_v, g_tri, new_tri, row_tri_n, col_tri_n,
    w_in_v, w_pairin_v, w_tri_v, vecs_v,
    row_in_v, col_in_v, row_pairin_v, col_pairin_v, row_tri_v, col_tri_v, sq_vecs_v,
    loss_o, count_o, g_in_o, row_in_o, col_in_o, new_in_o, g_pairin_o, row_pairin_o, col_pairin_o,
    new_pairin_o, g_tri_o, row_tri_o, col_tri_o, new_tri_o, g_vecs_o, sq_vecs_o, new_vecs_o,
    loss_s, count_s, g_in, row_in_n, col_in_n, new_in, g_pairin, row_pairin_n, col_pairin_n,
    new_pairin, g_vecs, sq_vecs_n, new_vecs,
    ds_v, sq_in, sq_rest, sum_in, sum_rest, store_sem,
):
    chans = vecs_v.shape[1]
    width, node = w_in_v.shape
    stores = []

    def store(src, dst):
        copy = pltpu.make_async_copy(src, dst, store_sem.at[len(stores)])
        stores.append(copy)
        copy.start()

    store(g_tri, g_tri_o)
    store(new_tri, new_tri_o)
    store(row_tri_n, row_tri_o)
    store(col_tri_n, col_tri_o)
    totals = tail_v[0, ROWS : ROWS + 8, 0:chans] + tail_v[1, ROWS : ROWS + 8, 0:chans]
    inv = 1.0 / totals[5:6, :]
    inv2 = jnp.concatenate([inv, inv], 1)
    d_side = [tail_v[i, 0:ROWS, :] * inv2 for i in range(2)]

    pads = jnp.zeros((WIDE - ROWS, node), f32)
    side_parts = []
    for i in range(2):
        parts = split(d_side[i], 2)
        side_parts.append(parts)
        st = jnp.concatenate([p.astype(f32) for p in parts], 0).astype(bf16)
        ds = dot_nt(st[:, 0:chans], w_pairin_v[0].astype(bf16)) + dot_nt(
            st[:, chans : 2 * chans], w_pairin_v[1].astype(bf16)
        )
        ds = ds[0:ROWS] + ds[ROWS : 2 * ROWS]
        for k, p in enumerate(split(ds, 2)):
            at = (2 * k + i) * WIDE
            ds_v[at : at + WIDE, :] = jnp.concatenate([p.astype(f32), pads], 0).astype(bf16)
    fz = jnp.concatenate([frozen_v[0], frozen_v[1], frozen_v[0], frozen_v[1]], 0)
    g_in[...] = dot_tn(fz, ds_v[...])
    store(g_in, g_in_o)

    sg = [single_v[i, 0:ROWS] for i in range(2)]
    sg = jnp.concatenate(sg + sg, 0).astype(bf16)
    st = jnp.concatenate(
        [side_parts[i][k].astype(f32) for k in range(2) for i in range(2)], 0
    ).astype(bf16)
    for k in range(2):
        g_pairin[k] = dot_tn(sg, st[:, k * chans : (k + 1) * chans])
    store(g_pairin, g_pairin_o)
    loss_s[...] = totals[4:5, :]
    count_s[...] = totals[5:6, :]
    g_vecs[...] = totals[0:4, :] * inv
    store(loss_s, loss_o)
    store(count_s, count_o)
    store(g_vecs, g_vecs_o)

    blk = chans
    n_in = width // blk
    n_pr = w_pairin_v.shape[1] // blk
    for b in range(n_in):
        g = g_in[b * blk : (b + 1) * blk, :]
        sq_in[b * blk : (b + 1) * blk, :] = (g * g).astype(bf16)
    for k in range(2):
        for b in range(n_pr):
            g = g_pairin[k, b * blk : (b + 1) * blk, :]
            j = k * n_pr + b
            sq_rest[j * blk : (j + 1) * blk, :] = (g * g).astype(bf16)
    sum_in[...] = dot(sq_in[...], jnp.ones((node, chans), bf16))
    sum_rest[...] = dot(sq_rest[...], jnp.ones((chans, chans), bf16))
    for b in range(n_in):
        total = sum_in[b * blk : (b + 1) * blk, :].T[0:1, :]
        row_in_n[b : b + 1, :] = fresh(row_in_v[b : b + 1, :], total, node)
    for k in range(2):
        for b in range(n_pr):
            j = k * n_pr + b
            total = sum_rest[j * blk : (j + 1) * blk, :].T[0:1, :]
            c = slice(b * blk, (b + 1) * blk)
            row_pairin_n[k : k + 1, c] = fresh(row_pairin_v[k : k + 1, c], total, chans)
    store(row_in_n, row_in_o)
    store(row_pairin_n, row_pairin_o)

    def put(ref, k):
        def put_col(h, col):
            at = k if k is not None else h
            ref[at : at + 1, :] = col

        return put_col

    adafactor(
        g_in, w_in_v, new_in, lambda h: col_in_v[h : h + 1, :], put(col_in_n, None), sum_in,
        old_v.at[pl.ds(0, width)], scale_v[0:1, :],
    )
    store(new_in, new_in_o)
    store(col_in_n, col_in_o)
    for k in range(2):
        adafactor(
            g_pairin.at[k], w_pairin_v.at[k], new_pairin.at[k],
            lambda h, k=k: col_pairin_v[k : k + 1, :], put(col_pairin_n, k),
            sum_rest.at[pl.ds(k * n_pr * blk, n_pr * blk)],
            old_v.at[pl.ds((n_in + k * n_pr) * blk, n_pr * blk)], scale_v[1 + k : 2 + k, :],
        )
    store(new_pairin, new_pairin_o)
    store(col_pairin_n, col_pairin_o)

    g = g_vecs[...]
    sq = BETA * sq_vecs_v[...] + (1.0 - BETA) * (g * g + 1e-30)
    sq_vecs_n[...] = sq
    step = g * lax.rsqrt(sq)
    step = step / jnp.maximum(1.0, jnp.sqrt(mean_last(step * step)))
    v = vecs_v[...]
    scale = jnp.maximum(0.001, jnp.sqrt(mean_last(v * v)))
    new_vecs[...] = v - RATE * scale * step
    store(sq_vecs_n, sq_vecs_o)
    store(new_vecs, new_vecs_o)
    for c in stores:
        c.wait()


def shards(
    tokens, lengths, recycle, resolved, coords, plm_embed, plm_uv, plm_qk, plm_affine, plm_out,
    w_in, w_pairin, w_tri, vecs, row_in, col_in, row_pairin, col_pairin, row_tri, col_tri, sq_vecs,
):
    heads = lax.axis_size("head")
    seq = tokens.shape[1]
    width = plm_embed.shape[1]
    units = plm_uv.shape[2]
    chans = vecs.shape[1]
    node = w_in.shape[1]
    shared_by = 2 if units % 256 == 0 else 1
    unit_part = units // shared_by
    anywhere = pl.BlockSpec(memory_space=pl.ANY)
    inside = pl.BlockSpec(memory_space=pltpu.VMEM)
    table = ROWS * ROWS

    def vm(*shape, dtype=f32):
        return pltpu.VMEM(shape, dtype)

    def like(x):
        return pltpu.VMEM(x.shape, x.dtype)

    coords = jnp.transpose(coords, (1, 0, 2))
    row_in2 = row_in.reshape(-1, chans)
    col_in2 = col_in.reshape(-1, chans)
    operands = (
        tokens, lengths, recycle, resolved, coords, plm_embed, plm_uv, plm_qk, plm_affine, plm_out,
        w_in, w_pairin, w_tri, vecs, row_in2, col_in2, row_pairin, col_pairin, row_tri, col_tri, sq_vecs,
    )
    kept = operands[10:]
    scratch = [
        like(tokens), like(resolved),
        like(coords), like(plm_embed), vm(2, width, unit_part, dtype=bf16), like(plm_qk),
        like(plm_affine), vm(shared_by, unit_part, width, dtype=bf16),
        vm(WIDE, width), vm(shared_by, ROWS, unit_part), vm(shared_by, WIDE, unit_part, dtype=bf16),
        vm(ROWS, width), vm(heads, 2, 16, width // 2 + width // 4, dtype=bf16),
        vm(width, node, dtype=bf16), vm(node, 2 * chans, dtype=bf16),
        vm(2 * chans, 6 * chans, dtype=bf16), vm(WIDE, chans), vm(seq, seq), vm(chans, seq),
        vm(table, chans), vm(table, chans), vm(table, chans), vm(table, chans),
        vm(table, chans, dtype=bf16), vm(table, 5 * chans), vm(table, chans), vm(table, chans),
        vm(table, chans), vm(table, chans), vm(table, chans), vm(table, chans), vm(table, chans),
        vm(table, chans), vm(table, chans, dtype=bf16),
        vm(table, chans), vm(table, chans), vm(table, chans, dtype=bf16), vm(table, chans),
        vm(table, chans), vm(table, 2 * chans), vm(table, 2 * chans), vm(table, 2 * chans),
        vm(table, chans), vm(table, chans), vm(table, 5 * chans, dtype=bf16),
        vm(chans, chans), vm(seq, chans, dtype=bf16),
        vm(2, 6, chans, chans), vm(6 * chans, chans, dtype=bf16), vm(6 * chans, chans),
        pltpu.SemaphoreType.DMA((19 + shared_by,)),
        pltpu.SemaphoreType.DMA((heads - 1, 2)), pltpu.SemaphoreType.DMA((heads, 2)),
        pltpu.SemaphoreType.DMA((2,)), pltpu.SemaphoreType.DMA((2,)),
        pltpu.SemaphoreType.DMA((6,)), pltpu.SemaphoreType.DMA((6,)),
    ]
    operands = tuple(
        x if x.size == 1 else pltpu.with_memory_space_constraint(x, pltpu.HBM) for x in operands
    )
    sds = jax.ShapeDtypeStruct
    n_blk = width // chans + 2 * (node // chans) + 6
    made = pl.pallas_call(
        functools.partial(tables_kernel, heads=heads, shared_by=shared_by, unit_part=unit_part),
        out_shape=(
            sds((2, WIDE, width), bf16), sds((2, WIDE, node), f32), sds((2, WIDE, 2 * chans), f32),
            sds((n_blk * chans, chans), f32), sds((16, chans), f32), sds(w_tri.shape, f32),
            sds(w_tri.shape, f32), sds(row_tri.shape, f32), sds(col_tri.shape, f32),
        )
        + tuple(sds(x.shape, x.dtype) for x in kept),
        in_specs=[
            pl.BlockSpec(memory_space=pltpu.SMEM) if x.size == 1 else anywhere for x in operands
        ],
        out_specs=[inside] * (9 + len(kept)),
        scratch_shapes=scratch,
        compiler_params=pltpu.CompilerParams(
            collective_id=0, has_side_effects=True, vmem_limit_bytes=48 << 20
        ),
        name="tables",
    )(*operands)

    operands = tuple(made)
    outs = (
        sds((1, chans), f32), sds((1, chans), f32), w_in, row_in2, col_in2, w_in, w_pairin,
        row_pairin, col_pairin, w_pairin, w_tri, row_tri, col_tri, w_tri, vecs, vecs, vecs,
    )
    outs = tuple(sds(x.shape, x.dtype) for x in outs)
    scratch = (
        [like(x) for k, x in enumerate(outs) if k not in (10, 11, 12, 13)]
        + [
            vm(4 * WIDE, node, dtype=bf16), vm(width, node, dtype=bf16),
            vm(2 * node, chans, dtype=bf16), vm(width, chans), vm(2 * node, chans),
            pltpu.SemaphoreType.DMA((17,)),
        ]
    )
    res = list(
        pl.pallas_call(
            update_kernel,
            out_shape=outs,
            in_specs=[inside] * len(operands),
            out_specs=[anywhere] * len(outs),
            scratch_shapes=scratch,
            compiler_params=pltpu.CompilerParams(vmem_limit_bytes=32 << 20),
            name="update",
        )(*operands)
    )
    res[0] = res[0][0, 0]
    res[1] = res[1][0, 0]
    res[3] = res[3].reshape(-1)
    res[4] = res[4].reshape(-1)
    return tuple(res)


def solution(mesh):
    whole = P()
    in_specs = (
        P("grp", None), P("grp"), P("grp"), P("grp", None), P("grp", None, None), whole,
        P(None, None, "head"), whole, whole, P("head", None),
    ) + (whole,) * 11
    return jax.shard_map(
        shards, mesh=mesh, in_specs=in_specs, out_specs=(whole,) * 17, check_vma=False
    )
```

```python
import functools
import math

import jax
import jax.numpy as jnp
from jax import lax
from jax.experimental import pallas as pl
from jax.experimental.pallas import tpu as pltpu
from jax.sharding import PartitionSpec as P


STEP = 10
ORDER = (0, 1, 4, 2, 3)
BETA = 1.0 - STEP ** (-0.8)
RATE = 0.3
MESH = pl.DeviceIdType.MESH
f32 = jnp.float32
bf16 = jnp.bfloat16
ROWS = 24
WIDE = 32


def dot(a, b):
    return jnp.dot(a, b, preferred_element_type=f32)


def dot_nt(a, b):
    return lax.dot_general(a, b, (((1,), (1,)), ((), ())), preferred_element_type=f32)


def dot_tn(a, b):
    return lax.dot_general(a, b, (((0,), (0,)), ((), ())), preferred_element_type=f32)


def silu(x):
    return x * jax.nn.sigmoid(x)


def mean_last(x):
    return jnp.mean(x, -1, keepdims=True)


def split(x, parts):
    out = []
    for _ in range(parts):
        part = x.astype(bf16)
        out.append(part)
        x = x - part.astype(f32)
    return out


def iota(shape, dim):
    return lax.broadcasted_iota(jnp.int32, shape, dim)


def fresh(old, total, n):
    return BETA * old + ((1.0 - BETA) / n * total + (1.0 - BETA) * 1e-30)


def fold(x):
    return jnp.sum(x.reshape(x.shape[0] // 8, 8, x.shape[1]), 0)


def adafactor(grad, weight, new, col_old, col_new, sums, old, scale):
    n_rows, n_cols = grad.shape
    chans = old.shape[1]
    blk = chans
    halves = n_cols // chans
    col_sum = [jnp.zeros((8, chans), f32)] * halves
    scaled = [jnp.zeros((8, chans), f32)] * halves
    row_sum = jnp.zeros((8, chans), f32)
    for b in range(n_rows // blk):
        s = slice(b * blk, (b + 1) * blk)
        row = old[s, :] + ((1.0 - BETA) / n_cols * sums[s, :] + (1.0 - BETA) * 1e-30)
        row_sum = row_sum + fold(row)
        root = lax.rsqrt(row)
        for h in range(halves):
            c = slice(h * chans, (h + 1) * chans)
            g = grad[s, c]
            step = g * root
            new[s, c] = step
            col_sum[h] = col_sum[h] + fold(g * g)
            scaled[h] = scaled[h] + fold(step * step)
    row_mean = jnp.sum(row_sum, 0, keepdims=True) / n_rows
    power = jnp.zeros((1, chans), f32)
    by_col = []
    for h in range(halves):
        col = fresh(col_old(h), jnp.sum(col_sum[h], 0, keepdims=True), n_rows)
        col_new(h, col)
        power = power + jnp.sum(scaled[h], 0, keepdims=True) / col
        by_col.append(lax.rsqrt(col))
    rms = jnp.sqrt(row_mean * jnp.sum(power, -1, keepdims=True) / (n_rows * n_cols))
    coef = scale * jnp.sqrt(row_mean) / jnp.maximum(1.0, rms)
    by_col = [x * coef for x in by_col]

    def second(b, carry):
        s = pl.ds(b * blk, blk)
        for h in range(halves):
            c = slice(h * chans, (h + 1) * chans)
            new[s, c] = weight[s, c] - new[s, c] * by_col[h]
        return carry

    if n_rows == blk:
        second(0, 0)
    else:
        lax.fori_loop(0, n_rows // blk, second, 0)


def tables_kernel(
    tokens_h, lengths_s, recycle_s, resolved_h, coords_h, embed_h, uv_h, qk_h, affine_h, out_h,
    w_in_h, w_pairin_h, w_tri_h, vecs_h, row_in_h, col_in_h, row_pairin_h, col_pairin_h, row_tri_h,
    col_tri_h, sq_vecs_h,
    frozen_o, single_o, tail_o, old_o, scale_o, g_tri_o, new_tri_o, row_tri_o, col_tri_o,
    w_in_v, w_pairin_v, w_tri_v, vecs_v, row_in_v, col_in_v, row_pairin_v, col_pairin_v, row_tri_v,
    col_tri_v, sq_vecs_v,
    tokens_v, resolved_v, coords_v, embed_v, uv_v, qk_v, affine_v, out_v,
    emb, item_x, gate_x, value_x, partial_v, part, w_in_b, w_pair_b, w_tri_b, cnt_b, true_d, cols,
    pair, sb, n1, s1, pnorm, proj, sig_l, sig_r, gate, left, right, upd, n2, s2, unorm,
    branch, final, dbranch, left_n, gated_b, dunorm, dpnorm, dlast, dleft, dright, upd_t, dproj,
    old_v, one_t, gtri_x, sq_tri, sum_tri,
    load_sem, part_send, part_recv, unit_send, unit_recv, peer_send, peer_recv,
    *, heads, shared_by, unit_part,
):
    grp = lax.axis_index("grp")
    head = lax.axis_index("head")
    other = 1 - grp
    turned = lax.rem(head, 2)
    item = lax.rem(grp + head, 2)

    def partner(d):
        peer = lax.rem(head + d, heads)
        return {"grp": lax.rem(item + peer, 2), "head": peer}

    seq = tokens_v.shape[1]
    width = emb.shape[1]
    chans = vecs_v.shape[1]
    vocab = embed_v.shape[0]
    half = width // 2
    quarter = width // 4

    loads = []

    def load(src, dst):
        copy = pltpu.make_async_copy(src, dst, load_sem.at[len(loads)])
        loads.append(copy)
        copy.start()
        return copy

    c_small = [
        load(embed_h, embed_v),
        load(tokens_h, tokens_v),
        load(resolved_h, resolved_v),
        load(coords_h, coords_v),
        load(affine_h, affine_v),
    ]
    mine = grp if shared_by == 2 else 0
    at_mine = pl.multiple_of(mine * unit_part, 128)
    c_gate = load(uv_h.at[0, :, pl.ds(at_mine, unit_part)], uv_v.at[0])
    c_value = load(uv_h.at[1, :, pl.ds(at_mine, unit_part)], uv_v.at[1])
    c_qk = load(qk_h, qk_v)
    c_out = []
    for k in range(shared_by):
        at = pl.multiple_of(lax.rem(mine + k, shared_by) * unit_part, 128)
        c_out.append(load(out_h.at[pl.ds(at, unit_part)], out_v.at[k]))
    c_par = [
        load(w_in_h, w_in_v),
        load(w_pairin_h, w_pairin_v),
        load(w_tri_h, w_tri_v),
        load(vecs_h, vecs_v),
        load(row_in_h, row_in_v),
        load(row_pairin_h, row_pairin_v),
        load(row_tri_h, row_tri_v),
        load(col_in_h, col_in_v),
        load(col_pairin_h, col_pairin_v),
        load(col_tri_h, col_tri_v),
        load(sq_vecs_h, sq_vecs_v),
    ]

    barrier = pltpu.get_barrier_semaphore()
    pl.semaphore_signal(barrier, inc=1, device_id={"grp": other}, device_id_type=MESH)
    for d in range(1, heads):
        pl.semaphore_signal(barrier, inc=1, device_id=partner(d), device_id_type=MESH)

    for c in c_small:
        c.wait()
    emb[...] = jnp.zeros_like(emb)
    emb[0:vocab, :] = embed_v[...].astype(f32)
    e = emb[...]
    centre = e - mean_last(e)
    normed = (centre * lax.rsqrt(mean_last(centre * centre) + 1e-05)).astype(bf16)

    key_ok = (iota((1, seq), 1) < lengths_s[0]).astype(f32)
    for k in range(3):
        item_x[0, k : k + 1, :] = coords_v[k]
    item_x[0, 3:4, :] = key_ok * (resolved_v[...] > 0).astype(f32)
    item_x[0, 4:5, :] = tokens_v[...].astype(f32)
    item_x[0, 5:6, :] = key_ok
    item_x[0, 6:8, :] = jnp.broadcast_to(recycle_s[0].astype(f32), (2, seq))
    pl.semaphore_wait(barrier, heads)
    unit_sends = []

    def swap(ref, k):
        copy = pltpu.make_async_remote_copy(
            src_ref=ref.at[0],
            dst_ref=ref.at[1],
            send_sem=unit_send.at[k],
            recv_sem=unit_recv.at[k],
            device_id={"grp": other},
            device_id_type=MESH,
        )
        copy.start()
        unit_sends.append(copy)
        return copy

    c_item = swap(item_x, 2)

    c_gate.wait()
    ugate = silu(dot(normed, uv_v[0]))
    gate_x[0] = ugate[0:ROWS]
    if shared_by == 2:
        swap(gate_x, 0)
    c_value.wait()
    value_x[0] = silu(dot(normed, uv_v[1])).astype(bf16)
    if shared_by == 2:
        swap(value_x, 1)

    c_item.wait_recv()
    cols[0:8, :] = jnp.where(turned > 0, item_x[1], item_x[0])
    valid = cols[3:4, :]
    key_ok = cols[5:6, :]
    recycle = cols[6:7, 0:1]
    onehot = (iota((WIDE, seq), 0) == cols[4:5, :].astype(jnp.int32)).astype(f32)
    one_b = onehot.astype(bf16)
    cnt_col = jnp.sum(onehot, -1, keepdims=True)
    cnt_b[...] = jnp.broadcast_to(cnt_col, (WIDE, chans))
    ones = jnp.ones((16, seq), bf16)
    cnt_row = dot_nt(ones, one_b)[0:1, :]
    key_row = dot_nt(ones, (onehot * key_ok).astype(bf16))[0:1, :]

    c_qk.wait()
    shared = silu(dot(normed, qk_v[...]))
    query = (shared * affine_v[0:1, :] + affine_v[1:2, :]).astype(bf16)
    keyed = (shared * affine_v[2:3, :] + affine_v[3:4, :]).astype(bf16)
    scores = dot_nt(query, keyed) / math.sqrt(qk_v.shape[1])
    masked = jnp.where(key_row > 0, scores, -1000000000.0)
    top = jnp.exp(masked - jnp.max(masked, -1, keepdims=True))
    attn = (top / jnp.sum(top * key_row, -1, keepdims=True)).astype(bf16).astype(f32)
    attn = jnp.concatenate(split(attn * key_row, 2), 0)

    def mix(k):
        seen = dot(attn, value_x[k])
        seen = seen[0:ROWS] + seen[WIDE : WIDE + ROWS]
        return (gate_x[k] * seen).astype(bf16)

    mixed = mix(0)
    c_out[0].wait()
    if shared_by == 2:
        partial_v[...] = dot(mixed, out_v[0])
        for c in unit_sends[1:]:
            c.wait_recv()
        mixed = mix(1)
        c_out[1].wait()
    sends = []
    for n in range(2):
        s = slice(n * half, (n + 1) * half)
        p = dot(mixed, out_v[shared_by - 1, :, s])
        if shared_by == 2:
            p = p + partial_v[:, s]
        part[head, n, :, 0:half] = p[0:16].astype(bf16)
        part[head, n, :, half : half + quarter] = jnp.concatenate(
            [p[16:24, 0:quarter], p[16:24, quarter:half]], 0
        ).astype(bf16)
        for d in range(1, heads):
            copy = pltpu.make_async_remote_copy(
                src_ref=part.at[head, n],
                dst_ref=part.at[head, n],
                send_sem=part_send.at[d - 1, n],
                recv_sem=part_recv.at[head, n],
                device_id=partner(d),
                device_id_type=MESH,
            )
            copy.start()
            sends.append(copy)

    for c in c_par:
        c.wait()
    w_in_b[...] = w_in_v[...].astype(bf16)
    for k in range(2):
        w_pair_b[:, k * chans : (k + 1) * chans] = w_pairin_v[k].astype(bf16)
    v0 = vecs_v[0:1, :]
    v1 = vecs_v[1:2, :]
    v2 = vecs_v[2:3, :]
    v3 = vecs_v[3:4, :]
    gain_one = vecs_v[...].T[:, 1:2]
    gain_two = vecs_v[...].T[:, 2:3]
    for k, m in enumerate(ORDER + (5,)):
        c = slice(k * chans, (k + 1) * chans)
        w = w_tri_v[m].astype(bf16)
        w_tri_b[0:chans, c] = w
        w = w.astype(f32) * (gain_two if m == 5 else gain_one)
        w = jnp.sum(w, 0, keepdims=True) * (1.0 / chans)
        w_tri_b[chans : 2 * chans, c] = jnp.broadcast_to(w, (chans, chans)).astype(bf16)
    cols[8:chans, :] = jnp.zeros((chans - 8, seq), f32)
    one_v = (onehot * valid).astype(bf16)
    weight_j = recycle * valid
    blk = 128
    n_blk = seq // blk
    places = []
    for b in range(n_blk):
        t = cols[:, b * blk : (b + 1) * blk].T
        hot = lax.bitwise_and(iota((blk, chans), 1), WIDE - 1) == t[:, 4:5].astype(jnp.int32)
        hot = hot & (iota((blk, chans), 1) < 3 * WIDE)
        one_t[b * blk : (b + 1) * blk, :] = hot.astype(f32).astype(bf16)
        places.append(t)
        d2 = None
        for k in range(3):
            delta = t[:, k : k + 1] - cols[k : k + 1, :]
            d2 = delta * delta if d2 is None else d2 + delta * delta
        true_d[b * blk : (b + 1) * blk, :] = jnp.sqrt(d2)
    n_valid = jnp.sum(valid, -1, keepdims=True)
    loss_count = recycle * n_valid * n_valid

    present = cnt_b[0:ROWS, :] > 0
    sc = jnp.where((cnt_row > 0) & (cnt_col > 0), scores, 0.0)[0:ROWS]

    n_chunk = ROWS // 2
    two = 2 * ROWS

    def rows(k):
        return slice(k * two, (k + 1) * two)

    def both(f, k):
        return jnp.concatenate([f(2 * k), f(2 * k + 1)], 0)

    v0c = v0 - mean_last(v0)
    for k in range(n_chunk):
        r = rows(k)
        sbk = both(lambda u: jnp.broadcast_to(sc[:, u : u + 1], (ROWS, chans)), k)
        sb[r] = sbk
        pair[r] = sbk * v0
        n1[r] = sbk * v0c
    lane = iota((ROWS, chans), 1)
    score_logit = jnp.sum(v0 * v3, -1, keepdims=True) * jnp.concatenate(
        [sc, jnp.zeros((ROWS, chans - WIDE), f32)], 1
    )

    n_in = width // chans
    n_pr = w_pairin_v.shape[1] // chans
    at_tri = n_in + 2 * n_pr
    old_v[...] = jnp.zeros_like(old_v)
    old_v[0:n_in, :] = row_in_v[...]
    for k in range(2):
        for b in range(n_pr):
            j = n_in + k * n_pr + b
            old_v[j : j + 1, :] = row_pairin_v[k : k + 1, b * chans : (b + 1) * chans]
    old_v[at_tri : at_tri + 6, :] = row_tri_v[...]
    old = BETA * old_v[...].T
    for k in range(at_tri + 6):
        old_o[k * chans : (k + 1) * chans, :] = jnp.broadcast_to(old[:, k : k + 1], (chans, chans))
    scale_o[...] = jnp.zeros_like(scale_o)
    mats = [w_in_v] + [w_pairin_v.at[k] for k in range(2)] + [w_tri_v.at[m] for m in range(6)]
    for k, w in enumerate(mats):
        x = w[...]
        x = jnp.sum(jnp.sum(x * x, 0, keepdims=True), -1, keepdims=True) / (w.shape[0] * w.shape[1])
        x = RATE * jnp.maximum(0.001, jnp.sqrt(x))
        scale_o[k : k + 1, :] = jnp.broadcast_to(x, (1, chans))

    for n in range(2):
        for d in range(1, heads):
            peer = lax.rem(head + d, heads)
            pltpu.make_async_remote_copy(
                src_ref=part.at[peer, n],
                dst_ref=part.at[peer, n],
                send_sem=part_send.at[d - 1, n],
                recv_sem=part_recv.at[peer, n],
                device_id=partner(d),
                device_id_type=MESH,
            ).wait_recv()
    for n in range(2):
        s = slice(n * half, (n + 1) * half)
        low = None
        for k in range(heads):
            a = part[k, n, :, 0:half].astype(f32)
            b = part[k, n, :, half : half + quarter].astype(f32)
            b = jnp.concatenate([b[0:8], b[8:16]], 1)
            low = [a, b] if low is None else [low[0] + a, low[1] + b]
        emb[0:16, s] += low[0]
        emb[16:24, s] += low[1]
    state = emb[0:ROWS, :]
    centre = state - mean_last(state)
    frozen = centre * lax.rsqrt(mean_last(centre * centre) + 1e-05)
    frozen = jnp.concatenate([frozen, jnp.zeros((WIDE - ROWS, width), f32)], 0).astype(bf16)
    frozen_o[item] = frozen

    peers = []

    def give(ref):
        k = len(peers)
        copy = pltpu.make_async_remote_copy(
            src_ref=ref,
            dst_ref=ref,
            send_sem=peer_send.at[k],
            recv_sem=peer_recv.at[k],
            device_id={"grp": other},
            device_id_type=MESH,
        )
        copy.start()
        peers.append(copy)
        return copy

    give(frozen_o.at[item])
    single = dot(frozen, w_in_b[...]).astype(bf16)
    single_o[item] = jnp.concatenate(
        [single[0:ROWS].astype(f32), jnp.broadcast_to(loss_count, (8, single.shape[1]))], 0
    )
    c_single = give(single_o.at[item])
    side = dot(single, w_pair_b[...])[0:ROWS]
    side_a = jnp.where(present, side[:, 0:chans], 0.0)
    side_b = jnp.where(present, side[:, chans : 2 * chans], 0.0)
    side_ac = side_a - mean_last(side_a)
    side_bc = side_b - mean_last(side_b)

    own = iota((ROWS, chans), 0) == lane
    logit_b = jnp.sum(
        jnp.where(own, jnp.sum(side_b * v3, -1, keepdims=True), 0.0), 0, keepdims=True
    )
    logit = score_logit + jnp.sum(side_a * v3, -1, keepdims=True) + logit_b
    for k in range(n_chunk):
        r = rows(k)
        pair[r] = pair[r] + both(lambda u: side_a + side_b[u : u + 1, :], k)
        centre = n1[r] + both(lambda u: side_ac + side_bc[u : u + 1, :], k)
        scale = lax.rsqrt(mean_last(centre * centre) + 1e-05)
        normal = centre * scale
        n1[r] = normal
        s1[r] = jnp.broadcast_to(scale, (two, chans))
        pnorm[r] = (normal * v1).astype(bf16)
    proj[...] = dot(pnorm[...], w_tri_b[0:chans, 0 : 5 * chans])
    for k in range(n_chunk):
        r = rows(k)
        sl = jax.nn.sigmoid(proj[r, chans : 2 * chans])
        sr = jax.nn.sigmoid(proj[r, 4 * chans : 5 * chans])
        sig_l[r] = sl
        sig_r[r] = sr
        left[r] = (sl * proj[r, 0:chans]).astype(bf16).astype(f32)
        right[r] = (sr * proj[r, 3 * chans : 4 * chans]).astype(bf16).astype(f32)
        gate[r] = jax.nn.sigmoid(proj[r, 2 * chans : 3 * chans])
        left_n[r] = left[r] * both(
            lambda u: jnp.broadcast_to(cnt_b[u : u + 1, :], (ROWS, chans)), k
        )

    def triangle(dst, moving, fixed, row_of, weighted):
        group = 4
        for a0 in range(0, ROWS, group):
            total = [None] * group
            for b in range(vocab):
                x = moving(b)
                for q in range(group):
                    y = x * fixed[pl.ds(row_of(a0 + q, b), 1), :]
                    total[q] = y if total[q] is None else total[q] + y
            for q in range(group):
                a = a0 + q
                t = total[q]
                if weighted:
                    t = t * cnt_b[a : a + 1, :]
                dst[a * ROWS : (a + 1) * ROWS, :] = t

    triangle(
        upd, lambda u: left_n[u * ROWS : (u + 1) * ROWS, :], right, lambda v, u: u * ROWS + v, False
    )
    for k in range(n_chunk):
        r = rows(k)
        x = upd[r]
        centre = x - mean_last(x)
        scale = lax.rsqrt(mean_last(centre * centre) + 1e-05)
        normal = centre * scale
        n2[r] = normal
        s2[r] = jnp.broadcast_to(scale, (two, chans))
        unorm[r] = (normal * v2).astype(bf16)
    branch[...] = dot(unorm[...], w_tri_b[0:chans, 5 * chans : 6 * chans])
    gated = jnp.zeros((ROWS, chans), f32)
    for k in range(n_chunk):
        r = rows(k)
        move = gate[r] * branch[r]
        final[r] = pair[r] + move
        col = jnp.sum(move * v3, -1, keepdims=True)
        gated_b[r] = jnp.broadcast_to(col, (two, chans))
        for q in range(2):
            gated = jnp.where(lane == 2 * k + q, col[q * ROWS : (q + 1) * ROWS], gated)
    logit = logit + gated

    dist = jnp.maximum(logit, 0.0) + jnp.log(1.0 + jnp.exp(-jnp.abs(logit)))
    dist = jnp.concatenate([dist, jnp.zeros((WIDE - ROWS, chans), f32)], 0)
    dist = jnp.concatenate(split(dist, 3), 0)
    by_col = dot(dist[:, 0:WIDE], one_b).astype(bf16)
    for k in range(n_chunk):
        r = rows(k)
        sl, sr, gt = sig_l[r], sig_r[r], gate[r]
        proj[r, 0:chans] = proj[r, 0:chans] * sl * (1.0 - sl)
        proj[r, 3 * chans : 4 * chans] = proj[r, 3 * chans : 4 * chans] * sr * (1.0 - sr)
        gt3 = gt * v3
        proj[r, 2 * chans : 3 * chans] = gt3 * (1.0 - gt) * branch[r]
        gate[r] = gt3
    loss_row = jnp.zeros((1, seq), f32)
    by_first = jnp.zeros((WIDE, seq), f32)
    for b in range(n_blk):
        s = slice(b * blk, (b + 1) * blk)
        diff = dot(one_t[s, 0 : 3 * WIDE], by_col) - true_d[s, :]
        sq = diff * diff + 1.0
        inv = lax.rsqrt(sq)
        loss_row = loss_row + jnp.sum(
            places[b][:, 3:4] * (sq * inv - 1.0), 0, keepdims=True
        )
        by_first = by_first + dot(one_v[:, s], (diff * inv).astype(bf16))
    loss = jnp.sum(loss_row * weight_j, -1, keepdims=True)
    by_pair = dot_nt(jnp.concatenate(split(by_first * weight_j, 2), 0), one_b)
    by_pair = (by_pair[0:WIDE] + by_pair[WIDE : 2 * WIDE])[0:ROWS]
    dlogit = by_pair * jax.nn.sigmoid(logit)[:, 0:WIDE]

    g_dist = jnp.zeros((two, chans), f32)
    for k in range(n_chunk):
        r = rows(k)
        g = both(lambda u: jnp.broadcast_to(dlogit[:, u : u + 1], (ROWS, chans)), k)
        g_dist = g_dist + g * final[r]
        dfinal = g * v3
        pair[r] = dfinal
        dbranch[r] = (g * gate[r]).astype(bf16)
        dproj[r, 2 * chans : 3 * chans] = (g * proj[r, 2 * chans : 3 * chans]).astype(bf16)
        gated_b[r] = g * gated_b[r] * (1.0 / chans)
    dunorm[...] = dot_nt(dbranch[...], w_tri_b[:, 5 * chans : 6 * chans])
    gtri_x[item, 5] = dot_tn(unorm[...], dbranch[...])
    gtri_x[item, 4] = dot_tn(pnorm[...], dproj[:, 2 * chans : 3 * chans])
    c_pair = [give(gtri_x.at[item, pl.ds(4, 2)])]
    g_two = jnp.zeros((two, chans), f32)
    for k in range(n_chunk):
        r = rows(k)
        dn = dunorm[r, 0:chans]
        normal = n2[r]
        g_two = g_two + dn * normal
        upd[r] = s2[r] * (dn * v2 - dunorm[r, chans : 2 * chans] - normal * gated_b[r])
    triangle(
        dleft, lambda v: upd[v * ROWS : (v + 1) * ROWS, :], right, lambda u, v: u * ROWS + v, True
    )
    for k in range(n_chunk):
        r = rows(k)
        d, sl = dleft[r], sig_l[r]
        dproj[r, 0:chans] = (d * sl).astype(bf16)
        dproj[r, chans : 2 * chans] = (d * proj[r, 0:chans]).astype(bf16)
    dpnorm[...] = dot_nt(dproj[:, 0 : 3 * chans], w_tri_b[:, 0 : 3 * chans])
    g = dot_tn(pnorm[...], dproj[:, 0 : 2 * chans])
    gtri_x[item, 0] = g[:, 0:chans]
    gtri_x[item, 1] = g[:, chans : 2 * chans]
    c_pair.append(give(gtri_x.at[item, pl.ds(0, 2)]))
    for t in range(vocab):
        upd_t[t * ROWS : (t + 1) * ROWS, :] = upd[pl.ds(t, ROWS, stride=ROWS), :]
    triangle(
        dright, lambda t: upd_t[t * ROWS : (t + 1) * ROWS, :], left, lambda u, t: u * ROWS + t, True
    )
    for k in range(n_chunk):
        r = rows(k)
        d, sr = dright[r], sig_r[r]
        dproj[r, 3 * chans : 4 * chans] = (d * sr).astype(bf16)
        dproj[r, 4 * chans : 5 * chans] = (d * proj[r, 3 * chans : 4 * chans]).astype(bf16)
    dlast[...] = dot_nt(dproj[:, 3 * chans : 5 * chans], w_tri_b[:, 3 * chans : 5 * chans])
    g = dot_tn(pnorm[...], dproj[:, 3 * chans : 5 * chans])
    gtri_x[item, 2] = g[:, 0:chans]
    gtri_x[item, 3] = g[:, chans : 2 * chans]
    c_pair.append(give(gtri_x.at[item, pl.ds(2, 2)]))
    g_one = jnp.zeros((two, chans), f32)
    g_score = jnp.zeros((two, chans), f32)
    d_a = jnp.zeros((ROWS, chans), f32)
    tail_o[item] = jnp.zeros((WIDE, 2 * chans), f32)
    for k in range(n_chunk):
        r = rows(k)
        dn = dpnorm[r, 0:chans] + dlast[r, 0:chans]
        mean = dpnorm[r, chans : 2 * chans] + dlast[r, chans : 2 * chans]
        normal = n1[r]
        along = dn * normal
        g_one = g_one + along
        dpair = pair[r] + s1[r] * (dn * v1 - mean - normal * mean_last(along * v1))
        g_score = g_score + sb[r] * dpair
        d_a = d_a + dpair[0:ROWS] + dpair[ROWS:two]
        for q in range(2):
            tail_o[item, 2 * k + q : 2 * k + q + 1, chans : 2 * chans] = jnp.sum(
                dpair[q * ROWS : (q + 1) * ROWS], 0, keepdims=True
            )
    tail_o[item, 0:ROWS, 0:chans] = d_a
    for k, g in enumerate((g_score, g_one, g_two, g_dist)):
        tail_o[item, ROWS + k : ROWS + k + 1, 0:chans] = jnp.sum(g, 0, keepdims=True)
    tail_o[item, ROWS + 4 : ROWS + 5, 0:chans] = jnp.broadcast_to(loss, (1, chans))
    tail_o[item, ROWS + 5 : ROWS + 6, 0:chans] = jnp.broadcast_to(loss_count, (1, chans))
    c_tail = give(tail_o.at[item])

    c_single.wait_recv()
    inv = 1.0 / (
        single_o[0, ROWS : ROWS + 1, 0:chans] + single_o[1, ROWS : ROWS + 1, 0:chans]
    )
    for pairs in ((0, 1), (2,)):
        mats = []
        for k in pairs:
            c_pair[k].wait_recv()
            first = (4, 0, 2)[k]
            mats += [first, first + 1]
        for m in mats:
            g = (gtri_x[0, m] + gtri_x[1, m]) * inv
            g_tri_o[m] = g
            sq_tri[m * chans : (m + 1) * chans, :] = (g * g).astype(bf16)
        for m in mats:
            r = slice(m * chans, (m + 1) * chans)
            sum_tri[r, :] = dot(sq_tri[r, :], jnp.ones((chans, chans), bf16))
        for m in mats:
            total = sum_tri[m * chans : (m + 1) * chans, :].T[0:1, :]
            row_tri_o[m : m + 1, :] = fresh(row_tri_v[m : m + 1, :], total, chans)

            def put_col(h, col, m=m):
                col_tri_o[m : m + 1, :] = col

            adafactor(
                g_tri_o.at[m], w_tri_v.at[m], new_tri_o.at[m],
                lambda h, m=m: col_tri_v[m : m + 1, :], put_col,
                sum_tri.at[pl.ds(m * chans, chans)],
                old_o.at[pl.ds((at_tri + m) * chans, chans)],
                scale_o[3 + m : 4 + m, :],
            )

    for c in sends + unit_sends + peers:
        c.wait_send()
    for c in peers:
        if c is not c_single and all(c is not x for x in c_pair):
            c.wait_recv()


def update_kernel(
    frozen_v, single_v, tail_v, old_v, scale_v, g_tri, new_tri, row_tri_n, col_tri_n,
    w_in_v, w_pairin_v, w_tri_v, vecs_v,
    row_in_v, col_in_v, row_pairin_v, col_pairin_v, row_tri_v, col_tri_v, sq_vecs_v,
    loss_o, count_o, g_in_o, row_in_o, col_in_o, new_in_o, g_pairin_o, row_pairin_o, col_pairin_o,
    new_pairin_o, g_tri_o, row_tri_o, col_tri_o, new_tri_o, g_vecs_o, sq_vecs_o, new_vecs_o,
    loss_s, count_s, g_in, row_in_n, col_in_n, new_in, g_pairin, row_pairin_n, col_pairin_n,
    new_pairin, g_vecs, sq_vecs_n, new_vecs,
    ds_v, sq_in, sq_rest, sum_in, sum_rest, store_sem,
):
    chans = vecs_v.shape[1]
    width, node = w_in_v.shape
    stores = []

    def store(src, dst):
        copy = pltpu.make_async_copy(src, dst, store_sem.at[len(stores)])
        stores.append(copy)
        copy.start()

    store(g_tri, g_tri_o)
    store(new_tri, new_tri_o)
    store(row_tri_n, row_tri_o)
    store(col_tri_n, col_tri_o)
    totals = tail_v[0, ROWS : ROWS + 8, 0:chans] + tail_v[1, ROWS : ROWS + 8, 0:chans]
    inv = 1.0 / totals[5:6, :]
    inv2 = jnp.concatenate([inv, inv], 1)
    d_side = [tail_v[i, 0:ROWS, :] * inv2 for i in range(2)]

    pads = jnp.zeros((WIDE - ROWS, node), f32)
    side_parts = []
    for i in range(2):
        parts = split(d_side[i], 2)
        side_parts.append(parts)
        st = jnp.concatenate([p.astype(f32) for p in parts], 0).astype(bf16)
        ds = dot_nt(st[:, 0:chans], w_pairin_v[0].astype(bf16)) + dot_nt(
            st[:, chans : 2 * chans], w_pairin_v[1].astype(bf16)
        )
        ds = ds[0:ROWS] + ds[ROWS : 2 * ROWS]
        for k, p in enumerate(split(ds, 2)):
            at = (2 * k + i) * WIDE
            ds_v[at : at + WIDE, :] = jnp.concatenate([p.astype(f32), pads], 0).astype(bf16)
    fz = jnp.concatenate([frozen_v[0], frozen_v[1], frozen_v[0], frozen_v[1]], 0)
    g_in[...] = dot_tn(fz, ds_v[...])
    store(g_in, g_in_o)

    sg = [single_v[i, 0:ROWS] for i in range(2)]
    sg = jnp.concatenate(sg + sg, 0).astype(bf16)
    st = jnp.concatenate(
        [side_parts[i][k].astype(f32) for k in range(2) for i in range(2)], 0
    ).astype(bf16)
    for k in range(2):
        g_pairin[k] = dot_tn(sg, st[:, k * chans : (k + 1) * chans])
    store(g_pairin, g_pairin_o)
    loss_s[...] = totals[4:5, :]
    count_s[...] = totals[5:6, :]
    g_vecs[...] = totals[0:4, :] * inv
    store(loss_s, loss_o)
    store(count_s, count_o)
    store(g_vecs, g_vecs_o)

    blk = chans
    n_in = width // blk
    n_pr = w_pairin_v.shape[1] // blk
    for b in range(n_in):
        g = g_in[b * blk : (b + 1) * blk, :]
        sq_in[b * blk : (b + 1) * blk, :] = (g * g).astype(bf16)
    for k in range(2):
        for b in range(n_pr):
            g = g_pairin[k, b * blk : (b + 1) * blk, :]
            j = k * n_pr + b
            sq_rest[j * blk : (j + 1) * blk, :] = (g * g).astype(bf16)
    sum_in[...] = dot(sq_in[...], jnp.ones((node, chans), bf16))
    sum_rest[...] = dot(sq_rest[...], jnp.ones((chans, chans), bf16))
    for b in range(n_in):
        total = sum_in[b * blk : (b + 1) * blk, :].T[0:1, :]
        row_in_n[b : b + 1, :] = fresh(row_in_v[b : b + 1, :], total, node)
    for k in range(2):
        for b in range(n_pr):
            j = k * n_pr + b
            total = sum_rest[j * blk : (j + 1) * blk, :].T[0:1, :]
            c = slice(b * blk, (b + 1) * blk)
            row_pairin_n[k : k + 1, c] = fresh(row_pairin_v[k : k + 1, c], total, chans)
    store(row_in_n, row_in_o)
    store(row_pairin_n, row_pairin_o)

    def put(ref, k):
        def put_col(h, col):
            at = k if k is not None else h
            ref[at : at + 1, :] = col

        return put_col

    adafactor(
        g_in, w_in_v, new_in, lambda h: col_in_v[h : h + 1, :], put(col_in_n, None), sum_in,
        old_v.at[pl.ds(0, width)], scale_v[0:1, :],
    )
    store(new_in, new_in_o)
    store(col_in_n, col_in_o)
    for k in range(2):
        adafactor(
            g_pairin.at[k], w_pairin_v.at[k], new_pairin.at[k],
            lambda h, k=k: col_pairin_v[k : k + 1, :], put(col_pairin_n, k),
            sum_rest.at[pl.ds(k * n_pr * blk, n_pr * blk)],
            old_v.at[pl.ds((n_in + k * n_pr) * blk, n_pr * blk)], scale_v[1 + k : 2 + k, :],
        )
    store(new_pairin, new_pairin_o)
    store(col_pairin_n, col_pairin_o)

    g = g_vecs[...]
    sq = BETA * sq_vecs_v[...] + (1.0 - BETA) * (g * g + 1e-30)
    sq_vecs_n[...] = sq
    step = g * lax.rsqrt(sq)
    step = step / jnp.maximum(1.0, jnp.sqrt(mean_last(step * step)))
    v = vecs_v[...]
    scale = jnp.maximum(0.001, jnp.sqrt(mean_last(v * v)))
    new_vecs[...] = v - RATE * scale * step
    store(sq_vecs_n, sq_vecs_o)
    store(new_vecs, new_vecs_o)
    for c in stores:
        c.wait()


def shards(
    tokens, lengths, recycle, resolved, coords, plm_embed, plm_uv, plm_qk, plm_affine, plm_out,
    w_in, w_pairin, w_tri, vecs, row_in, col_in, row_pairin, col_pairin, row_tri, col_tri, sq_vecs,
):
    heads = lax.axis_size("head")
    seq = tokens.shape[1]
    width = plm_embed.shape[1]
    units = plm_uv.shape[2]
    chans = vecs.shape[1]
    node = w_in.shape[1]
    shared_by = 2 if units % 256 == 0 else 1
    unit_part = units // shared_by
    anywhere = pl.BlockSpec(memory_space=pl.ANY)
    inside = pl.BlockSpec(memory_space=pltpu.VMEM)
    table = ROWS * ROWS

    def vm(*shape, dtype=f32):
        return pltpu.VMEM(shape, dtype)

    def like(x):
        return pltpu.VMEM(x.shape, x.dtype)

    coords = jnp.transpose(coords, (1, 0, 2))
    row_in2 = row_in.reshape(-1, chans)
    col_in2 = col_in.reshape(-1, chans)
    operands = (
        tokens, lengths, recycle, resolved, coords, plm_embed, plm_uv, plm_qk, plm_affine, plm_out,
        w_in, w_pairin, w_tri, vecs, row_in2, col_in2, row_pairin, col_pairin, row_tri, col_tri, sq_vecs,
    )
    kept = operands[10:]
    scratch = [
        like(tokens), like(resolved),
        like(coords), like(plm_embed), vm(2, width, unit_part, dtype=bf16), like(plm_qk),
        like(plm_affine), vm(shared_by, unit_part, width, dtype=bf16),
        vm(WIDE, width), vm(2, 8, seq), vm(shared_by, ROWS, unit_part), vm(shared_by, WIDE, unit_part, dtype=bf16),
        vm(ROWS, width), vm(heads, 2, 16, width // 2 + width // 4, dtype=bf16),
        vm(width, node, dtype=bf16), vm(node, 2 * chans, dtype=bf16),
        vm(2 * chans, 6 * chans, dtype=bf16), vm(WIDE, chans), vm(seq, seq), vm(chans, seq),
        vm(table, chans), vm(table, chans), vm(table, chans), vm(table, chans),
        vm(table, chans, dtype=bf16), vm(table, 5 * chans), vm(table, chans), vm(table, chans),
        vm(table, chans), vm(table, chans), vm(table, chans), vm(table, chans), vm(table, chans),
        vm(table, chans), vm(table, chans, dtype=bf16),
        vm(table, chans), vm(table, chans), vm(table, chans, dtype=bf16), vm(table, chans),
        vm(table, chans), vm(table, 2 * chans), vm(table, 2 * chans), vm(table, 2 * chans),
        vm(table, chans), vm(table, chans), vm(table, chans), vm(table, 5 * chans, dtype=bf16),
        vm(chans, chans), vm(seq, chans, dtype=bf16),
        vm(2, 6, chans, chans), vm(6 * chans, chans, dtype=bf16), vm(6 * chans, chans),
        pltpu.SemaphoreType.DMA((19 + shared_by,)),
        pltpu.SemaphoreType.DMA((heads - 1, 2)), pltpu.SemaphoreType.DMA((heads, 2)),
        pltpu.SemaphoreType.DMA((3,)), pltpu.SemaphoreType.DMA((3,)),
        pltpu.SemaphoreType.DMA((6,)), pltpu.SemaphoreType.DMA((6,)),
    ]
    operands = tuple(
        x if x.size == 1 else pltpu.with_memory_space_constraint(x, pltpu.HBM) for x in operands
    )
    sds = jax.ShapeDtypeStruct
    n_blk = width // chans + 2 * (node // chans) + 6
    made = pl.pallas_call(
        functools.partial(tables_kernel, heads=heads, shared_by=shared_by, unit_part=unit_part),
        out_shape=(
            sds((2, WIDE, width), bf16), sds((2, WIDE, node), f32), sds((2, WIDE, 2 * chans), f32),
            sds((n_blk * chans, chans), f32), sds((16, chans), f32), sds(w_tri.shape, f32),
            sds(w_tri.shape, f32), sds(row_tri.shape, f32), sds(col_tri.shape, f32),
        )
        + tuple(sds(x.shape, x.dtype) for x in kept),
        in_specs=[
            pl.BlockSpec(memory_space=pltpu.SMEM) if x.size == 1 else anywhere for x in operands
        ],
        out_specs=[inside] * (9 + len(kept)),
        scratch_shapes=scratch,
        compiler_params=pltpu.CompilerParams(
            collective_id=0, has_side_effects=True, vmem_limit_bytes=48 << 20
        ),
        name="tables",
    )(*operands)

    operands = tuple(made)
    outs = (
        sds((1, chans), f32), sds((1, chans), f32), w_in, row_in2, col_in2, w_in, w_pairin,
        row_pairin, col_pairin, w_pairin, w_tri, row_tri, col_tri, w_tri, vecs, vecs, vecs,
    )
    outs = tuple(sds(x.shape, x.dtype) for x in outs)
    scratch = (
        [like(x) for k, x in enumerate(outs) if k not in (10, 11, 12, 13)]
        + [
            vm(4 * WIDE, node, dtype=bf16), vm(width, node, dtype=bf16),
            vm(2 * node, chans, dtype=bf16), vm(width, chans), vm(2 * node, chans),
            pltpu.SemaphoreType.DMA((17,)),
        ]
    )
    res = list(
        pl.pallas_call(
            update_kernel,
            out_shape=outs,
            in_specs=[inside] * len(operands),
            out_specs=[anywhere] * len(outs),
            scratch_shapes=scratch,
            compiler_params=pltpu.CompilerParams(vmem_limit_bytes=32 << 20),
            name="update",
        )(*operands)
    )
    res[0] = res[0][0, 0]
    res[1] = res[1][0, 0]
    res[3] = res[3].reshape(-1)
    res[4] = res[4].reshape(-1)
    return tuple(res)


def solution(mesh):
    whole = P()
    in_specs = (
        P("grp", None), P("grp"), P("grp"), P("grp", None), P("grp", None, None), whole,
        P(None, None, "head"), whole, whole, P("head", None),
    ) + (whole,) * 11
    return jax.shard_map(
        shards, mesh=mesh, in_specs=in_specs, out_specs=(whole,) * 17, check_vma=False
    )
```

```python
import functools
import math

import jax
import jax.numpy as jnp
from jax import lax
from jax.experimental import pallas as pl
from jax.experimental.pallas import tpu as pltpu
from jax.sharding import PartitionSpec as P


STEP = 10
ORDER = (0, 1, 4, 2, 3)
BETA = 1.0 - STEP ** (-0.8)
RATE = 0.3
MESH = pl.DeviceIdType.MESH
f32 = jnp.float32
bf16 = jnp.bfloat16
ROWS = 24
WIDE = 32


def dot(a, b):
    return jnp.dot(a, b, preferred_element_type=f32)


def dot_nt(a, b):
    return lax.dot_general(a, b, (((1,), (1,)), ((), ())), preferred_element_type=f32)


def dot_tn(a, b):
    return lax.dot_general(a, b, (((0,), (0,)), ((), ())), preferred_element_type=f32)


def sigmoid(x):
    return 0.5 * jnp.tanh(0.5 * x) + 0.5


def silu(x):
    return x * sigmoid(x)


def mean_last(x):
    return jnp.mean(x, -1, keepdims=True)


def split(x, parts):
    out = []
    for _ in range(parts):
        part = x.astype(bf16)
        out.append(part)
        x = x - part.astype(f32)
    return out


def iota(shape, dim):
    return lax.broadcasted_iota(jnp.int32, shape, dim)


def fresh(old, total, n):
    return BETA * old + ((1.0 - BETA) / n * total + (1.0 - BETA) * 1e-30)


def fold(x):
    return jnp.sum(x.reshape(x.shape[0] // 8, 8, x.shape[1]), 0)


def adafactor(grad, weight, new, col_old, col_new, sums, old, scale):
    n_rows, n_cols = grad.shape
    chans = old.shape[1]
    blk = chans
    halves = n_cols // chans
    col_sum = [jnp.zeros((8, chans), f32)] * halves
    scaled = [jnp.zeros((8, chans), f32)] * halves
    row_sum = jnp.zeros((8, chans), f32)
    for b in range(n_rows // blk):
        s = slice(b * blk, (b + 1) * blk)
        row = old[s, :] + ((1.0 - BETA) / n_cols * sums[s, :] + (1.0 - BETA) * 1e-30)
        row_sum = row_sum + fold(row)
        root = lax.rsqrt(row)
        for h in range(halves):
            c = slice(h * chans, (h + 1) * chans)
            g = grad[s, c]
            step = g * root
            new[s, c] = step
            col_sum[h] = col_sum[h] + fold(g * g)
            scaled[h] = scaled[h] + fold(step * step)
    row_mean = jnp.sum(row_sum, 0, keepdims=True) / n_rows
    power = jnp.zeros((1, chans), f32)
    by_col = []
    for h in range(halves):
        col = fresh(col_old(h), jnp.sum(col_sum[h], 0, keepdims=True), n_rows)
        col_new(h, col)
        power = power + jnp.sum(scaled[h], 0, keepdims=True) / col
        by_col.append(lax.rsqrt(col))
    rms = jnp.sqrt(row_mean * jnp.sum(power, -1, keepdims=True) / (n_rows * n_cols))
    coef = scale * jnp.sqrt(row_mean) / jnp.maximum(1.0, rms)
    by_col = [x * coef for x in by_col]

    def second(b, carry):
        s = pl.ds(b * blk, blk)
        for h in range(halves):
            c = slice(h * chans, (h + 1) * chans)
            new[s, c] = weight[s, c] - new[s, c] * by_col[h]
        return carry

    if n_rows <= 2 * blk:
        for b in range(n_rows // blk):
            second(b, 0)
    else:
        lax.fori_loop(0, n_rows // blk, second, 0)


def tables_kernel(
    tokens_h, lengths_s, recycle_s, resolved_h, coords_h, embed_h, uv_h, qk_h, affine_h, out_h,
    w_in_h, w_pairin_h, w_tri_h, vecs_h, row_in_h, col_in_h, row_pairin_h, col_pairin_h, row_tri_h,
    col_tri_h, sq_vecs_h,
    frozen_o, single_o, tail_o, old_o, scale_o, g_tri_o, new_tri_o, row_tri_o, col_tri_o,
    w_in_v, w_pairin_v, w_tri_v, vecs_v, row_in_v, col_in_v, row_pairin_v, col_pairin_v, row_tri_v,
    col_tri_v, sq_vecs_v,
    tokens_v, resolved_v, coords_v, embed_v, uv_v, qk_v, affine_v, out_v,
    emb, item_x, gate_x, value_x, partial_v, part, w_in_b, w_pair_b, w_tri_b, cnt_b, true_d, cols,
    pair, sb, n1, s1, pnorm, proj, sig_l, sig_r, gate, left, right, upd, n2, s2, unorm,
    branch, final, dbranch, left_n, gated_b, dunorm, dpnorm, dlast, dleft, dright, upd_t, dproj,
    old_v, one_t, gtri_x, sq_tri, sum_tri,
    load_sem, part_send, part_recv, unit_send, unit_recv, peer_send, peer_recv,
    *, heads, shared_by, unit_part,
):
    grp = lax.axis_index("grp")
    head = lax.axis_index("head")
    other = 1 - grp
    turned = lax.rem(head, 2)
    item = lax.rem(grp + head, 2)

    def partner(d):
        peer = lax.rem(head + d, heads)
        return {"grp": lax.rem(item + peer, 2), "head": peer}

    seq = tokens_v.shape[1]
    width = emb.shape[1]
    chans = vecs_v.shape[1]
    vocab = embed_v.shape[0]
    half = width // 2
    quarter = width // 4

    loads = []

    def load(src, dst):
        copy = pltpu.make_async_copy(src, dst, load_sem.at[len(loads)])
        loads.append(copy)
        copy.start()
        return copy

    c_small = [
        load(embed_h, embed_v),
        load(tokens_h, tokens_v),
        load(resolved_h, resolved_v),
        load(coords_h, coords_v),
        load(affine_h, affine_v),
    ]
    mine = grp if shared_by == 2 else 0
    at_mine = pl.multiple_of(mine * unit_part, 128)
    c_gate = load(uv_h.at[0, :, pl.ds(at_mine, unit_part)], uv_v.at[0])
    c_value = load(uv_h.at[1, :, pl.ds(at_mine, unit_part)], uv_v.at[1])
    c_qk = load(qk_h, qk_v)
    c_out = []
    for k in range(shared_by):
        at = pl.multiple_of(lax.rem(mine + k, shared_by) * unit_part, 128)
        c_out.append(load(out_h.at[pl.ds(at, unit_part)], out_v.at[k]))
    c_par = [
        load(w_in_h, w_in_v),
        load(w_pairin_h, w_pairin_v),
        load(w_tri_h, w_tri_v),
        load(vecs_h, vecs_v),
        load(row_in_h, row_in_v),
        load(row_pairin_h, row_pairin_v),
        load(row_tri_h, row_tri_v),
        load(col_in_h, col_in_v),
        load(col_pairin_h, col_pairin_v),
        load(col_tri_h, col_tri_v),
        load(sq_vecs_h, sq_vecs_v),
    ]

    barrier = pltpu.get_barrier_semaphore()
    pl.semaphore_signal(barrier, inc=1, device_id={"grp": other}, device_id_type=MESH)
    for d in range(1, heads):
        pl.semaphore_signal(barrier, inc=1, device_id=partner(d), device_id_type=MESH)

    for c in c_small:
        c.wait()
    emb[...] = jnp.zeros_like(emb)
    emb[0:vocab, :] = embed_v[...].astype(f32)
    e = emb[...]
    centre = e - mean_last(e)
    normed = (centre * lax.rsqrt(mean_last(centre * centre) + 1e-05)).astype(bf16)

    key_ok = (iota((1, seq), 1) < lengths_s[0]).astype(f32)
    for k in range(3):
        item_x[0, k : k + 1, :] = coords_v[k]
    item_x[0, 3:4, :] = key_ok * (resolved_v[...] > 0).astype(f32)
    item_x[0, 4:5, :] = tokens_v[...].astype(f32)
    item_x[0, 5:6, :] = key_ok
    item_x[0, 6:8, :] = jnp.broadcast_to(recycle_s[0].astype(f32), (2, seq))
    pl.semaphore_wait(barrier, heads)
    unit_sends = []

    def swap(ref, k):
        copy = pltpu.make_async_remote_copy(
            src_ref=ref.at[0],
            dst_ref=ref.at[1],
            send_sem=unit_send.at[k],
            recv_sem=unit_recv.at[k],
            device_id={"grp": other},
            device_id_type=MESH,
        )
        copy.start()
        unit_sends.append(copy)
        return copy

    c_item = swap(item_x, 2)

    c_gate.wait()
    ugate = silu(dot(normed, uv_v[0]))
    gate_x[0] = ugate[0:ROWS]
    if shared_by == 2:
        swap(gate_x, 0)
    c_value.wait()
    value_x[0] = silu(dot(normed, uv_v[1])).astype(bf16)
    if shared_by == 2:
        swap(value_x, 1)

    c_item.wait_recv()
    cols[0:8, :] = jnp.where(turned > 0, item_x[1], item_x[0])
    valid = cols[3:4, :]
    key_ok = cols[5:6, :]
    recycle = cols[6:7, 0:1]
    onehot = (iota((WIDE, seq), 0) == cols[4:5, :].astype(jnp.int32)).astype(f32)
    one_b = onehot.astype(bf16)
    cnt_col = jnp.sum(onehot, -1, keepdims=True)
    cnt_b[...] = jnp.broadcast_to(cnt_col, (WIDE, chans))
    ones = jnp.ones((16, seq), bf16)
    cnt_row = dot_nt(ones, one_b)[0:1, :]
    key_row = dot_nt(ones, (onehot * key_ok).astype(bf16))[0:1, :]

    c_qk.wait()
    shared = silu(dot(normed, qk_v[...]))
    query = (shared * affine_v[0:1, :] + affine_v[1:2, :]).astype(bf16)
    keyed = (shared * affine_v[2:3, :] + affine_v[3:4, :]).astype(bf16)
    scores = dot_nt(query, keyed) / math.sqrt(qk_v.shape[1])
    masked = jnp.where(key_row > 0, scores, -1000000000.0)
    top = jnp.exp(masked - jnp.max(masked, -1, keepdims=True))
    attn = (top / jnp.sum(top * key_row, -1, keepdims=True)).astype(bf16).astype(f32)
    attn = jnp.concatenate(split(attn * key_row, 2), 0)

    def mix(k):
        seen = dot(attn, value_x[k])
        seen = seen[0:ROWS] + seen[WIDE : WIDE + ROWS]
        return (gate_x[k] * seen).astype(bf16)

    mixed = mix(0)
    c_out[0].wait()
    if shared_by == 2:
        partial_v[...] = dot(mixed, out_v[0])
        for c in unit_sends[1:]:
            c.wait_recv()
        mixed = mix(1)
        c_out[1].wait()
    sends = []
    for n in range(2):
        s = slice(n * half, (n + 1) * half)
        p = dot(mixed, out_v[shared_by - 1, :, s])
        if shared_by == 2:
            p = p + partial_v[:, s]
        part[head, n, :, 0:half] = p[0:16].astype(bf16)
        part[head, n, :, half : half + quarter] = jnp.concatenate(
            [p[16:24, 0:quarter], p[16:24, quarter:half]], 0
        ).astype(bf16)
        for d in range(1, heads):
            copy = pltpu.make_async_remote_copy(
                src_ref=part.at[head, n],
                dst_ref=part.at[head, n],
                send_sem=part_send.at[d - 1, n],
                recv_sem=part_recv.at[head, n],
                device_id=partner(d),
                device_id_type=MESH,
            )
            copy.start()
            sends.append(copy)

    for c in c_par:
        c.wait()
    w_in_b[...] = w_in_v[...].astype(bf16)
    for k in range(2):
        w_pair_b[:, k * chans : (k + 1) * chans] = w_pairin_v[k].astype(bf16)
    v0 = vecs_v[0:1, :]
    v1 = vecs_v[1:2, :]
    v2 = vecs_v[2:3, :]
    v3 = vecs_v[3:4, :]
    gain_one = vecs_v[...].T[:, 1:2]
    gain_two = vecs_v[...].T[:, 2:3]
    for k, m in enumerate(ORDER + (5,)):
        c = slice(k * chans, (k + 1) * chans)
        w = w_tri_v[m].astype(bf16)
        w_tri_b[0:chans, c] = w
        w = w.astype(f32) * (gain_two if m == 5 else gain_one)
        w = jnp.sum(w, 0, keepdims=True) * (1.0 / chans)
        w_tri_b[chans : 2 * chans, c] = jnp.broadcast_to(w, (chans, chans)).astype(bf16)
    cols[8:chans, :] = jnp.zeros((chans - 8, seq), f32)
    one_v = (onehot * valid).astype(bf16)
    weight_j = recycle * valid
    blk = 128
    n_blk = seq // blk
    places = []
    for b in range(n_blk):
        t = cols[:, b * blk : (b + 1) * blk].T
        hot = lax.bitwise_and(iota((blk, chans), 1), WIDE - 1) == t[:, 4:5].astype(jnp.int32)
        hot = hot & (iota((blk, chans), 1) < 3 * WIDE)
        one_t[b * blk : (b + 1) * blk, :] = hot.astype(f32).astype(bf16)
        places.append(t)
        d2 = None
        for k in range(3):
            delta = t[:, k : k + 1] - cols[k : k + 1, :]
            d2 = delta * delta if d2 is None else d2 + delta * delta
        true_d[b * blk : (b + 1) * blk, :] = jnp.sqrt(d2)
    n_valid = jnp.sum(valid, -1, keepdims=True)
    loss_count = recycle * n_valid * n_valid

    present = cnt_b[0:ROWS, :] > 0
    sc = jnp.where((cnt_row > 0) & (cnt_col > 0), scores, 0.0)[0:ROWS]

    n_chunk = ROWS // 2
    two = 2 * ROWS

    def rows(k):
        return slice(k * two, (k + 1) * two)

    def both(f, k):
        return jnp.concatenate([f(2 * k), f(2 * k + 1)], 0)

    v0c = v0 - mean_last(v0)
    for k in range(n_chunk):
        r = rows(k)
        sbk = both(lambda u: jnp.broadcast_to(sc[:, u : u + 1], (ROWS, chans)), k)
        sb[r] = sbk
        pair[r] = sbk * v0
        n1[r] = sbk * v0c
    lane = iota((ROWS, chans), 1)
    score_logit = jnp.sum(v0 * v3, -1, keepdims=True) * jnp.concatenate(
        [sc, jnp.zeros((ROWS, chans - WIDE), f32)], 1
    )

    n_in = width // chans
    n_pr = w_pairin_v.shape[1] // chans
    at_tri = n_in + 2 * n_pr
    old_v[...] = jnp.zeros_like(old_v)
    old_v[0:n_in, :] = row_in_v[...]
    for k in range(2):
        for b in range(n_pr):
            j = n_in + k * n_pr + b
            old_v[j : j + 1, :] = row_pairin_v[k : k + 1, b * chans : (b + 1) * chans]
    old_v[at_tri : at_tri + 6, :] = row_tri_v[...]
    old = BETA * old_v[...].T
    for k in range(at_tri + 6):
        old_o[k * chans : (k + 1) * chans, :] = jnp.broadcast_to(old[:, k : k + 1], (chans, chans))
    scale_o[...] = jnp.zeros_like(scale_o)
    mats = [w_in_v] + [w_pairin_v.at[k] for k in range(2)] + [w_tri_v.at[m] for m in range(6)]
    for k, w in enumerate(mats):
        x = w[...]
        x = jnp.sum(jnp.sum(x * x, 0, keepdims=True), -1, keepdims=True) / (w.shape[0] * w.shape[1])
        x = RATE * jnp.maximum(0.001, jnp.sqrt(x))
        scale_o[k : k + 1, :] = jnp.broadcast_to(x, (1, chans))

    for n in range(2):
        for d in range(1, heads):
            peer = lax.rem(head + d, heads)
            pltpu.make_async_remote_copy(
                src_ref=part.at[peer, n],
                dst_ref=part.at[peer, n],
                send_sem=part_send.at[d - 1, n],
                recv_sem=part_recv.at[peer, n],
                device_id=partner(d),
                device_id_type=MESH,
            ).wait_recv()
    for n in range(2):
        s = slice(n * half, (n + 1) * half)
        low = None
        for k in range(heads):
            a = part[k, n, :, 0:half].astype(f32)
            b = part[k, n, :, half : half + quarter].astype(f32)
            b = jnp.concatenate([b[0:8], b[8:16]], 1)
            low = [a, b] if low is None else [low[0] + a, low[1] + b]
        emb[0:16, s] += low[0]
        emb[16:24, s] += low[1]
    state = emb[0:ROWS, :]
    centre = state - mean_last(state)
    frozen = centre * lax.rsqrt(mean_last(centre * centre) + 1e-05)
    frozen = jnp.concatenate([frozen, jnp.zeros((WIDE - ROWS, width), f32)], 0).astype(bf16)
    frozen_o[item] = frozen

    peers = []

    def give(ref):
        k = len(peers)
        copy = pltpu.make_async_remote_copy(
            src_ref=ref,
            dst_ref=ref,
            send_sem=peer_send.at[k],
            recv_sem=peer_recv.at[k],
            device_id={"grp": other},
            device_id_type=MESH,
        )
        copy.start()
        peers.append(copy)
        return copy

    give(frozen_o.at[item])
    single = dot(frozen, w_in_b[...]).astype(bf16)
    single_o[item] = jnp.concatenate(
        [single[0:ROWS].astype(f32), jnp.broadcast_to(loss_count, (8, single.shape[1]))], 0
    )
    c_single = give(single_o.at[item])
    side = dot(single, w_pair_b[...])[0:ROWS]
    side_a = jnp.where(present, side[:, 0:chans], 0.0)
    side_b = jnp.where(present, side[:, chans : 2 * chans], 0.0)
    side_ac = side_a - mean_last(side_a)
    side_bc = side_b - mean_last(side_b)

    own = iota((ROWS, chans), 0) == lane
    logit_b = jnp.sum(
        jnp.where(own, jnp.sum(side_b * v3, -1, keepdims=True), 0.0), 0, keepdims=True
    )
    logit = score_logit + jnp.sum(side_a * v3, -1, keepdims=True) + logit_b
    for k in range(n_chunk):
        r = rows(k)
        pair[r] = pair[r] + both(lambda u: side_a + side_b[u : u + 1, :], k)
        centre = n1[r] + both(lambda u: side_ac + side_bc[u : u + 1, :], k)
        scale = lax.rsqrt(mean_last(centre * centre) + 1e-05)
        normal = centre * scale
        n1[r] = normal
        s1[r] = jnp.broadcast_to(scale, (two, chans))
        pnorm[r] = (normal * v1).astype(bf16)
    proj[...] = dot(pnorm[...], w_tri_b[0:chans, 0 : 5 * chans])
    for k in range(n_chunk):
        r = rows(k)
        sl = sigmoid(proj[r, chans : 2 * chans])
        sr = sigmoid(proj[r, 4 * chans : 5 * chans])
        sig_l[r] = sl
        sig_r[r] = sr
        left[r] = (sl * proj[r, 0:chans]).astype(bf16).astype(f32)
        right[r] = (sr * proj[r, 3 * chans : 4 * chans]).astype(bf16).astype(f32)
        gate[r] = sigmoid(proj[r, 2 * chans : 3 * chans])
        left_n[r] = left[r] * both(
            lambda u: jnp.broadcast_to(cnt_b[u : u + 1, :], (ROWS, chans)), k
        )

    def triangle(dst, moving, fixed, row_of, weighted):
        group = 8
        for a0 in range(0, ROWS, group):
            total = [None] * group
            for b in range(vocab):
                x = moving(b)
                for q in range(group):
                    y = x * fixed[pl.ds(row_of(a0 + q, b), 1), :]
                    total[q] = y if total[q] is None else total[q] + y
            for q in range(group):
                a = a0 + q
                t = total[q]
                if weighted:
                    t = t * cnt_b[a : a + 1, :]
                dst[a * ROWS : (a + 1) * ROWS, :] = t

    triangle(
        upd, lambda u: left_n[u * ROWS : (u + 1) * ROWS, :], right, lambda v, u: u * ROWS + v, False
    )
    for k in range(n_chunk):
        r = rows(k)
        x = upd[r]
        centre = x - mean_last(x)
        scale = lax.rsqrt(mean_last(centre * centre) + 1e-05)
        normal = centre * scale
        n2[r] = normal
        s2[r] = jnp.broadcast_to(scale, (two, chans))
        unorm[r] = (normal * v2).astype(bf16)
    branch[...] = dot(unorm[...], w_tri_b[0:chans, 5 * chans : 6 * chans])
    gated = jnp.zeros((ROWS, chans), f32)
    for k in range(n_chunk):
        r = rows(k)
        move = gate[r] * branch[r]
        final[r] = pair[r] + move
        col = jnp.sum(move * v3, -1, keepdims=True)
        gated_b[r] = jnp.broadcast_to(col, (two, chans))
        for q in range(2):
            gated = jnp.where(lane == 2 * k + q, col[q * ROWS : (q + 1) * ROWS], gated)
    logit = logit + gated

    dist = jnp.maximum(logit, 0.0) + jnp.log(1.0 + jnp.exp(-jnp.abs(logit)))
    dist = jnp.concatenate([dist, jnp.zeros((WIDE - ROWS, chans), f32)], 0)
    dist = jnp.concatenate(split(dist, 3), 0)
    by_col = dot(dist[:, 0:WIDE], one_b).astype(bf16)
    for k in range(n_chunk):
        r = rows(k)
        sl, sr, gt = sig_l[r], sig_r[r], gate[r]
        proj[r, 0:chans] = proj[r, 0:chans] * sl * (1.0 - sl)
        proj[r, 3 * chans : 4 * chans] = proj[r, 3 * chans : 4 * chans] * sr * (1.0 - sr)
        gt3 = gt * v3
        proj[r, 2 * chans : 3 * chans] = gt3 * (1.0 - gt) * branch[r]
        gate[r] = gt3
    loss_row = jnp.zeros((1, seq), f32)
    by_first = jnp.zeros((WIDE, seq), f32)
    for b in range(n_blk):
        s = slice(b * blk, (b + 1) * blk)
        diff = dot(one_t[s, 0 : 3 * WIDE], by_col) - true_d[s, :]
        sq = diff * diff + 1.0
        inv = lax.rsqrt(sq)
        loss_row = loss_row + jnp.sum(
            places[b][:, 3:4] * (sq * inv - 1.0), 0, keepdims=True
        )
        by_first = by_first + dot(one_v[:, s], (diff * inv).astype(bf16))
    loss = jnp.sum(loss_row * weight_j, -1, keepdims=True)
    by_pair = dot_nt(jnp.concatenate(split(by_first * weight_j, 2), 0), one_b)
    by_pair = (by_pair[0:WIDE] + by_pair[WIDE : 2 * WIDE])[0:ROWS]
    dlogit = by_pair * sigmoid(logit)[:, 0:WIDE]

    g_dist = jnp.zeros((two, chans), f32)
    for k in range(n_chunk):
        r = rows(k)
        g = both(lambda u: jnp.broadcast_to(dlogit[:, u : u + 1], (ROWS, chans)), k)
        g_dist = g_dist + g * final[r]
        dfinal = g * v3
        pair[r] = dfinal
        dbranch[r] = (g * gate[r]).astype(bf16)
        dproj[r, 2 * chans : 3 * chans] = (g * proj[r, 2 * chans : 3 * chans]).astype(bf16)
        gated_b[r] = g * gated_b[r] * (1.0 / chans)
    dunorm[...] = dot_nt(dbranch[...], w_tri_b[:, 5 * chans : 6 * chans])
    gtri_x[item, 5] = dot_tn(unorm[...], dbranch[...])
    gtri_x[item, 4] = dot_tn(pnorm[...], dproj[:, 2 * chans : 3 * chans])
    c_pair = [give(gtri_x.at[item, pl.ds(4, 2)])]
    g_two = jnp.zeros((two, chans), f32)
    for k in range(n_chunk):
        r = rows(k)
        dn = dunorm[r, 0:chans]
        normal = n2[r]
        g_two = g_two + dn * normal
        upd[r] = s2[r] * (dn * v2 - dunorm[r, chans : 2 * chans] - normal * gated_b[r])
    triangle(
        dleft, lambda v: upd[v * ROWS : (v + 1) * ROWS, :], right, lambda u, v: u * ROWS + v, True
    )
    for k in range(n_chunk):
        r = rows(k)
        d, sl = dleft[r], sig_l[r]
        dproj[r, 0:chans] = (d * sl).astype(bf16)
        dproj[r, chans : 2 * chans] = (d * proj[r, 0:chans]).astype(bf16)
    dpnorm[...] = dot_nt(dproj[:, 0 : 3 * chans], w_tri_b[:, 0 : 3 * chans])
    g = dot_tn(pnorm[...], dproj[:, 0 : 2 * chans])
    gtri_x[item, 0] = g[:, 0:chans]
    gtri_x[item, 1] = g[:, chans : 2 * chans]
    c_pair.append(give(gtri_x.at[item, pl.ds(0, 2)]))
    for t in range(vocab):
        upd_t[t * ROWS : (t + 1) * ROWS, :] = upd[pl.ds(t, ROWS, stride=ROWS), :]
    triangle(
        dright, lambda t: upd_t[t * ROWS : (t + 1) * ROWS, :], left, lambda u, t: u * ROWS + t, True
    )
    for k in range(n_chunk):
        r = rows(k)
        d, sr = dright[r], sig_r[r]
        dproj[r, 3 * chans : 4 * chans] = (d * sr).astype(bf16)
        dproj[r, 4 * chans : 5 * chans] = (d * proj[r, 3 * chans : 4 * chans]).astype(bf16)
    dlast[...] = dot_nt(dproj[:, 3 * chans : 5 * chans], w_tri_b[:, 3 * chans : 5 * chans])
    g = dot_tn(pnorm[...], dproj[:, 3 * chans : 5 * chans])
    gtri_x[item, 2] = g[:, 0:chans]
    gtri_x[item, 3] = g[:, chans : 2 * chans]
    c_pair.append(give(gtri_x.at[item, pl.ds(2, 2)]))
    g_one = jnp.zeros((two, chans), f32)
    g_score = jnp.zeros((two, chans), f32)
    d_a = jnp.zeros((ROWS, chans), f32)
    tail_o[item] = jnp.zeros((WIDE, 2 * chans), f32)
    for k in range(n_chunk):
        r = rows(k)
        dn = dpnorm[r, 0:chans] + dlast[r, 0:chans]
        mean = dpnorm[r, chans : 2 * chans] + dlast[r, chans : 2 * chans]
        normal = n1[r]
        along = dn * normal
        g_one = g_one + along
        dpair = pair[r] + s1[r] * (dn * v1 - mean - normal * mean_last(along * v1))
        g_score = g_score + sb[r] * dpair
        d_a = d_a + dpair[0:ROWS] + dpair[ROWS:two]
        for q in range(2):
            tail_o[item, 2 * k + q : 2 * k + q + 1, chans : 2 * chans] = jnp.sum(
                dpair[q * ROWS : (q + 1) * ROWS], 0, keepdims=True
            )
    tail_o[item, 0:ROWS, 0:chans] = d_a
    for k, g in enumerate((g_score, g_one, g_two, g_dist)):
        tail_o[item, ROWS + k : ROWS + k + 1, 0:chans] = jnp.sum(g, 0, keepdims=True)
    tail_o[item, ROWS + 4 : ROWS + 5, 0:chans] = jnp.broadcast_to(loss, (1, chans))
    tail_o[item, ROWS + 5 : ROWS + 6, 0:chans] = jnp.broadcast_to(loss_count, (1, chans))
    c_tail = give(tail_o.at[item])

    c_single.wait_recv()
    inv = 1.0 / (
        single_o[0, ROWS : ROWS + 1, 0:chans] + single_o[1, ROWS : ROWS + 1, 0:chans]
    )
    for pairs in ((0, 1), (2,)):
        mats = []
        for k in pairs:
            c_pair[k].wait_recv()
            first = (4, 0, 2)[k]
            mats += [first, first + 1]
        for m in mats:
            g = (gtri_x[0, m] + gtri_x[1, m]) * inv
            g_tri_o[m] = g
            sq_tri[m * chans : (m + 1) * chans, :] = (g * g).astype(bf16)
        for m in mats:
            r = slice(m * chans, (m + 1) * chans)
            sum_tri[r, :] = dot(sq_tri[r, :], jnp.ones((chans, chans), bf16))
        for m in mats:
            total = sum_tri[m * chans : (m + 1) * chans, :].T[0:1, :]
            row_tri_o[m : m + 1, :] = fresh(row_tri_v[m : m + 1, :], total, chans)

            def put_col(h, col, m=m):
                col_tri_o[m : m + 1, :] = col

            adafactor(
                g_tri_o.at[m], w_tri_v.at[m], new_tri_o.at[m],
                lambda h, m=m: col_tri_v[m : m + 1, :], put_col,
                sum_tri.at[pl.ds(m * chans, chans)],
                old_o.at[pl.ds((at_tri + m) * chans, chans)],
                scale_o[3 + m : 4 + m, :],
            )

    for c in sends + unit_sends + peers:
        c.wait_send()
    for c in peers:
        if c is not c_single and all(c is not x for x in c_pair):
            c.wait_recv()


def update_kernel(
    frozen_v, single_v, tail_v, old_v, scale_v, g_tri, new_tri, row_tri_n, col_tri_n,
    w_in_v, w_pairin_v, w_tri_v, vecs_v,
    row_in_v, col_in_v, row_pairin_v, col_pairin_v, row_tri_v, col_tri_v, sq_vecs_v,
    loss_o, count_o, g_in_o, row_in_o, col_in_o, new_in_o, g_pairin_o, row_pairin_o, col_pairin_o,
    new_pairin_o, g_tri_o, row_tri_o, col_tri_o, new_tri_o, g_vecs_o, sq_vecs_o, new_vecs_o,
    loss_s, count_s, g_in, row_in_n, col_in_n, new_in, g_pairin, row_pairin_n, col_pairin_n,
    new_pairin, g_vecs, sq_vecs_n, new_vecs,
    ds_v, sq_in, sq_rest, sum_in, sum_rest, store_sem,
):
    chans = vecs_v.shape[1]
    width, node = w_in_v.shape
    stores = []

    def store(src, dst):
        copy = pltpu.make_async_copy(src, dst, store_sem.at[len(stores)])
        stores.append(copy)
        copy.start()

    store(g_tri, g_tri_o)
    store(new_tri, new_tri_o)
    store(row_tri_n, row_tri_o)
    store(col_tri_n, col_tri_o)
    totals = tail_v[0, ROWS : ROWS + 8, 0:chans] + tail_v[1, ROWS : ROWS + 8, 0:chans]
    inv = 1.0 / totals[5:6, :]
    inv2 = jnp.concatenate([inv, inv], 1)
    d_side = [tail_v[i, 0:ROWS, :] * inv2 for i in range(2)]

    pads = jnp.zeros((WIDE - ROWS, node), f32)
    side_parts = []
    for i in range(2):
        parts = split(d_side[i], 2)
        side_parts.append(parts)
        st = jnp.concatenate([p.astype(f32) for p in parts], 0).astype(bf16)
        ds = dot_nt(st[:, 0:chans], w_pairin_v[0].astype(bf16)) + dot_nt(
            st[:, chans : 2 * chans], w_pairin_v[1].astype(bf16)
        )
        ds = ds[0:ROWS] + ds[ROWS : 2 * ROWS]
        for k, p in enumerate(split(ds, 2)):
            at = (2 * k + i) * WIDE
            ds_v[at : at + WIDE, :] = jnp.concatenate([p.astype(f32), pads], 0).astype(bf16)
    fz = jnp.concatenate([frozen_v[0], frozen_v[1], frozen_v[0], frozen_v[1]], 0)
    g_in[...] = dot_tn(fz, ds_v[...])
    store(g_in, g_in_o)

    sg = [single_v[i, 0:ROWS] for i in range(2)]
    sg = jnp.concatenate(sg + sg, 0).astype(bf16)
    st = jnp.concatenate(
        [side_parts[i][k].astype(f32) for k in range(2) for i in range(2)], 0
    ).astype(bf16)
    for k in range(2):
        g_pairin[k] = dot_tn(sg, st[:, k * chans : (k + 1) * chans])
    store(g_pairin, g_pairin_o)
    loss_s[...] = totals[4:5, :]
    count_s[...] = totals[5:6, :]
    g_vecs[...] = totals[0:4, :] * inv
    store(loss_s, loss_o)
    store(count_s, count_o)
    store(g_vecs, g_vecs_o)

    blk = chans
    n_in = width // blk
    n_pr = w_pairin_v.shape[1] // blk
    for b in range(n_in):
        g = g_in[b * blk : (b + 1) * blk, :]
        sq_in[b * blk : (b + 1) * blk, :] = (g * g).astype(bf16)
    for k in range(2):
        for b in range(n_pr):
            g = g_pairin[k, b * blk : (b + 1) * blk, :]
            j = k * n_pr + b
            sq_rest[j * blk : (j + 1) * blk, :] = (g * g).astype(bf16)
    sum_in[...] = dot(sq_in[...], jnp.ones((node, chans), bf16))
    sum_rest[...] = dot(sq_rest[...], jnp.ones((chans, chans), bf16))
    for b in range(n_in):
        total = sum_in[b * blk : (b + 1) * blk, :].T[0:1, :]
        row_in_n[b : b + 1, :] = fresh(row_in_v[b : b + 1, :], total, node)
    for k in range(2):
        for b in range(n_pr):
            j = k * n_pr + b
            total = sum_rest[j * blk : (j + 1) * blk, :].T[0:1, :]
            c = slice(b * blk, (b + 1) * blk)
            row_pairin_n[k : k + 1, c] = fresh(row_pairin_v[k : k + 1, c], total, chans)
    store(row_in_n, row_in_o)
    store(row_pairin_n, row_pairin_o)

    def put(ref, k):
        def put_col(h, col):
            at = k if k is not None else h
            ref[at : at + 1, :] = col

        return put_col

    adafactor(
        g_in, w_in_v, new_in, lambda h: col_in_v[h : h + 1, :], put(col_in_n, None), sum_in,
        old_v.at[pl.ds(0, width)], scale_v[0:1, :],
    )
    store(new_in, new_in_o)
    store(col_in_n, col_in_o)
    for k in range(2):
        adafactor(
            g_pairin.at[k], w_pairin_v.at[k], new_pairin.at[k],
            lambda h, k=k: col_pairin_v[k : k + 1, :], put(col_pairin_n, k),
            sum_rest.at[pl.ds(k * n_pr * blk, n_pr * blk)],
            old_v.at[pl.ds((n_in + k * n_pr) * blk, n_pr * blk)], scale_v[1 + k : 2 + k, :],
        )
    store(new_pairin, new_pairin_o)
    store(col_pairin_n, col_pairin_o)

    g = g_vecs[...]
    sq = BETA * sq_vecs_v[...] + (1.0 - BETA) * (g * g + 1e-30)
    sq_vecs_n[...] = sq
    step = g * lax.rsqrt(sq)
    step = step / jnp.maximum(1.0, jnp.sqrt(mean_last(step * step)))
    v = vecs_v[...]
    scale = jnp.maximum(0.001, jnp.sqrt(mean_last(v * v)))
    new_vecs[...] = v - RATE * scale * step
    store(sq_vecs_n, sq_vecs_o)
    store(new_vecs, new_vecs_o)
    for c in stores:
        c.wait()


def shards(
    tokens, lengths, recycle, resolved, coords, plm_embed, plm_uv, plm_qk, plm_affine, plm_out,
    w_in, w_pairin, w_tri, vecs, row_in, col_in, row_pairin, col_pairin, row_tri, col_tri, sq_vecs,
):
    heads = lax.axis_size("head")
    seq = tokens.shape[1]
    width = plm_embed.shape[1]
    units = plm_uv.shape[2]
    chans = vecs.shape[1]
    node = w_in.shape[1]
    shared_by = 2 if units % 256 == 0 else 1
    unit_part = units // shared_by
    anywhere = pl.BlockSpec(memory_space=pl.ANY)
    inside = pl.BlockSpec(memory_space=pltpu.VMEM)
    table = ROWS * ROWS

    def vm(*shape, dtype=f32):
        return pltpu.VMEM(shape, dtype)

    def like(x):
        return pltpu.VMEM(x.shape, x.dtype)

    coords = jnp.transpose(coords, (1, 0, 2))
    row_in2 = row_in.reshape(-1, chans)
    col_in2 = col_in.reshape(-1, chans)
    operands = (
        tokens, lengths, recycle, resolved, coords, plm_embed, plm_uv, plm_qk, plm_affine, plm_out,
        w_in, w_pairin, w_tri, vecs, row_in2, col_in2, row_pairin, col_pairin, row_tri, col_tri, sq_vecs,
    )
    kept = operands[10:]
    scratch = [
        like(tokens), like(resolved),
        like(coords), like(plm_embed), vm(2, width, unit_part, dtype=bf16), like(plm_qk),
        like(plm_affine), vm(shared_by, unit_part, width, dtype=bf16),
        vm(WIDE, width), vm(2, 8, seq), vm(shared_by, ROWS, unit_part), vm(shared_by, WIDE, unit_part, dtype=bf16),
        vm(ROWS, width), vm(heads, 2, 16, width // 2 + width // 4, dtype=bf16),
        vm(width, node, dtype=bf16), vm(node, 2 * chans, dtype=bf16),
        vm(2 * chans, 6 * chans, dtype=bf16), vm(WIDE, chans), vm(seq, seq), vm(chans, seq),
        vm(table, chans), vm(table, chans), vm(table, chans), vm(table, chans),
        vm(table, chans, dtype=bf16), vm(table, 5 * chans), vm(table, chans), vm(table, chans),
        vm(table, chans), vm(table, chans), vm(table, chans), vm(table, chans), vm(table, chans),
        vm(table, chans), vm(table, chans, dtype=bf16),
        vm(table, chans), vm(table, chans), vm(table, chans, dtype=bf16), vm(table, chans),
        vm(table, chans), vm(table, 2 * chans), vm(table, 2 * chans), vm(table, 2 * chans),
        vm(table, chans), vm(table, chans), vm(table, chans), vm(table, 5 * chans, dtype=bf16),
        vm(chans, chans), vm(seq, chans, dtype=bf16),
        vm(2, 6, chans, chans), vm(6 * chans, chans, dtype=bf16), vm(6 * chans, chans),
        pltpu.SemaphoreType.DMA((19 + shared_by,)),
        pltpu.SemaphoreType.DMA((heads - 1, 2)), pltpu.SemaphoreType.DMA((heads, 2)),
        pltpu.SemaphoreType.DMA((3,)), pltpu.SemaphoreType.DMA((3,)),
        pltpu.SemaphoreType.DMA((6,)), pltpu.SemaphoreType.DMA((6,)),
    ]
    operands = tuple(
        x if x.size == 1 else pltpu.with_memory_space_constraint(x, pltpu.HBM) for x in operands
    )
    sds = jax.ShapeDtypeStruct
    n_blk = width // chans + 2 * (node // chans) + 6
    made = pl.pallas_call(
        functools.partial(tables_kernel, heads=heads, shared_by=shared_by, unit_part=unit_part),
        out_shape=(
            sds((2, WIDE, width), bf16), sds((2, WIDE, node), f32), sds((2, WIDE, 2 * chans), f32),
            sds((n_blk * chans, chans), f32), sds((16, chans), f32), sds(w_tri.shape, f32),
            sds(w_tri.shape, f32), sds(row_tri.shape, f32), sds(col_tri.shape, f32),
        )
        + tuple(sds(x.shape, x.dtype) for x in kept),
        in_specs=[
            pl.BlockSpec(memory_space=pltpu.SMEM) if x.size == 1 else anywhere for x in operands
        ],
        out_specs=[inside] * (9 + len(kept)),
        scratch_shapes=scratch,
        compiler_params=pltpu.CompilerParams(
            collective_id=0, has_side_effects=True, vmem_limit_bytes=48 << 20
        ),
        name="tables",
    )(*operands)

    operands = tuple(made)
    outs = (
        sds((1, chans), f32), sds((1, chans), f32), w_in, row_in2, col_in2, w_in, w_pairin,
        row_pairin, col_pairin, w_pairin, w_tri, row_tri, col_tri, w_tri, vecs, vecs, vecs,
    )
    outs = tuple(sds(x.shape, x.dtype) for x in outs)
    scratch = (
        [like(x) for k, x in enumerate(outs) if k not in (10, 11, 12, 13)]
        + [
            vm(4 * WIDE, node, dtype=bf16), vm(width, node, dtype=bf16),
            vm(2 * node, chans, dtype=bf16), vm(width, chans), vm(2 * node, chans),
            pltpu.SemaphoreType.DMA((17,)),
        ]
    )
    res = list(
        pl.pallas_call(
            update_kernel,
            out_shape=outs,
            in_specs=[inside] * len(operands),
            out_specs=[anywhere] * len(outs),
            scratch_shapes=scratch,
            compiler_params=pltpu.CompilerParams(vmem_limit_bytes=32 << 20),
            name="update",
        )(*operands)
    )
    res[0] = res[0][0, 0]
    res[1] = res[1][0, 0]
    res[3] = res[3].reshape(-1)
    res[4] = res[4].reshape(-1)
    return tuple(res)


def solution(mesh):
    whole = P()
    in_specs = (
        P("grp", None), P("grp"), P("grp"), P("grp", None), P("grp", None, None), whole,
        P(None, None, "head"), whole, whole, P("head", None),
    ) + (whole,) * 11
    return jax.shard_map(
        shards, mesh=mesh, in_specs=in_specs, out_specs=(whole,) * 17, check_vma=False
    )
```

```python
import functools
import math

import jax
import jax.numpy as jnp
from jax import lax
from jax.experimental import pallas as pl
from jax.experimental.pallas import tpu as pltpu
from jax.sharding import PartitionSpec as P


STEP = 10
ORDER = (0, 1, 4, 2, 3)
BETA = 1.0 - STEP ** (-0.8)
RATE = 0.3
MESH = pl.DeviceIdType.MESH
f32 = jnp.float32
bf16 = jnp.bfloat16
ROWS = 24
WIDE = 32


def dot(a, b):
    return jnp.dot(a, b, preferred_element_type=f32)


def dot_nt(a, b):
    return lax.dot_general(a, b, (((1,), (1,)), ((), ())), preferred_element_type=f32)


def dot_tn(a, b):
    return lax.dot_general(a, b, (((0,), (0,)), ((), ())), preferred_element_type=f32)


def sigmoid(x):
    return 0.5 * jnp.tanh(0.5 * x) + 0.5


def silu(x):
    return x * sigmoid(x)


def mean_last(x):
    return jnp.mean(x, -1, keepdims=True)


def split(x, parts):
    out = []
    for _ in range(parts):
        part = x.astype(bf16)
        out.append(part)
        x = x - part.astype(f32)
    return out


def iota(shape, dim):
    return lax.broadcasted_iota(jnp.int32, shape, dim)


def fresh(old, total, n):
    return BETA * old + ((1.0 - BETA) / n * total + (1.0 - BETA) * 1e-30)


def fold(x):
    return jnp.sum(x.reshape(x.shape[0] // 8, 8, x.shape[1]), 0)


def adafactor(grad, weight, new, col_old, col_new, sums, old, scale):
    n_rows, n_cols = grad.shape
    chans = old.shape[1]
    blk = chans
    halves = n_cols // chans
    col_sum = [jnp.zeros((8, chans), f32)] * halves
    scaled = [jnp.zeros((8, chans), f32)] * halves
    row_sum = jnp.zeros((8, chans), f32)
    for b in range(n_rows // blk):
        s = slice(b * blk, (b + 1) * blk)
        row = old[s, :] + ((1.0 - BETA) / n_cols * sums[s, :] + (1.0 - BETA) * 1e-30)
        row_sum = row_sum + fold(row)
        root = lax.rsqrt(row)
        for h in range(halves):
            c = slice(h * chans, (h + 1) * chans)
            g = grad[s, c]
            step = g * root
            new[s, c] = step
            col_sum[h] = col_sum[h] + fold(g * g)
            scaled[h] = scaled[h] + fold(step * step)
    row_mean = jnp.sum(row_sum, 0, keepdims=True) / n_rows
    power = jnp.zeros((1, chans), f32)
    by_col = []
    for h in range(halves):
        col = fresh(col_old(h), jnp.sum(col_sum[h], 0, keepdims=True), n_rows)
        col_new(h, col)
        power = power + jnp.sum(scaled[h], 0, keepdims=True) / col
        by_col.append(lax.rsqrt(col))
    rms = jnp.sqrt(row_mean * jnp.sum(power, -1, keepdims=True) / (n_rows * n_cols))
    coef = scale * jnp.sqrt(row_mean) / jnp.maximum(1.0, rms)
    by_col = [x * coef for x in by_col]

    def second(b, carry):
        s = pl.ds(b * blk, blk)
        for h in range(halves):
            c = slice(h * chans, (h + 1) * chans)
            new[s, c] = weight[s, c] - new[s, c] * by_col[h]
        return carry

    if n_rows <= 2 * blk:
        for b in range(n_rows // blk):
            second(b, 0)
    else:
        lax.fori_loop(0, n_rows // blk, second, 0)


def tables_kernel(
    tokens_h, lengths_s, recycle_s, resolved_h, coords_h, embed_h, uv_h, qk_h, affine_h, out_h,
    w_in_h, w_pairin_h, w_tri_h, vecs_h, row_in_h, col_in_h, row_pairin_h, col_pairin_h, row_tri_h,
    col_tri_h, sq_vecs_h,
    frozen_o, single_o, tail_o, old_o, scale_o, g_tri_o, new_tri_o, row_tri_o, col_tri_o,
    w_in_v, w_pairin_v, w_tri_v, vecs_v, row_in_v, col_in_v, row_pairin_v, col_pairin_v, row_tri_v,
    col_tri_v, sq_vecs_v,
    tokens_v, resolved_v, coords_v, embed_v, uv_v, qk_v, affine_v, out_v,
    emb, item_x, gate_x, value_x, partial_v, part, w_in_b, w_pair_b, w_tri_b, cnt_b, true_d, cols,
    pair, sb, n1, s1, pnorm, proj, sig_l, sig_r, gate, left, right, upd, n2, s2, unorm,
    branch, final, dbranch, left_n, gated_b, dunorm, dpnorm, dlast, dleft, dright, upd_t, dproj,
    old_v, one_t, gtri_x, sq_tri, sum_tri,
    load_sem, part_send, part_recv, unit_send, unit_recv, peer_send, peer_recv,
    *, heads, shared_by, unit_part,
):
    grp = lax.axis_index("grp")
    head = lax.axis_index("head")
    other = 1 - grp
    turned = lax.rem(head, 2)
    item = lax.rem(grp + head, 2)

    def partner(d):
        peer = lax.rem(head + d, heads)
        return {"grp": lax.rem(item + peer, 2), "head": peer}

    seq = tokens_v.shape[1]
    width = emb.shape[1]
    chans = vecs_v.shape[1]
    vocab = embed_v.shape[0]
    half = width // 2
    quarter = width // 4

    loads = []

    def load(src, dst):
        copy = pltpu.make_async_copy(src, dst, load_sem.at[len(loads)])
        loads.append(copy)
        copy.start()
        return copy

    c_small = [
        load(embed_h, embed_v),
        load(tokens_h, tokens_v),
        load(resolved_h, resolved_v),
        load(coords_h, coords_v),
        load(affine_h, affine_v),
    ]
    mine = grp if shared_by == 2 else 0
    at_mine = pl.multiple_of(mine * unit_part, 128)
    c_gate = load(uv_h.at[0, :, pl.ds(at_mine, unit_part)], uv_v.at[0])
    c_value = load(uv_h.at[1, :, pl.ds(at_mine, unit_part)], uv_v.at[1])
    c_qk = load(qk_h, qk_v)
    c_out = []
    for k in range(shared_by):
        at = pl.multiple_of(lax.rem(mine + k, shared_by) * unit_part, 128)
        c_out.append(load(out_h.at[pl.ds(at, unit_part)], out_v.at[k]))
    c_par = [
        load(w_in_h, w_in_v),
        load(w_pairin_h, w_pairin_v),
        load(w_tri_h, w_tri_v),
        load(vecs_h, vecs_v),
        load(row_in_h, row_in_v),
        load(row_pairin_h, row_pairin_v),
        load(row_tri_h, row_tri_v),
        load(col_in_h, col_in_v),
        load(col_pairin_h, col_pairin_v),
        load(col_tri_h, col_tri_v),
        load(sq_vecs_h, sq_vecs_v),
    ]

    barrier = pltpu.get_barrier_semaphore()
    pl.semaphore_signal(barrier, inc=1, device_id={"grp": other}, device_id_type=MESH)
    for d in range(1, heads):
        pl.semaphore_signal(barrier, inc=1, device_id=partner(d), device_id_type=MESH)

    for c in c_small:
        c.wait()
    emb[...] = jnp.zeros_like(emb)
    emb[0:vocab, :] = embed_v[...].astype(f32)
    e = emb[...]
    centre = e - mean_last(e)
    normed = (centre * lax.rsqrt(mean_last(centre * centre) + 1e-05)).astype(bf16)

    key_ok = (iota((1, seq), 1) < lengths_s[0]).astype(f32)
    for k in range(3):
        item_x[0, k : k + 1, :] = coords_v[k]
    item_x[0, 3:4, :] = key_ok * (resolved_v[...] > 0).astype(f32)
    item_x[0, 4:5, :] = tokens_v[...].astype(f32)
    item_x[0, 5:6, :] = key_ok
    item_x[0, 6:8, :] = jnp.broadcast_to(recycle_s[0].astype(f32), (2, seq))
    pl.semaphore_wait(barrier, heads)
    unit_sends = []

    def swap(ref, k):
        copy = pltpu.make_async_remote_copy(
            src_ref=ref.at[0],
            dst_ref=ref.at[1],
            send_sem=unit_send.at[k],
            recv_sem=unit_recv.at[k],
            device_id={"grp": other},
            device_id_type=MESH,
        )
        copy.start()
        unit_sends.append(copy)
        return copy

    c_item = swap(item_x, 2)

    c_gate.wait()
    ugate = silu(dot(normed, uv_v[0]))
    gate_x[0] = ugate[0:ROWS]
    if shared_by == 2:
        swap(gate_x, 0)
    c_value.wait()
    value_x[0] = silu(dot(normed, uv_v[1])).astype(bf16)
    if shared_by == 2:
        swap(value_x, 1)

    c_item.wait_recv()
    cols[0:8, :] = jnp.where(turned > 0, item_x[1], item_x[0])
    valid = cols[3:4, :]
    key_ok = cols[5:6, :]
    recycle = cols[6:7, 0:1]
    onehot = (iota((WIDE, seq), 0) == cols[4:5, :].astype(jnp.int32)).astype(f32)
    one_b = onehot.astype(bf16)
    cnt_col = jnp.sum(onehot, -1, keepdims=True)
    cnt_b[...] = jnp.broadcast_to(cnt_col, (WIDE, chans))
    ones = jnp.ones((16, seq), bf16)
    cnt_row = dot_nt(ones, one_b)[0:1, :]
    key_row = dot_nt(ones, (onehot * key_ok).astype(bf16))[0:1, :]

    c_qk.wait()
    shared = silu(dot(normed, qk_v[...]))
    query = (shared * affine_v[0:1, :] + affine_v[1:2, :]).astype(bf16)
    keyed = (shared * affine_v[2:3, :] + affine_v[3:4, :]).astype(bf16)
    scores = dot_nt(query, keyed) / math.sqrt(qk_v.shape[1])
    masked = jnp.where(key_row > 0, scores, -1000000000.0)
    top = jnp.exp(masked - jnp.max(masked, -1, keepdims=True))
    attn = (top / jnp.sum(top * key_row, -1, keepdims=True)).astype(bf16).astype(f32)
    attn = jnp.concatenate(split(attn * key_row, 2), 0)

    def mix(k):
        seen = dot(attn, value_x[k])
        seen = seen[0:ROWS] + seen[WIDE : WIDE + ROWS]
        return (gate_x[k] * seen).astype(bf16)

    mixed = mix(0)
    c_out[0].wait()
    if shared_by == 2:
        partial_v[...] = dot(mixed, out_v[0])
        for c in unit_sends[1:]:
            c.wait_recv()
        mixed = mix(1)
        c_out[1].wait()
    sends = []
    for n in range(2):
        s = slice(n * half, (n + 1) * half)
        p = dot(mixed, out_v[shared_by - 1, :, s])
        if shared_by == 2:
            p = p + partial_v[:, s]
        part[head, n, :, 0:half] = p[0:16].astype(bf16)
        part[head, n, :, half : half + quarter] = jnp.concatenate(
            [p[16:24, 0:quarter], p[16:24, quarter:half]], 0
        ).astype(bf16)
        for d in range(1, heads):
            copy = pltpu.make_async_remote_copy(
                src_ref=part.at[head, n],
                dst_ref=part.at[head, n],
                send_sem=part_send.at[d - 1, n],
                recv_sem=part_recv.at[head, n],
                device_id=partner(d),
                device_id_type=MESH,
            )
            copy.start()
            sends.append(copy)

    for c in c_par:
        c.wait()
    w_in_b[...] = w_in_v[...].astype(bf16)
    for k in range(2):
        w_pair_b[:, k * chans : (k + 1) * chans] = w_pairin_v[k].astype(bf16)
    v0 = vecs_v[0:1, :]
    v1 = vecs_v[1:2, :]
    v2 = vecs_v[2:3, :]
    v3 = vecs_v[3:4, :]
    gain_one = vecs_v[...].T[:, 1:2]
    gain_two = vecs_v[...].T[:, 2:3]
    for k, m in enumerate(ORDER + (5,)):
        c = slice(k * chans, (k + 1) * chans)
        w = w_tri_v[m].astype(bf16)
        w_tri_b[0:chans, c] = w
        w = w.astype(f32) * (gain_two if m == 5 else gain_one)
        w = jnp.sum(w, 0, keepdims=True) * (1.0 / chans)
        w_tri_b[chans : 2 * chans, c] = jnp.broadcast_to(w, (chans, chans)).astype(bf16)
    cols[8:chans, :] = jnp.zeros((chans - 8, seq), f32)
    one_v = (onehot * valid).astype(bf16)
    weight_j = recycle * valid
    blk = 128
    n_blk = seq // blk
    places = []
    for b in range(n_blk):
        t = cols[:, b * blk : (b + 1) * blk].T
        hot = lax.bitwise_and(iota((blk, chans), 1), WIDE - 1) == t[:, 4:5].astype(jnp.int32)
        hot = hot & (iota((blk, chans), 1) < 3 * WIDE)
        one_t[b * blk : (b + 1) * blk, :] = hot.astype(f32).astype(bf16)
        places.append(t)
        d2 = None
        for k in range(3):
            delta = t[:, k : k + 1] - cols[k : k + 1, :]
            d2 = delta * delta if d2 is None else d2 + delta * delta
        true_d[b * blk : (b + 1) * blk, :] = jnp.sqrt(d2)
    n_valid = jnp.sum(valid, -1, keepdims=True)
    loss_count = recycle * n_valid * n_valid

    present = cnt_b[0:ROWS, :] > 0
    sc = jnp.where((cnt_row > 0) & (cnt_col > 0), scores, 0.0)[0:ROWS]

    n_chunk = ROWS // 2
    two = 2 * ROWS

    def rows(k):
        return slice(k * two, (k + 1) * two)

    def both(f, k):
        return jnp.concatenate([f(2 * k), f(2 * k + 1)], 0)

    v0c = v0 - mean_last(v0)
    for k in range(n_chunk):
        r = rows(k)
        sbk = both(lambda u: jnp.broadcast_to(sc[:, u : u + 1], (ROWS, chans)), k)
        sb[r] = sbk
        pair[r] = sbk * v0
        n1[r] = sbk * v0c
    lane = iota((ROWS, chans), 1)
    score_logit = jnp.sum(v0 * v3, -1, keepdims=True) * jnp.concatenate(
        [sc, jnp.zeros((ROWS, chans - WIDE), f32)], 1
    )

    n_in = width // chans
    n_pr = w_pairin_v.shape[1] // chans
    at_tri = n_in + 2 * n_pr
    old_v[...] = jnp.zeros_like(old_v)
    old_v[0:n_in, :] = row_in_v[...]
    for k in range(2):
        for b in range(n_pr):
            j = n_in + k * n_pr + b
            old_v[j : j + 1, :] = row_pairin_v[k : k + 1, b * chans : (b + 1) * chans]
    old_v[at_tri : at_tri + 6, :] = row_tri_v[...]
    old = BETA * old_v[...].T
    for k in range(at_tri + 6):
        old_o[k * chans : (k + 1) * chans, :] = jnp.broadcast_to(old[:, k : k + 1], (chans, chans))
    scale_o[...] = jnp.zeros_like(scale_o)
    mats = [w_in_v] + [w_pairin_v.at[k] for k in range(2)] + [w_tri_v.at[m] for m in range(6)]
    for k, w in enumerate(mats):
        x = w[...]
        x = jnp.sum(jnp.sum(x * x, 0, keepdims=True), -1, keepdims=True) / (w.shape[0] * w.shape[1])
        x = RATE * jnp.maximum(0.001, jnp.sqrt(x))
        scale_o[k : k + 1, :] = jnp.broadcast_to(x, (1, chans))

    for n in range(2):
        for d in range(1, heads):
            peer = lax.rem(head + d, heads)
            pltpu.make_async_remote_copy(
                src_ref=part.at[peer, n],
                dst_ref=part.at[peer, n],
                send_sem=part_send.at[d - 1, n],
                recv_sem=part_recv.at[peer, n],
                device_id=partner(d),
                device_id_type=MESH,
            ).wait_recv()
    for n in range(2):
        s = slice(n * half, (n + 1) * half)
        low = None
        for k in range(heads):
            a = part[k, n, :, 0:half].astype(f32)
            b = part[k, n, :, half : half + quarter].astype(f32)
            b = jnp.concatenate([b[0:8], b[8:16]], 1)
            low = [a, b] if low is None else [low[0] + a, low[1] + b]
        emb[0:16, s] += low[0]
        emb[16:24, s] += low[1]
    state = emb[0:ROWS, :]
    centre = state - mean_last(state)
    frozen = centre * lax.rsqrt(mean_last(centre * centre) + 1e-05)
    frozen = jnp.concatenate([frozen, jnp.zeros((WIDE - ROWS, width), f32)], 0).astype(bf16)
    frozen_o[item] = frozen

    peers = []

    def give(ref):
        k = len(peers)
        copy = pltpu.make_async_remote_copy(
            src_ref=ref,
            dst_ref=ref,
            send_sem=peer_send.at[k],
            recv_sem=peer_recv.at[k],
            device_id={"grp": other},
            device_id_type=MESH,
        )
        copy.start()
        peers.append(copy)
        return copy

    single = dot(frozen, w_in_b[...]).astype(bf16)
    single_o[item] = jnp.concatenate(
        [single[0:ROWS].astype(f32), jnp.broadcast_to(loss_count, (8, single.shape[1]))], 0
    )
    side = dot(single, w_pair_b[...])[0:ROWS]
    side_a = jnp.where(present, side[:, 0:chans], 0.0)
    side_b = jnp.where(present, side[:, chans : 2 * chans], 0.0)
    side_ac = side_a - mean_last(side_a)
    side_bc = side_b - mean_last(side_b)

    own = iota((ROWS, chans), 0) == lane
    logit_b = jnp.sum(
        jnp.where(own, jnp.sum(side_b * v3, -1, keepdims=True), 0.0), 0, keepdims=True
    )
    logit = score_logit + jnp.sum(side_a * v3, -1, keepdims=True) + logit_b
    for k in range(n_chunk):
        r = rows(k)
        pair[r] = pair[r] + both(lambda u: side_a + side_b[u : u + 1, :], k)
        centre = n1[r] + both(lambda u: side_ac + side_bc[u : u + 1, :], k)
        scale = lax.rsqrt(mean_last(centre * centre) + 1e-05)
        normal = centre * scale
        n1[r] = normal
        s1[r] = jnp.broadcast_to(scale, (two, chans))
        pnorm[r] = (normal * v1).astype(bf16)
    proj[...] = dot(pnorm[...], w_tri_b[0:chans, 0 : 5 * chans])
    for k in range(n_chunk):
        r = rows(k)
        sl = sigmoid(proj[r, chans : 2 * chans])
        sr = sigmoid(proj[r, 4 * chans : 5 * chans])
        sig_l[r] = sl
        sig_r[r] = sr
        left[r] = (sl * proj[r, 0:chans]).astype(bf16).astype(f32)
        right[r] = (sr * proj[r, 3 * chans : 4 * chans]).astype(bf16).astype(f32)
        gate[r] = sigmoid(proj[r, 2 * chans : 3 * chans])
        left_n[r] = left[r] * both(
            lambda u: jnp.broadcast_to(cnt_b[u : u + 1, :], (ROWS, chans)), k
        )

    def triangle(dst, moving, fixed, row_of, weighted):
        group = 8
        for a0 in range(0, ROWS, group):
            total = [None] * group
            for b in range(vocab):
                x = moving(b)
                for q in range(group):
                    y = x * fixed[pl.ds(row_of(a0 + q, b), 1), :]
                    total[q] = y if total[q] is None else total[q] + y
            for q in range(group):
                a = a0 + q
                t = total[q]
                if weighted:
                    t = t * cnt_b[a : a + 1, :]
                dst[a * ROWS : (a + 1) * ROWS, :] = t

    triangle(
        upd, lambda u: left_n[u * ROWS : (u + 1) * ROWS, :], right, lambda v, u: u * ROWS + v, False
    )
    give(frozen_o.at[item])
    c_single = give(single_o.at[item])
    for k in range(n_chunk):
        r = rows(k)
        x = upd[r]
        centre = x - mean_last(x)
        scale = lax.rsqrt(mean_last(centre * centre) + 1e-05)
        normal = centre * scale
        n2[r] = normal
        s2[r] = jnp.broadcast_to(scale, (two, chans))
        unorm[r] = (normal * v2).astype(bf16)
    branch[...] = dot(unorm[...], w_tri_b[0:chans, 5 * chans : 6 * chans])
    gated = jnp.zeros((ROWS, chans), f32)
    for k in range(n_chunk):
        r = rows(k)
        move = gate[r] * branch[r]
        final[r] = pair[r] + move
        col = jnp.sum(move * v3, -1, keepdims=True)
        gated_b[r] = jnp.broadcast_to(col, (two, chans))
        for q in range(2):
            gated = jnp.where(lane == 2 * k + q, col[q * ROWS : (q + 1) * ROWS], gated)
    logit = logit + gated

    dist = jnp.maximum(logit, 0.0) + jnp.log(1.0 + jnp.exp(-jnp.abs(logit)))
    dist = jnp.concatenate([dist, jnp.zeros((WIDE - ROWS, chans), f32)], 0)
    dist = jnp.concatenate(split(dist, 3), 0)
    by_col = dot(dist[:, 0:WIDE], one_b).astype(bf16)
    for k in range(n_chunk):
        r = rows(k)
        sl, sr, gt = sig_l[r], sig_r[r], gate[r]
        proj[r, 0:chans] = proj[r, 0:chans] * sl * (1.0 - sl)
        proj[r, 3 * chans : 4 * chans] = proj[r, 3 * chans : 4 * chans] * sr * (1.0 - sr)
        gt3 = gt * v3
        proj[r, 2 * chans : 3 * chans] = gt3 * (1.0 - gt) * branch[r]
        gate[r] = gt3
    loss_row = jnp.zeros((1, seq), f32)
    by_first = jnp.zeros((WIDE, seq), f32)
    for b in range(n_blk):
        s = slice(b * blk, (b + 1) * blk)
        diff = dot(one_t[s, 0 : 3 * WIDE], by_col) - true_d[s, :]
        sq = diff * diff + 1.0
        inv = lax.rsqrt(sq)
        loss_row = loss_row + jnp.sum(
            places[b][:, 3:4] * (sq * inv - 1.0), 0, keepdims=True
        )
        by_first = by_first + dot(one_v[:, s], (diff * inv).astype(bf16))
    loss = jnp.sum(loss_row * weight_j, -1, keepdims=True)
    by_pair = dot_nt(jnp.concatenate(split(by_first * weight_j, 2), 0), one_b)
    by_pair = (by_pair[0:WIDE] + by_pair[WIDE : 2 * WIDE])[0:ROWS]
    dlogit = by_pair * sigmoid(logit)[:, 0:WIDE]

    g_dist = jnp.zeros((two, chans), f32)
    for k in range(n_chunk):
        r = rows(k)
        g = both(lambda u: jnp.broadcast_to(dlogit[:, u : u + 1], (ROWS, chans)), k)
        g_dist = g_dist + g * final[r]
        dfinal = g * v3
        pair[r] = dfinal
        dbranch[r] = (g * gate[r]).astype(bf16)
        dproj[r, 2 * chans : 3 * chans] = (g * proj[r, 2 * chans : 3 * chans]).astype(bf16)
        gated_b[r] = g * gated_b[r] * (1.0 / chans)
    dunorm[...] = dot_nt(dbranch[...], w_tri_b[:, 5 * chans : 6 * chans])
    gtri_x[item, 5] = dot_tn(unorm[...], dbranch[...])
    gtri_x[item, 4] = dot_tn(pnorm[...], dproj[:, 2 * chans : 3 * chans])
    c_pair = [give(gtri_x.at[item, pl.ds(4, 2)])]
    g_two = jnp.zeros((two, chans), f32)
    for k in range(n_chunk):
        r = rows(k)
        dn = dunorm[r, 0:chans]
        normal = n2[r]
        g_two = g_two + dn * normal
        upd[r] = s2[r] * (dn * v2 - dunorm[r, chans : 2 * chans] - normal * gated_b[r])
    triangle(
        dleft, lambda v: upd[v * ROWS : (v + 1) * ROWS, :], right, lambda u, v: u * ROWS + v, True
    )
    for k in range(n_chunk):
        r = rows(k)
        d, sl = dleft[r], sig_l[r]
        dproj[r, 0:chans] = (d * sl).astype(bf16)
        dproj[r, chans : 2 * chans] = (d * proj[r, 0:chans]).astype(bf16)
    dpnorm[...] = dot_nt(dproj[:, 0 : 3 * chans], w_tri_b[:, 0 : 3 * chans])
    g = dot_tn(pnorm[...], dproj[:, 0 : 2 * chans])
    gtri_x[item, 0] = g[:, 0:chans]
    gtri_x[item, 1] = g[:, chans : 2 * chans]
    c_pair.append(give(gtri_x.at[item, pl.ds(0, 2)]))
    for t in range(vocab):
        upd_t[t * ROWS : (t + 1) * ROWS, :] = upd[pl.ds(t, ROWS, stride=ROWS), :]
    triangle(
        dright, lambda t: upd_t[t * ROWS : (t + 1) * ROWS, :], left, lambda u, t: u * ROWS + t, True
    )
    for k in range(n_chunk):
        r = rows(k)
        d, sr = dright[r], sig_r[r]
        dproj[r, 3 * chans : 4 * chans] = (d * sr).astype(bf16)
        dproj[r, 4 * chans : 5 * chans] = (d * proj[r, 3 * chans : 4 * chans]).astype(bf16)
    dlast[...] = dot_nt(dproj[:, 3 * chans : 5 * chans], w_tri_b[:, 3 * chans : 5 * chans])
    g = dot_tn(pnorm[...], dproj[:, 3 * chans : 5 * chans])
    gtri_x[item, 2] = g[:, 0:chans]
    gtri_x[item, 3] = g[:, chans : 2 * chans]
    c_pair.append(give(gtri_x.at[item, pl.ds(2, 2)]))
    g_one = jnp.zeros((two, chans), f32)
    g_score = jnp.zeros((two, chans), f32)
    d_a = jnp.zeros((ROWS, chans), f32)
    tail_o[item] = jnp.zeros((WIDE, 2 * chans), f32)
    for k in range(n_chunk):
        r = rows(k)
        dn = dpnorm[r, 0:chans] + dlast[r, 0:chans]
        mean = dpnorm[r, chans : 2 * chans] + dlast[r, chans : 2 * chans]
        normal = n1[r]
        along = dn * normal
        g_one = g_one + along
        dpair = pair[r] + s1[r] * (dn * v1 - mean - normal * mean_last(along * v1))
        g_score = g_score + sb[r] * dpair
        d_a = d_a + dpair[0:ROWS] + dpair[ROWS:two]
        for q in range(2):
            tail_o[item, 2 * k + q : 2 * k + q + 1, chans : 2 * chans] = jnp.sum(
                dpair[q * ROWS : (q + 1) * ROWS], 0, keepdims=True
            )
    tail_o[item, 0:ROWS, 0:chans] = d_a
    for k, g in enumerate((g_score, g_one, g_two, g_dist)):
        tail_o[item, ROWS + k : ROWS + k + 1, 0:chans] = jnp.sum(g, 0, keepdims=True)
    tail_o[item, ROWS + 4 : ROWS + 5, 0:chans] = jnp.broadcast_to(loss, (1, chans))
    tail_o[item, ROWS + 5 : ROWS + 6, 0:chans] = jnp.broadcast_to(loss_count, (1, chans))
    c_tail = give(tail_o.at[item])

    c_single.wait_recv()
    inv = 1.0 / (
        single_o[0, ROWS : ROWS + 1, 0:chans] + single_o[1, ROWS : ROWS + 1, 0:chans]
    )
    for pairs in ((0, 1), (2,)):
        mats = []
        for k in pairs:
            c_pair[k].wait_recv()
            first = (4, 0, 2)[k]
            mats += [first, first + 1]
        for m in mats:
            g = (gtri_x[0, m] + gtri_x[1, m]) * inv
            g_tri_o[m] = g
            sq_tri[m * chans : (m + 1) * chans, :] = (g * g).astype(bf16)
        for m in mats:
            r = slice(m * chans, (m + 1) * chans)
            sum_tri[r, :] = dot(sq_tri[r, :], jnp.ones((chans, chans), bf16))
        for m in mats:
            total = sum_tri[m * chans : (m + 1) * chans, :].T[0:1, :]
            row_tri_o[m : m + 1, :] = fresh(row_tri_v[m : m + 1, :], total, chans)

            def put_col(h, col, m=m):
                col_tri_o[m : m + 1, :] = col

            adafactor(
                g_tri_o.at[m], w_tri_v.at[m], new_tri_o.at[m],
                lambda h, m=m: col_tri_v[m : m + 1, :], put_col,
                sum_tri.at[pl.ds(m * chans, chans)],
                old_o.at[pl.ds((at_tri + m) * chans, chans)],
                scale_o[3 + m : 4 + m, :],
            )

    for c in sends + unit_sends + peers:
        c.wait_send()
    for c in peers:
        if c is not c_single and all(c is not x for x in c_pair):
            c.wait_recv()


def update_kernel(
    frozen_v, single_v, tail_v, old_v, scale_v, g_tri, new_tri, row_tri_n, col_tri_n,
    w_in_v, w_pairin_v, w_tri_v, vecs_v,
    row_in_v, col_in_v, row_pairin_v, col_pairin_v, row_tri_v, col_tri_v, sq_vecs_v,
    loss_o, count_o, g_in_o, row_in_o, col_in_o, new_in_o, g_pairin_o, row_pairin_o, col_pairin_o,
    new_pairin_o, g_tri_o, row_tri_o, col_tri_o, new_tri_o, g_vecs_o, sq_vecs_o, new_vecs_o,
    loss_s, count_s, g_in, row_in_n, col_in_n, new_in, g_pairin, row_pairin_n, col_pairin_n,
    new_pairin, g_vecs, sq_vecs_n, new_vecs,
    ds_v, sq_in, sq_rest, sum_in, sum_rest, store_sem,
):
    chans = vecs_v.shape[1]
    width, node = w_in_v.shape
    stores = []

    def store(src, dst):
        copy = pltpu.make_async_copy(src, dst, store_sem.at[len(stores)])
        stores.append(copy)
        copy.start()

    store(g_tri, g_tri_o)
    store(new_tri, new_tri_o)
    store(row_tri_n, row_tri_o)
    store(col_tri_n, col_tri_o)
    totals = tail_v[0, ROWS : ROWS + 8, 0:chans] + tail_v[1, ROWS : ROWS + 8, 0:chans]
    inv = 1.0 / totals[5:6, :]
    inv2 = jnp.concatenate([inv, inv], 1)
    d_side = [tail_v[i, 0:ROWS, :] * inv2 for i in range(2)]

    pads = jnp.zeros((WIDE - ROWS, node), f32)
    side_parts = []
    for i in range(2):
        parts = split(d_side[i], 2)
        side_parts.append(parts)
        st = jnp.concatenate([p.astype(f32) for p in parts], 0).astype(bf16)
        ds = dot_nt(st[:, 0:chans], w_pairin_v[0].astype(bf16)) + dot_nt(
            st[:, chans : 2 * chans], w_pairin_v[1].astype(bf16)
        )
        ds = ds[0:ROWS] + ds[ROWS : 2 * ROWS]
        for k, p in enumerate(split(ds, 2)):
            at = (2 * k + i) * WIDE
            ds_v[at : at + WIDE, :] = jnp.concatenate([p.astype(f32), pads], 0).astype(bf16)
    fz = jnp.concatenate([frozen_v[0], frozen_v[1], frozen_v[0], frozen_v[1]], 0)
    g_in[...] = dot_tn(fz, ds_v[...])
    store(g_in, g_in_o)

    sg = [single_v[i, 0:ROWS] for i in range(2)]
    sg = jnp.concatenate(sg + sg, 0).astype(bf16)
    st = jnp.concatenate(
        [side_parts[i][k].astype(f32) for k in range(2) for i in range(2)], 0
    ).astype(bf16)
    for k in range(2):
        g_pairin[k] = dot_tn(sg, st[:, k * chans : (k + 1) * chans])
    store(g_pairin, g_pairin_o)
    loss_s[...] = totals[4:5, :]
    count_s[...] = totals[5:6, :]
    g_vecs[...] = totals[0:4, :] * inv
    store(loss_s, loss_o)
    store(count_s, count_o)
    store(g_vecs, g_vecs_o)

    blk = chans
    n_in = width // blk
    n_pr = w_pairin_v.shape[1] // blk
    for b in range(n_in):
        g = g_in[b * blk : (b + 1) * blk, :]
        sq_in[b * blk : (b + 1) * blk, :] = (g * g).astype(bf16)
    for k in range(2):
        for b in range(n_pr):
            g = g_pairin[k, b * blk : (b + 1) * blk, :]
            j = k * n_pr + b
            sq_rest[j * blk : (j + 1) * blk, :] = (g * g).astype(bf16)
    sum_in[...] = dot(sq_in[...], jnp.ones((node, chans), bf16))
    sum_rest[...] = dot(sq_rest[...], jnp.ones((chans, chans), bf16))
    for b in range(n_in):
        total = sum_in[b * blk : (b + 1) * blk, :].T[0:1, :]
        row_in_n[b : b + 1, :] = fresh(row_in_v[b : b + 1, :], total, node)
    for k in range(2):
        for b in range(n_pr):
            j = k * n_pr + b
            total = sum_rest[j * blk : (j + 1) * blk, :].T[0:1, :]
            c = slice(b * blk, (b + 1) * blk)
            row_pairin_n[k : k + 1, c] = fresh(row_pairin_v[k : k + 1, c], total, chans)
    store(row_in_n, row_in_o)
    store(row_pairin_n, row_pairin_o)

    def put(ref, k):
        def put_col(h, col):
            at = k if k is not None else h
            ref[at : at + 1, :] = col

        return put_col

    adafactor(
        g_in, w_in_v, new_in, lambda h: col_in_v[h : h + 1, :], put(col_in_n, None), sum_in,
        old_v.at[pl.ds(0, width)], scale_v[0:1, :],
    )
    store(new_in, new_in_o)
    store(col_in_n, col_in_o)
    for k in range(2):
        adafactor(
            g_pairin.at[k], w_pairin_v.at[k], new_pairin.at[k],
            lambda h, k=k: col_pairin_v[k : k + 1, :], put(col_pairin_n, k),
            sum_rest.at[pl.ds(k * n_pr * blk, n_pr * blk)],
            old_v.at[pl.ds((n_in + k * n_pr) * blk, n_pr * blk)], scale_v[1 + k : 2 + k, :],
        )
    store(new_pairin, new_pairin_o)
    store(col_pairin_n, col_pairin_o)

    g = g_vecs[...]
    sq = BETA * sq_vecs_v[...] + (1.0 - BETA) * (g * g + 1e-30)
    sq_vecs_n[...] = sq
    step = g * lax.rsqrt(sq)
    step = step / jnp.maximum(1.0, jnp.sqrt(mean_last(step * step)))
    v = vecs_v[...]
    scale = jnp.maximum(0.001, jnp.sqrt(mean_last(v * v)))
    new_vecs[...] = v - RATE * scale * step
    store(sq_vecs_n, sq_vecs_o)
    store(new_vecs, new_vecs_o)
    for c in stores:
        c.wait()


def shards(
    tokens, lengths, recycle, resolved, coords, plm_embed, plm_uv, plm_qk, plm_affine, plm_out,
    w_in, w_pairin, w_tri, vecs, row_in, col_in, row_pairin, col_pairin, row_tri, col_tri, sq_vecs,
):
    heads = lax.axis_size("head")
    seq = tokens.shape[1]
    width = plm_embed.shape[1]
    units = plm_uv.shape[2]
    chans = vecs.shape[1]
    node = w_in.shape[1]
    shared_by = 2 if units % 256 == 0 else 1
    unit_part = units // shared_by
    anywhere = pl.BlockSpec(memory_space=pl.ANY)
    inside = pl.BlockSpec(memory_space=pltpu.VMEM)
    table = ROWS * ROWS

    def vm(*shape, dtype=f32):
        return pltpu.VMEM(shape, dtype)

    def like(x):
        return pltpu.VMEM(x.shape, x.dtype)

    coords = jnp.transpose(coords, (1, 0, 2))
    row_in2 = row_in.reshape(-1, chans)
    col_in2 = col_in.reshape(-1, chans)
    operands = (
        tokens, lengths, recycle, resolved, coords, plm_embed, plm_uv, plm_qk, plm_affine, plm_out,
        w_in, w_pairin, w_tri, vecs, row_in2, col_in2, row_pairin, col_pairin, row_tri, col_tri, sq_vecs,
    )
    kept = operands[10:]
    scratch = [
        like(tokens), like(resolved),
        like(coords), like(plm_embed), vm(2, width, unit_part, dtype=bf16), like(plm_qk),
        like(plm_affine), vm(shared_by, unit_part, width, dtype=bf16),
        vm(WIDE, width), vm(2, 8, seq), vm(shared_by, ROWS, unit_part), vm(shared_by, WIDE, unit_part, dtype=bf16),
        vm(ROWS, width), vm(heads, 2, 16, width // 2 + width // 4, dtype=bf16),
        vm(width, node, dtype=bf16), vm(node, 2 * chans, dtype=bf16),
        vm(2 * chans, 6 * chans, dtype=bf16), vm(WIDE, chans), vm(seq, seq), vm(chans, seq),
        vm(table, chans), vm(table, chans), vm(table, chans), vm(table, chans),
        vm(table, chans, dtype=bf16), vm(table, 5 * chans), vm(table, chans), vm(table, chans),
        vm(table, chans), vm(table, chans), vm(table, chans), vm(table, chans), vm(table, chans),
        vm(table, chans), vm(table, chans, dtype=bf16),
        vm(table, chans), vm(table, chans), vm(table, chans, dtype=bf16), vm(table, chans),
        vm(table, chans), vm(table, 2 * chans), vm(table, 2 * chans), vm(table, 2 * chans),
        vm(table, chans), vm(table, chans), vm(table, chans), vm(table, 5 * chans, dtype=bf16),
        vm(chans, chans), vm(seq, chans, dtype=bf16),
        vm(2, 6, chans, chans), vm(6 * chans, chans, dtype=bf16), vm(6 * chans, chans),
        pltpu.SemaphoreType.DMA((19 + shared_by,)),
        pltpu.SemaphoreType.DMA((heads - 1, 2)), pltpu.SemaphoreType.DMA((heads, 2)),
        pltpu.SemaphoreType.DMA((3,)), pltpu.SemaphoreType.DMA((3,)),
        pltpu.SemaphoreType.DMA((6,)), pltpu.SemaphoreType.DMA((6,)),
    ]
    operands = tuple(
        x if x.size == 1 else pltpu.with_memory_space_constraint(x, pltpu.HBM) for x in operands
    )
    sds = jax.ShapeDtypeStruct
    n_blk = width // chans + 2 * (node // chans) + 6
    made = pl.pallas_call(
        functools.partial(tables_kernel, heads=heads, shared_by=shared_by, unit_part=unit_part),
        out_shape=(
            sds((2, WIDE, width), bf16), sds((2, WIDE, node), f32), sds((2, WIDE, 2 * chans), f32),
            sds((n_blk * chans, chans), f32), sds((16, chans), f32), sds(w_tri.shape, f32),
            sds(w_tri.shape, f32), sds(row_tri.shape, f32), sds(col_tri.shape, f32),
        )
        + tuple(sds(x.shape, x.dtype) for x in kept),
        in_specs=[
            pl.BlockSpec(memory_space=pltpu.SMEM) if x.size == 1 else anywhere for x in operands
        ],
        out_specs=[inside] * (9 + len(kept)),
        scratch_shapes=scratch,
        compiler_params=pltpu.CompilerParams(
            collective_id=0, has_side_effects=True, vmem_limit_bytes=48 << 20
        ),
        name="tables",
    )(*operands)

    operands = tuple(made)
    outs = (
        sds((1, chans), f32), sds((1, chans), f32), w_in, row_in2, col_in2, w_in, w_pairin,
        row_pairin, col_pairin, w_pairin, w_tri, row_tri, col_tri, w_tri, vecs, vecs, vecs,
    )
    outs = tuple(sds(x.shape, x.dtype) for x in outs)
    scratch = (
        [like(x) for k, x in enumerate(outs) if k not in (10, 11, 12, 13)]
        + [
            vm(4 * WIDE, node, dtype=bf16), vm(width, node, dtype=bf16),
            vm(2 * node, chans, dtype=bf16), vm(width, chans), vm(2 * node, chans),
            pltpu.SemaphoreType.DMA((17,)),
        ]
    )
    res = list(
        pl.pallas_call(
            update_kernel,
            out_shape=outs,
            in_specs=[inside] * len(operands),
            out_specs=[anywhere] * len(outs),
            scratch_shapes=scratch,
            compiler_params=pltpu.CompilerParams(vmem_limit_bytes=32 << 20),
            name="update",
        )(*operands)
    )
    res[0] = res[0][0, 0]
    res[1] = res[1][0, 0]
    res[3] = res[3].reshape(-1)
    res[4] = res[4].reshape(-1)
    return tuple(res)


def solution(mesh):
    whole = P()
    in_specs = (
        P("grp", None), P("grp"), P("grp"), P("grp", None), P("grp", None, None), whole,
        P(None, None, "head"), whole, whole, P("head", None),
    ) + (whole,) * 11
    return jax.shard_map(
        shards, mesh=mesh, in_specs=in_specs, out_specs=(whole,) * 17, check_vma=False
    )
```
